32 devices in a mesh: outer: 4 (over y, x), inner: 8 (over z, core).
Axes of the slice: x: 2, y: 2, z: 4, core: 2. Of those that a mesh axis runs over, the one named last changes fastest.
Arguments:
- queries: bfloat16 [4096, 512], P(('outer', 'inner')), may hold values from -24 to 24
- keys: bfloat16 [4096, 512], P(('outer', 'inner')), may hold values from -24 to 24
- values: bfloat16 [4096, 512], P(('outer', 'inner')), may hold values from -6 to 6
- block_pos: int32 [32], P(('outer', 'inner')), may hold values from 0 to 31, each once
Outputs:
- attended: bfloat16 [4096, 512], P(('outer', 'inner'))
The draws below stay inside these ranges and needn't reach their ends.
All inputs are finite; a program needn't handle non-finite values.
Results may differ from the reference program's by a relative error of at most 0.009.
Values may be sent and summed in bfloat16 or wider, within the bound.
No kernel may reach another device: no remote copies, remote signals or barrier semaphores. Data moves between devices by JAX's collectives and lax.ppermute only.
A program may use at most 192 MiB of HBM per device.

```python
import math
import jax
import jax.numpy as jnp
from jax import lax

HEADS = 4
HEAD_DIM = 128
TOK_DEV = 128
BLOCKS = 32
TOKENS = 4096


def shared_keys(key):
    width = HEADS * HEAD_DIM
    return jax.random.truncated_normal(key, -6.0, 6.0, (TOKENS, width), jnp.float32)


def draw_keys(key, part):
    base = shared_keys(key)
    return base.astype(jnp.bfloat16)


def draw_queries(key, part):
    key = jax.random.fold_in(key, 5)
    width = HEADS * HEAD_DIM
    fresh = jax.random.truncated_normal(key, -6.0, 6.0, (TOKENS, width), jnp.float32)
    return fresh.astype(jnp.bfloat16)


def levels(key, shape, shards, least, top_value):
    gain, own = 1.0, jax.random.fold_in(key, 6)
    for axis_at, blocks in shards:
        draws = jnp.exp(jax.random.uniform(jax.random.fold_in(own, axis_at), (blocks,), jnp.float32, least / len(shards), top_value / len(shards)))
        gain = gain * jnp.repeat(draws, shape[axis_at] // blocks).reshape([-1 if axis == axis_at else 1 for axis in range(len(shape))])
    return gain


def bell_draw(own_key, shape, scale, limit, cuts=(), kind=jnp.bfloat16):
    values = jax.random.normal(own_key, shape, jnp.float32) * scale
    if len(cuts) > 0:
        values = levels(own_key, shape, cuts, -0.22, 0.18) * values
    return jnp.clip(values, min=-limit, max=limit).astype(kind)


def setup_inputs(seed: int = 0) -> dict:
    splits = jax.random.split(jax.random.key(seed), 5)
    return {
        "queries": draw_queries(jax.random.fold_in(splits[4], 71), 0),
        "keys": draw_keys(jax.random.fold_in(splits[4], 71), 0),
        "values": bell_draw(splits[2], (TOKENS, HEADS * HEAD_DIM), 1.0, 6.0, ((0, 32),)),
        "block_pos": jax.random.permutation(splits[3], BLOCKS).astype(jnp.int32),
    }


def reference(queries, keys, values, block_pos):
    width = HEADS * HEAD_DIM
    nblk = block_pos.shape[0]
    order = jnp.argsort(block_pos).astype(jnp.int32)
    q_sorted = queries.reshape(nblk, TOK_DEV, width)[order].reshape(TOKENS, width)
    k_sorted = keys.reshape(nblk, TOK_DEV, width)[order].reshape(TOKENS, width)
    v_sorted = values.reshape(nblk, TOK_DEV, width)[order].reshape(TOKENS, width)
    span = math.gcd(TOKENS, 1024)
    scale = HEAD_DIM ** -0.5

    def one_block(qi):
        qrows = lax.dynamic_slice_in_dim(q_sorted, qi * span, span, 0).astype(jnp.float32).reshape(span, HEADS, HEAD_DIM)
        qpos = qi * span + jnp.arange(span, dtype=jnp.int32)

        def step(kj, carry):
            acc, top, total = carry
            krows = lax.dynamic_slice_in_dim(k_sorted, kj * span, span, 0).astype(jnp.float32).reshape(span, HEADS, HEAD_DIM)
            vrows = lax.dynamic_slice_in_dim(v_sorted, kj * span, span, 0).astype(jnp.float32).reshape(span, HEADS, HEAD_DIM)
            kpos = kj * span + jnp.arange(span, dtype=jnp.int32)
            scores = jnp.einsum("qhd,khd->hqk", qrows, krows) * scale
            allowed = kpos[None, :] <= qpos[:, None]
            scores = jnp.where(allowed[None], scores, -1e30)
            newtop = jnp.maximum(top, jnp.max(scores, axis=-1))
            weights = jnp.where(allowed[None], jnp.exp(scores - newtop[..., None]), 0.0).astype(jnp.bfloat16)
            factor = jnp.exp(top - newtop)
            wide = weights.astype(jnp.float32)
            total = total * factor + jnp.sum(wide, axis=-1)
            acc = acc * factor.T[:, :, None] + jnp.einsum("hqk,khd->qhd", wide, vrows)
            return acc, newtop, total

        init = (jnp.zeros((span, HEADS, HEAD_DIM), jnp.float32), jnp.full((HEADS, span), -1e30, jnp.float32), jnp.zeros((HEADS, span), jnp.float32))
        acc, top, total = lax.fori_loop(0, qi + 1, step, init)
        return (acc / total.T[:, :, None]).reshape(span, width).astype(jnp.bfloat16)

    outs = lax.map(one_block, jnp.arange(TOKENS // span, dtype=jnp.int32))
    sorted_out = outs.reshape(nblk, TOK_DEV, width)
    return sorted_out[block_pos].reshape(TOKENS, width)
```

```python
import functools
import math

import jax
import jax.numpy as jnp
from jax import lax
from jax.experimental import pallas as pl
from jax.experimental.pallas import tpu as pltpu
from jax.sharding import PartitionSpec as P

HEADS = 4
CORES = 2
PAD = 16
LOW = -1e30
FLOOR = -1e29
BF16 = jnp.bfloat16
F32 = jnp.float32


def nt_dot(a, b):
    return lax.dot_general(a, b, (((1,), (1,)), ((), ())), preferred_element_type=F32)


def pack_kernel(pos_ref, q_ref, k_ref, v_ref, q_out, kv_out):
    tok = q_ref.shape[0]
    size = q_ref.shape[1] // HEADS
    per = HEADS // CORES
    pos = jnp.full((PAD, size), pos_ref[0].astype(F32), F32).astype(BF16)
    for c in range(CORES):
        parts_q, parts_kv = [], []
        for j in range(per):
            cols = slice((c * per + j) * size, (c * per + j + 1) * size)
            parts_q.append(q_ref[:, cols])
        for j in range(per):
            cols = slice((c * per + j) * size, (c * per + j + 1) * size)
            parts_kv.append(k_ref[:, cols])
        for j in range(per):
            cols = slice((c * per + j) * size, (c * per + j + 1) * size)
            parts_kv.append(v_ref[:, cols].astype(F32).T.astype(BF16))
        for d in range(q_out.shape[0] // CORES):
            for j, part in enumerate(parts_q):
                q_out[d * CORES + c, j * tok : (j + 1) * tok, :] = part
            q_out[d * CORES + c, per * tok :, :] = pos
        for d in range(kv_out.shape[0] // CORES):
            for j, part in enumerate(parts_kv):
                kv_out[d * CORES + c, j * tok : (j + 1) * tok, :] = part
            kv_out[d * CORES + c, 2 * per * tok :, :] = pos


def attend_kernel(q_ref, kv_ref, out_ref, k_all, v_all, kpos_all):
    nq, nk = q_ref.shape[0], kv_ref.shape[0]
    size = q_ref.shape[2]
    tok = size
    per = HEADS // CORES
    rate = size ** -0.5 * math.log2(math.e)
    for j in range(nk):
        for h in range(per):
            k_all[h, j * tok : (j + 1) * tok, :] = kv_ref[j, h * tok : (h + 1) * tok, :]
            v_all[h, 0:size, j * tok : (j + 1) * tok] = kv_ref[j, (per + h) * tok : (per + h + 1) * tok, :]
    for h in range(per):
        v_all[h, size:, :] = jnp.ones((PAD, nk * tok), BF16)
    two = 2 * tok
    for j in range(nk):
        base = kv_ref[j, 2 * per * tok : 2 * per * tok + 8, :].astype(F32)[0:1, :] * tok
        kpos_all[j] = jnp.concatenate([base, base], axis=1)
    rows = lax.broadcasted_iota(jnp.int32, (tok, two), 0).astype(F32)
    lanes = lax.broadcasted_iota(jnp.int32, (1, tok), 1).astype(F32)

    def body(i, _):
        q0, q1 = 2 * i, 2 * i + 1
        qp = [
            q_ref[q, per * tok : per * tok + 8, :].astype(F32)[0:1, :] * tok + lanes for q in (q0, q1)
        ]
        qpos = jnp.concatenate(qp, axis=1)
        stats = [[], []]
        for h in range(per):
            q = jnp.concatenate([q_ref[q0, h * tok : (h + 1) * tok, :], q_ref[q1, h * tok : (h + 1) * tok, :]], axis=0)
            s = nt_dot(k_all[h], q)
            parts = []
            for j in range(nk):
                keep = rows <= qpos - kpos_all[j]
                parts.append(jnp.where(keep, s[j * tok : (j + 1) * tok, :], LOW))
            s = jnp.concatenate(parts, axis=0)
            top = jnp.maximum(jnp.max(s, axis=0, keepdims=True), FLOOR).astype(BF16)
            p = jnp.exp2((s - top.astype(F32)) * rate).astype(BF16)
            o = jnp.dot(v_all[h], p, preferred_element_type=F32)
            total = o[size : size + 1, :]
            hi = total.astype(BF16)
            lo = (total - hi.astype(F32)).astype(BF16)
            for n, qi in enumerate((q0, q1)):
                cols = slice(n * tok, (n + 1) * tok)
                out_ref[qi, h * size : (h + 1) * size, :] = o[0:size, cols].astype(BF16)
                stats[n] += [top[:, cols].astype(F32), hi[:, cols].astype(F32), lo[:, cols].astype(F32)]
        for n, qi in enumerate((q0, q1)):
            rest = jnp.zeros((PAD - 3 * per, tok), F32)
            out_ref[qi, per * size :, :] = jnp.concatenate(stats[n] + [rest], axis=0).astype(BF16)
        return 0

    lax.fori_loop(0, nq // 2, body, 0, unroll=nq <= 8)


def combine_kernel(parts_ref, out_ref):
    n = parts_ref.shape[0]
    size = parts_ref.shape[2]
    per = HEADS // CORES
    rate = size ** -0.5 * math.log2(math.e)
    for c in range(CORES):
        stats = [parts_ref[w * CORES + c, per * size :, :].astype(F32) for w in range(n // CORES)]
        for h in range(per):
            tops = [s[3 * h : 3 * h + 1, :] for s in stats]
            best = functools.reduce(jnp.maximum, tops)
            factors = [jnp.exp2((t - best) * rate) for t in tops]
            denom = sum(f * (s[3 * h + 1 : 3 * h + 2, :] + s[3 * h + 2 : 3 * h + 3, :]) for f, s in zip(factors, stats))
            numer = sum(
                f * parts_ref[w * CORES + c, h * size : (h + 1) * size, :].astype(F32) for w, f in enumerate(factors)
            )
            col = (c * per + h) * size
            out_ref[:, col : col + size] = (numer / denom).T.astype(BF16)


def vmem(n=1):
    return [pl.BlockSpec(memory_space=pltpu.VMEM)] * n


def shards(n_out, n_in, queries, keys, values, block_pos):
    tok, width = queries.shape
    size = width // HEADS
    per = HEADS // CORES
    params = pltpu.CompilerParams(vmem_limit_bytes=40 * 1024 * 1024)
    with jax.named_scope("pack"):
        q_send, kv_send = pl.pallas_call(
            pack_kernel,
            out_shape=(
                jax.ShapeDtypeStruct((n_in, per * tok + PAD, size), BF16),
                jax.ShapeDtypeStruct((n_out * CORES, 2 * per * tok + PAD, size), BF16),
            ),
            in_specs=[pl.BlockSpec(memory_space=pltpu.SMEM)] + vmem(3),
            out_specs=tuple(vmem(2)),
            compiler_params=params,
            name="pack",
        )(block_pos, queries, keys, values)
    with jax.named_scope("exchange"):
        groups = [
            [o * n_in + w * CORES + c for o in range(n_out) for c in range(CORES)] for w in range(n_in // CORES)
        ]
        kv = lax.all_to_all(
            kv_send, ("outer", "inner"), split_axis=0, concat_axis=0, tiled=True, axis_index_groups=groups
        )
        q = lax.all_to_all(q_send, "inner", split_axis=0, concat_axis=0, tiled=True)
    nk = kv.shape[0]
    with jax.named_scope("attend"):
        parts = pl.pallas_call(
            attend_kernel,
            out_shape=jax.ShapeDtypeStruct((n_in, per * size + PAD, tok), BF16),
            in_specs=vmem(2),
            out_specs=vmem()[0],
            scratch_shapes=[
                pltpu.VMEM((per, nk * tok, size), BF16),
                pltpu.VMEM((per, size + PAD, nk * tok), BF16),
                pltpu.VMEM((nk, 1, 2 * tok), F32),
            ],
            compiler_params=params,
            name="attend",
        )(q, kv)
    with jax.named_scope("return"):
        parts = lax.all_to_all(parts, "inner", split_axis=0, concat_axis=0, tiled=True)
    with jax.named_scope("combine"):
        return pl.pallas_call(
            combine_kernel,
            out_shape=jax.ShapeDtypeStruct((tok, width), BF16),
            in_specs=vmem(),
            out_specs=vmem()[0],
            compiler_params=params,
            name="combine",
        )(parts)


def solution(mesh):
    n_out, n_in = mesh.shape["outer"], mesh.shape["inner"]
    return jax.shard_map(
        functools.partial(shards, n_out, n_in),
        mesh=mesh,
        in_specs=(
            P(("outer", "inner"), None),
            P(("outer", "inner"), None),
            P(("outer", "inner"), None),
            P(("outer", "inner")),
        ),
        out_specs=P(("outer", "inner"), None),
        check_vma=False,
    )
```

```python
import functools
import math

import jax
import jax.numpy as jnp
from jax import lax
from jax.experimental import pallas as pl
from jax.experimental.pallas import tpu as pltpu
from jax.sharding import PartitionSpec as P

HEADS = 4
CORES = 2
PER = HEADS // CORES
PAD = 16
LOW = -1e30
FLOOR = -1e29
BF16 = jnp.bfloat16
F32 = jnp.float32


def nt_dot(a, b):
    return lax.dot_general(a, b, (((1,), (1,)), ((), ())), preferred_element_type=F32)


def pack_kernel(pos_ref, q_ref, k_ref, v_ref, q_same, kv_same, q_other, kv_other, v_buf, sems):
    tok = q_ref.shape[0]
    size = q_ref.shape[1] // HEADS
    core = lax.rem(lax.axis_index("inner"), CORES)
    copies = [pltpu.make_async_copy(v_ref, v_buf, sems.at[0])]
    for x, (q_out, kv_out) in enumerate(((q_same, kv_same), (q_other, kv_other))):
        pair = jnp.bitwise_xor(core, x)
        for j in range(PER):
            cols = pl.ds(pl.multiple_of((pair * PER + j) * size, size), size)
            rows = pl.ds(j * tok, tok)
            at = 1 + 2 * (x * PER + j)
            copies.append(pltpu.make_async_copy(q_ref.at[:, cols], q_out.at[rows, :], sems.at[at]))
            copies.append(pltpu.make_async_copy(k_ref.at[:, cols], kv_out.at[rows, :], sems.at[at + 1]))
    for copy in copies:
        copy.start()
    pos = jnp.full((PAD, size), pos_ref[0].astype(F32), F32).astype(BF16)
    for q_out, kv_out in ((q_same, kv_same), (q_other, kv_other)):
        q_out[PER * tok :, :] = pos
        kv_out[2 * PER * tok :, :] = pos
    copies[0].wait()
    for x, kv_out in enumerate((kv_same, kv_other)):
        pair = jnp.bitwise_xor(core, x)
        for j in range(PER):
            cols = pl.ds(pl.multiple_of((pair * PER + j) * size, size), size)
            kv_out[(PER + j) * tok : (PER + j + 1) * tok, :] = v_buf[:, cols].astype(F32).T.astype(BF16)
    for copy in copies[1:]:
        copy.wait()


def attend_kernel(nq, nk, *refs):
    q_refs, kv_refs, out_refs = refs[:nq], refs[nq : nq + nk], refs[nq + nk : nq + nk + nq]
    k_all, v_all, kpos_all = refs[nq + nk + nq :]
    size = q_refs[0].shape[1]
    tok = size
    rate = size ** -0.5 * math.log2(math.e)
    for j in range(nk):
        for h in range(PER):
            k_all[h, j * tok : (j + 1) * tok, :] = kv_refs[j][h * tok : (h + 1) * tok, :]
            v_all[h, 0:size, j * tok : (j + 1) * tok] = kv_refs[j][(PER + h) * tok : (PER + h + 1) * tok, :]
    for h in range(PER):
        v_all[h, size:, :] = jnp.ones((PAD, nk * tok), BF16)
    two = 2 * tok
    for j in range(nk):
        base = kv_refs[j][2 * PER * tok : 2 * PER * tok + 8, :].astype(F32)[0:1, :] * tok
        kpos_all[j] = jnp.concatenate([base, base], axis=1)
    rows = lax.broadcasted_iota(jnp.int32, (tok, two), 0).astype(F32)
    lanes = lax.broadcasted_iota(jnp.int32, (1, tok), 1).astype(F32)

    for i in range(nq // 2):
        pair = (2 * i, 2 * i + 1)
        qpos = jnp.concatenate(
            [q_refs[q][PER * tok : PER * tok + 8, :].astype(F32)[0:1, :] * tok + lanes for q in pair], axis=1
        )
        stats = [[], []]
        for h in range(PER):
            q = jnp.concatenate([q_refs[n][h * tok : (h + 1) * tok, :] for n in pair], axis=0)
            s = nt_dot(k_all[h], q)
            parts = []
            for j in range(nk):
                keep = rows <= qpos - kpos_all[j]
                parts.append(jnp.where(keep, s[j * tok : (j + 1) * tok, :], LOW))
            s = jnp.concatenate(parts, axis=0)
            top = jnp.maximum(jnp.max(s, axis=0, keepdims=True), FLOOR).astype(BF16)
            p = jnp.exp2((s - top.astype(F32)) * rate).astype(BF16)
            o = jnp.dot(v_all[h], p, preferred_element_type=F32)
            total = o[size : size + 1, :]
            hi = total.astype(BF16)
            lo = (total - hi.astype(F32)).astype(BF16)
            for n, at in enumerate(pair):
                cols = slice(n * tok, (n + 1) * tok)
                out_refs[at][h * size : (h + 1) * size, :] = o[0:size, cols].astype(BF16)
                stats[n] += [top[:, cols].astype(F32), hi[:, cols].astype(F32), lo[:, cols].astype(F32)]
        for n, at in enumerate(pair):
            rest = jnp.zeros((PAD - 3 * PER, tok), F32)
            out_refs[at][PER * size :, :] = jnp.concatenate(stats[n] + [rest], axis=0).astype(BF16)


def combine_kernel(n, *refs):
    parts, out_ref = refs[:n], refs[n]
    size = parts[0].shape[1]
    rate = size ** -0.5 * math.log2(math.e)
    core = lax.rem(lax.axis_index("inner"), CORES)
    for x in range(CORES):
        mine = parts[x::CORES]
        pair = jnp.bitwise_xor(core, x)
        stats = [part[PER * size :, :].astype(F32) for part in mine]
        for h in range(PER):
            tops = [s[3 * h : 3 * h + 1, :] for s in stats]
            best = functools.reduce(jnp.maximum, tops)
            factors = [jnp.exp2((t - best) * rate) for t in tops]
            denom = sum(f * (s[3 * h + 1 : 3 * h + 2, :] + s[3 * h + 2 : 3 * h + 3, :]) for f, s in zip(factors, stats))
            numer = sum(f * part[h * size : (h + 1) * size, :].astype(F32) for f, part in zip(factors, mine))
            cols = pl.ds(pl.multiple_of((pair * PER + h) * size, size), size)
            out_ref[:, cols] = (numer / denom).T.astype(BF16)


def vmem(n=1):
    return [pl.BlockSpec(memory_space=pltpu.VMEM)] * n


def shards(n_out, n_in, queries, keys, values, block_pos):
    tok, width = queries.shape
    size = width // HEADS
    chips = n_in // CORES
    params = pltpu.CompilerParams(vmem_limit_bytes=40 * 1024 * 1024)
    q_piece = jax.ShapeDtypeStruct((PER * tok + PAD, size), BF16)
    kv_piece = jax.ShapeDtypeStruct((2 * PER * tok + PAD, size), BF16)
    with jax.named_scope("pack"):
        q_same, kv_same, q_other, kv_other = pl.pallas_call(
            pack_kernel,
            out_shape=(q_piece, kv_piece, q_piece, kv_piece),
            in_specs=[pl.BlockSpec(memory_space=pltpu.SMEM)] + [pl.BlockSpec(memory_space=pltpu.HBM)] * 3,
            out_specs=tuple(vmem(4)),
            scratch_shapes=[pltpu.VMEM((tok, width), BF16), pltpu.SemaphoreType.DMA((1 + 4 * PER,))],
            compiler_params=params,
            name="pack",
        )(block_pos, queries, keys, values)

    def along_inner(r, x):
        return [(w * CORES + c, (w + r) % chips * CORES + (c ^ x)) for w in range(chips) for c in range(CORES)]

    def along_plane(r, x):
        return [
            (o * n_in + w * CORES + c, (o + r) % n_out * n_in + w * CORES + (c ^ x))
            for o in range(n_out)
            for w in range(chips)
            for c in range(CORES)
        ]

    with jax.named_scope("exchange"):
        q_parts, kv_parts = [], []
        for r in range(n_out):
            for x in range(CORES):
                piece = (kv_same, kv_other)[x]
                kv_parts.append(piece if r + x == 0 else lax.ppermute(piece, ("outer", "inner"), along_plane(r, x)))
        for r in range(chips):
            for x in range(CORES):
                piece = (q_same, q_other)[x]
                q_parts.append(piece if r + x == 0 else lax.ppermute(piece, "inner", along_inner(r, x)))
    nq, nk = len(q_parts), len(kv_parts)
    with jax.named_scope("attend"):
        parts = pl.pallas_call(
            functools.partial(attend_kernel, nq, nk),
            out_shape=(jax.ShapeDtypeStruct((PER * size + PAD, tok), BF16),) * nq,
            in_specs=vmem(nq + nk),
            out_specs=tuple(vmem(nq)),
            scratch_shapes=[
                pltpu.VMEM((PER, nk * tok, size), BF16),
                pltpu.VMEM((PER, size + PAD, nk * tok), BF16),
                pltpu.VMEM((nk, 1, 2 * tok), F32),
            ],
            compiler_params=params,
            name="attend",
        )(*q_parts, *kv_parts)
    with jax.named_scope("return"):
        back = []
        for i, part in enumerate(parts):
            r, x = i // CORES, i % CORES
            back.append(part if i == 0 else lax.ppermute(part, "inner", along_inner(-r, x)))
    with jax.named_scope("combine"):
        return pl.pallas_call(
            functools.partial(combine_kernel, nq),
            out_shape=jax.ShapeDtypeStruct((tok, width), BF16),
            in_specs=vmem(nq),
            out_specs=vmem()[0],
            compiler_params=params,
            name="combine",
        )(*back)


def solution(mesh):
    n_out, n_in = mesh.shape["outer"], mesh.shape["inner"]
    return jax.shard_map(
        functools.partial(shards, n_out, n_in),
        mesh=mesh,
        in_specs=(
            P(("outer", "inner"), None),
            P(("outer", "inner"), None),
            P(("outer", "inner"), None),
            P(("outer", "inner")),
        ),
        out_specs=P(("outer", "inner"), None),
        check_vma=False,
    )
```

```python
import functools
import math

import jax
import jax.numpy as jnp
from jax import lax
from jax.experimental import pallas as pl
from jax.experimental.pallas import tpu as pltpu
from jax.sharding import PartitionSpec as P

HEADS = 4
CORES = 2
PER = HEADS // CORES
PAD = 16
LOW = -1e30
FLOOR = -1e29
BF16 = jnp.bfloat16
F32 = jnp.float32


def nt_dot(a, b):
    return lax.dot_general(a, b, (((1,), (1,)), ((), ())), preferred_element_type=F32)


def merge_kernel(p0, p1, q0, q1, k0, k1, v0, v1, q_out, kv_out):
    tok = q0.shape[0]
    size = q0.shape[1] // HEADS
    core = lax.rem(lax.axis_index("inner"), CORES)
    both = CORES * tok
    for b, (p, q, k, v) in enumerate(((p0, q0, k0, v0), (p1, q1, k1, v1))):
        for j in range(PER):
            cols = pl.ds(pl.multiple_of((core * PER + j) * size, size), size)
            q_out[j * both + b * tok : j * both + (b + 1) * tok, :] = q[:, cols]
            kv_out[j * both + b * tok : j * both + (b + 1) * tok, :] = k[:, cols]
            at = (PER + j) * both + b * tok
            kv_out[at : at + tok, :] = v[:, cols].astype(F32).T.astype(BF16)
    half = PAD // CORES
    pos = jnp.concatenate([jnp.full((half, size), p[0].astype(F32), F32) for p in (p0, p1)], axis=0).astype(BF16)
    q_out[PER * both :, :] = pos
    kv_out[2 * PER * both :, :] = pos


def attend_kernel(nk, q_ref, *refs):
    kv_refs, out_refs = refs[:nk], refs[nk:]
    size = q_ref.shape[1]
    tok = size
    both = CORES * tok
    half = PAD // CORES
    rate = size ** -0.5 * math.log2(math.e)
    rows = lax.broadcasted_iota(jnp.int32, (tok, both), 0).astype(F32)
    lanes = lax.broadcasted_iota(jnp.int32, (1, tok), 1).astype(F32)

    def start_of(ref, at):
        first = ref[at : at + PAD, :].astype(F32)
        return [first[b * half : b * half + 1, :] * tok for b in range(CORES)]

    qpos = jnp.concatenate([s + lanes for s in start_of(q_ref, PER * both)], axis=1)
    limits = []
    for ref in kv_refs:
        for s in start_of(ref, 2 * PER * both):
            limits.append(qpos - jnp.concatenate([s] * CORES, axis=1))
    stats = [[] for _ in range(CORES)]
    for h in range(PER):
        q = q_ref[h * both : (h + 1) * both, :]
        parts = []
        for j, ref in enumerate(kv_refs):
            s = nt_dot(ref[h * both : (h + 1) * both, :], q)
            for b in range(CORES):
                parts.append(jnp.where(rows <= limits[j * CORES + b], s[b * tok : (b + 1) * tok, :], LOW))
        s = jnp.concatenate(parts, axis=0)
        top = jnp.maximum(jnp.max(s, axis=0, keepdims=True), FLOOR).astype(BF16)
        p = jnp.exp2((s - top.astype(F32)) * rate).astype(BF16)
        at = (PER + h) * both
        vt = jnp.concatenate(
            [ref[at + b * tok : at + (b + 1) * tok, :] for ref in kv_refs for b in range(CORES)], axis=1
        )
        vt = jnp.concatenate([vt, jnp.ones((PAD, vt.shape[1]), BF16)], axis=0)
        o = jnp.dot(vt, p, preferred_element_type=F32)
        total = o[size : size + 1, :]
        hi = total.astype(BF16)
        lo = (total - hi.astype(F32)).astype(BF16)
        for b in range(CORES):
            cols = slice(b * tok, (b + 1) * tok)
            out_refs[b][h * size : (h + 1) * size, :] = o[0:size, cols].astype(BF16)
            stats[b] += [top[:, cols].astype(F32), hi[:, cols].astype(F32), lo[:, cols].astype(F32)]
    for b in range(CORES):
        rest = jnp.zeros((PAD - 3 * PER, tok), F32)
        out_refs[b][PER * size :, :] = jnp.concatenate(stats[b] + [rest], axis=0).astype(BF16)


def combine_kernel(n, *refs):
    parts, out_ref = refs[:n], refs[n]
    size = parts[0].shape[1]
    rate = size ** -0.5 * math.log2(math.e)
    core = lax.rem(lax.axis_index("inner"), CORES)
    for x in range(CORES):
        mine = parts[x::CORES]
        pair = jnp.bitwise_xor(core, x)
        stats = [part[PER * size :, :].astype(F32) for part in mine]
        for h in range(PER):
            tops = [s[3 * h : 3 * h + 1, :] for s in stats]
            best = functools.reduce(jnp.maximum, tops)
            factors = [jnp.exp2((t - best) * rate) for t in tops]
            denom = sum(f * (s[3 * h + 1 : 3 * h + 2, :] + s[3 * h + 2 : 3 * h + 3, :]) for f, s in zip(factors, stats))
            numer = sum(f * part[h * size : (h + 1) * size, :].astype(F32) for f, part in zip(factors, mine))
            cols = pl.ds(pl.multiple_of((pair * PER + h) * size, size), size)
            out_ref[:, cols] = (numer / denom).T.astype(BF16)


def vmem(n=1):
    return [pl.BlockSpec(memory_space=pltpu.VMEM)] * n


def shards(n_out, n_in, queries, keys, values, block_pos):
    tok, width = queries.shape
    size = width // HEADS
    chips = n_in // CORES
    both = CORES * tok
    params = pltpu.CompilerParams(vmem_limit_bytes=40 * 1024 * 1024)

    def along_inner(r, x):
        return [(w * CORES + c, (w ^ r) * CORES + (c ^ x)) for w in range(chips) for c in range(CORES)]

    with jax.named_scope("swap"):
        other = [lax.ppermute(a, "inner", along_inner(0, 1)) for a in (queries, keys, values, block_pos)]
    with jax.named_scope("merge"):
        smem = [pl.BlockSpec(memory_space=pltpu.SMEM)]
        q_piece, kv_piece = pl.pallas_call(
            merge_kernel,
            out_shape=(
                jax.ShapeDtypeStruct((PER * both + PAD, size), BF16),
                jax.ShapeDtypeStruct((2 * PER * both + PAD, size), BF16),
            ),
            in_specs=smem * 2 + vmem(6),
            out_specs=tuple(vmem(2)),
            compiler_params=params,
            name="merge",
        )(block_pos, other[3], queries, other[0], keys, other[1], values, other[2])
    with jax.named_scope("exchange"):
        kv = [kv_piece]
        for r in range(1, n_out):
            kv.append(lax.ppermute(kv_piece, "outer", [(o, o ^ r) for o in range(n_out)]))
        qs = [q_piece]
        for r in range(1, chips):
            qs.append(lax.ppermute(q_piece, "inner", along_inner(r, 0)))
    back = [None] * n_in
    work = 4 * PER * both * n_out * both * size
    for r in reversed(range(chips)):
        with jax.named_scope("attend"):
            parts = pl.pallas_call(
                functools.partial(attend_kernel, n_out),
                out_shape=(jax.ShapeDtypeStruct((PER * size + PAD, tok), BF16),) * CORES,
                in_specs=vmem(1 + n_out),
                out_specs=tuple(vmem(CORES)),
                compiler_params=params,
                cost_estimate=pl.CostEstimate(flops=work, bytes_accessed=2**20, transcendentals=work // (4 * size)),
                name="attend",
            )(qs[r], *kv)
        with jax.named_scope("return"):
            for x in range(CORES):
                part = parts[x]
                back[r * CORES + x] = part if r + x == 0 else lax.ppermute(part, "inner", along_inner(r, x))
    with jax.named_scope("combine"):
        return pl.pallas_call(
            functools.partial(combine_kernel, n_in),
            out_shape=jax.ShapeDtypeStruct((tok, width), BF16),
            in_specs=vmem(n_in),
            out_specs=vmem()[0],
            compiler_params=params,
            name="combine",
        )(*back)


def solution(mesh):
    n_out, n_in = mesh.shape["outer"], mesh.shape["inner"]
    return jax.shard_map(
        functools.partial(shards, n_out, n_in),
        mesh=mesh,
        in_specs=(
            P(("outer", "inner"), None),
            P(("outer", "inner"), None),
            P(("outer", "inner"), None),
            P(("outer", "inner")),
        ),
        out_specs=P(("outer", "inner"), None),
        check_vma=False,
    )
```

```python
import functools
import math

import jax
import jax.numpy as jnp
from jax import lax
from jax.experimental import pallas as pl
from jax.experimental.pallas import tpu as pltpu
from jax.sharding import PartitionSpec as P

HEADS = 4
CORES = 2
PER = HEADS // CORES
PAD = 16
LOW = -1e30
FLOOR = -1e29
BF16 = jnp.bfloat16
F32 = jnp.float32


def nt_dot(a, b):
    return lax.dot_general(a, b, (((1,), (1,)), ((), ())), preferred_element_type=F32)


def merge_kernel(p0, p1, own, q1, k1, v1, q_out, kv_out):
    tok = q1.shape[0]
    size = q1.shape[1] // HEADS
    q0, k0, v0 = (own.at[i * tok : (i + 1) * tok, :] for i in range(3))
    core = lax.rem(lax.axis_index("inner"), CORES)
    both = CORES * tok
    for b, (p, q, k, v) in enumerate(((p0, q0, k0, v0), (p1, q1, k1, v1))):
        for j in range(PER):
            cols = pl.ds(pl.multiple_of((core * PER + j) * size, size), size)
            q_out[j * both + b * tok : j * both + (b + 1) * tok, :] = q[:, cols]
            kv_out[j * both + b * tok : j * both + (b + 1) * tok, :] = k[:, cols]
            at = (PER + j) * both + b * tok
            kv_out[at : at + tok, :] = v[:, cols].astype(F32).T.astype(BF16)
    half = PAD // CORES
    pos = jnp.concatenate([jnp.full((half, size), p[0].astype(F32), F32) for p in (p0, p1)], axis=0).astype(BF16)
    q_out[PER * both :, :] = pos
    kv_out[2 * PER * both :, :] = pos


def attend_kernel(nk, q_ref, *refs):
    kv_refs, out_refs = refs[:nk], refs[nk:]
    size = q_ref.shape[1]
    tok = size
    both = CORES * tok
    half = PAD // CORES
    rate = size ** -0.5 * math.log2(math.e)
    rows = lax.broadcasted_iota(jnp.int32, (tok, both), 0).astype(F32)
    lanes = lax.broadcasted_iota(jnp.int32, (1, tok), 1).astype(F32)

    def start_of(ref, at):
        first = ref[at : at + PAD, :].astype(F32)
        return [first[b * half : b * half + 1, :] * tok for b in range(CORES)]

    qpos = jnp.concatenate([s + lanes for s in start_of(q_ref, PER * both)], axis=1)
    limits = []
    for ref in kv_refs:
        for s in start_of(ref, 2 * PER * both):
            limits.append(qpos - jnp.concatenate([s] * CORES, axis=1))
    stats = [[] for _ in range(CORES)]
    for h in range(PER):
        q = q_ref[h * both : (h + 1) * both, :]
        parts = []
        for j, ref in enumerate(kv_refs):
            s = nt_dot(ref[h * both : (h + 1) * both, :], q)
            for b in range(CORES):
                parts.append(jnp.where(rows <= limits[j * CORES + b], s[b * tok : (b + 1) * tok, :], LOW))
        s = jnp.concatenate(parts, axis=0)
        top = jnp.maximum(jnp.max(s, axis=0, keepdims=True), FLOOR).astype(BF16)
        p = jnp.exp2((s - top.astype(F32)) * rate).astype(BF16)
        at = (PER + h) * both
        vt = jnp.concatenate(
            [ref[at + b * tok : at + (b + 1) * tok, :] for ref in kv_refs for b in range(CORES)], axis=1
        )
        vt = jnp.concatenate([vt, jnp.ones((PAD, vt.shape[1]), BF16)], axis=0)
        o = jnp.dot(vt, p, preferred_element_type=F32)
        total = o[size : size + 1, :]
        hi = total.astype(BF16)
        lo = (total - hi.astype(F32)).astype(BF16)
        for b in range(CORES):
            cols = slice(b * tok, (b + 1) * tok)
            out_refs[b][h * size : (h + 1) * size, :] = o[0:size, cols].astype(BF16)
            stats[b] += [top[:, cols].astype(F32), hi[:, cols].astype(F32), lo[:, cols].astype(F32)]
    for b in range(CORES):
        rest = jnp.zeros((PAD - 3 * PER, tok), F32)
        out_refs[b][PER * size :, :] = jnp.concatenate(stats[b] + [rest], axis=0).astype(BF16)


def combine_kernel(n, *refs):
    parts, out_ref = refs[:n], refs[n]
    size = parts[0].shape[1]
    rate = size ** -0.5 * math.log2(math.e)
    core = lax.rem(lax.axis_index("inner"), CORES)
    for x in range(CORES):
        mine = parts[x::CORES]
        pair = jnp.bitwise_xor(core, x)
        stats = [part[PER * size :, :].astype(F32) for part in mine]
        for h in range(PER):
            tops = [s[3 * h : 3 * h + 1, :] for s in stats]
            best = functools.reduce(jnp.maximum, tops)
            factors = [jnp.exp2((t - best) * rate) for t in tops]
            denom = sum(f * (s[3 * h + 1 : 3 * h + 2, :] + s[3 * h + 2 : 3 * h + 3, :]) for f, s in zip(factors, stats))
            numer = sum(f * part[h * size : (h + 1) * size, :].astype(F32) for f, part in zip(factors, mine))
            cols = pl.ds(pl.multiple_of((pair * PER + h) * size, size), size)
            out_ref[:, cols] = (numer / denom).T.astype(BF16)


def vmem(n=1):
    return [pl.BlockSpec(memory_space=pltpu.VMEM)] * n


def shards(n_out, n_in, queries, keys, values, block_pos):
    tok, width = queries.shape
    size = width // HEADS
    chips = n_in // CORES
    both = CORES * tok
    params = pltpu.CompilerParams(vmem_limit_bytes=40 * 1024 * 1024)

    def along_inner(r, x):
        return [(w * CORES + c, (w ^ r) * CORES + (c ^ x)) for w in range(chips) for c in range(CORES)]

    with jax.named_scope("swap"):
        other = [lax.ppermute(a, "inner", along_inner(0, 1)) for a in (queries, keys, values, block_pos)]
        own = jnp.concatenate([queries, keys, values], axis=0)
    with jax.named_scope("merge"):
        smem = [pl.BlockSpec(memory_space=pltpu.SMEM)]
        q_piece, kv_piece = pl.pallas_call(
            merge_kernel,
            out_shape=(
                jax.ShapeDtypeStruct((PER * both + PAD, size), BF16),
                jax.ShapeDtypeStruct((2 * PER * both + PAD, size), BF16),
            ),
            in_specs=smem * 2 + vmem(4),
            out_specs=tuple(vmem(2)),
            compiler_params=params,
            name="merge",
        )(block_pos, other[3], own, *other[:3])
    with jax.named_scope("exchange"):
        kv = [kv_piece]
        for r in range(1, n_out):
            kv.append(lax.ppermute(kv_piece, "outer", [(o, o ^ r) for o in range(n_out)]))
        qs = [q_piece]
        for r in range(1, chips):
            piece = lax.optimization_barrier((q_piece, kv[1]))[0] if r == 1 else q_piece
            qs.append(lax.ppermute(piece, "inner", along_inner(r, 0)))
    back = [None] * n_in
    work = 4 * PER * both * n_out * both * size
    for r in reversed(range(chips)):
        with jax.named_scope("attend"):
            parts = pl.pallas_call(
                functools.partial(attend_kernel, n_out),
                out_shape=(jax.ShapeDtypeStruct((PER * size + PAD, tok), BF16),) * CORES,
                in_specs=vmem(1 + n_out),
                out_specs=tuple(vmem(CORES)),
                compiler_params=params,
                cost_estimate=pl.CostEstimate(flops=work, bytes_accessed=2**20, transcendentals=work // (4 * size)),
                name="attend",
            )(qs[r], *kv)
        with jax.named_scope("return"):
            for x in range(CORES):
                part = parts[x]
                back[r * CORES + x] = part if r + x == 0 else lax.ppermute(part, "inner", along_inner(r, x))
    with jax.named_scope("combine"):
        return pl.pallas_call(
            functools.partial(combine_kernel, n_in),
            out_shape=jax.ShapeDtypeStruct((tok, width), BF16),
            in_specs=vmem(n_in),
            out_specs=vmem()[0],
            compiler_params=params,
            name="combine",
        )(*back)


def solution(mesh):
    n_out, n_in = mesh.shape["outer"], mesh.shape["inner"]
    return jax.shard_map(
        functools.partial(shards, n_out, n_in),
        mesh=mesh,
        in_specs=(
            P(("outer", "inner"), None),
            P(("outer", "inner"), None),
            P(("outer", "inner"), None),
            P(("outer", "inner")),
        ),
        out_specs=P(("outer", "inner"), None),
        check_vma=False,
    )
```

```python
import functools
import math

import jax
import jax.numpy as jnp
from jax import lax
from jax.experimental import pallas as pl
from jax.experimental.pallas import tpu as pltpu
from jax.sharding import PartitionSpec as P

HEADS = 4
CORES = 2
PER = HEADS // CORES
PAD = 16
LOW = -1e30
FLOOR = -1e29
BF16 = jnp.bfloat16
F32 = jnp.float32


def nt_dot(a, b):
    return lax.dot_general(a, b, (((1,), (1,)), ((), ())), preferred_element_type=F32)


def merge_kernel(p0, p1, own, q1, k1, v1, q_out, kv_out):
    tok = q1.shape[0]
    size = q1.shape[1] // HEADS
    q0, k0, v0 = (own.at[i * tok : (i + 1) * tok, :] for i in range(3))
    core = lax.rem(lax.axis_index("inner"), CORES)
    both = CORES * tok
    for b, (q, k, v) in enumerate(((q0, k0, v0), (q1, k1, v1))):
        for j in range(PER):
            cols = pl.ds(pl.multiple_of((core * PER + j) * size, size), size)
            q_out[j * both + b * tok : j * both + (b + 1) * tok, :] = q[:, cols]
            kv_out[j * both + b * tok : j * both + (b + 1) * tok, :] = k[:, cols]
            at = PAD + (PER + j) * both + b * tok
            kv_out[at : at + tok, :] = v[:, cols].astype(F32).T.astype(BF16)
    half = PAD // CORES
    pos = jnp.concatenate([jnp.full((half, size), p[0].astype(F32), F32) for p in (p0, p1)], axis=0).astype(BF16)
    q_out[PER * both :, :] = pos
    kv_out[PER * both : PER * both + PAD, :] = pos


def attend_kernel(wide, where, q_ref, *refs):
    n = 1 + max(w[2] for w in where)
    kv_refs, out_refs = refs[:n], refs[n:]
    size = q_ref.shape[1]
    tok = size
    both = CORES * tok
    half = PAD // CORES
    block = PER * size + PAD
    rate = size ** -0.5 * math.log2(math.e)
    rows = lax.broadcasted_iota(jnp.int32, (tok, both), 0).astype(F32)
    lanes = lax.broadcasted_iota(jnp.int32, (1, tok), 1).astype(F32)

    def start_of(ref, at):
        first = ref[at : at + PAD, :].astype(F32)
        return [first[b * half : b * half + 1, :] * tok for b in range(CORES)]

    def store(b, at, value):
        if wide:
            out_refs[0][b * block + at : b * block + at + value.shape[0], :] = value
        else:
            out_refs[b][at : at + value.shape[0], :] = value

    qpos = jnp.concatenate([s + lanes for s in start_of(q_ref, PER * both)], axis=1)
    limits = []
    for k, k_at, _, _ in where:
        for s in start_of(kv_refs[k], k_at + PER * both):
            limits.append(qpos - jnp.concatenate([s] * CORES, axis=1))
    stats = [[] for _ in range(CORES)]
    for h in range(PER):
        q = q_ref[h * both : (h + 1) * both, :]
        parts, vals = [], []
        for j, (k, k_at, v, v_at) in enumerate(where):
            s = nt_dot(kv_refs[k][k_at + h * both : k_at + (h + 1) * both, :], q)
            for b in range(CORES):
                parts.append(jnp.where(rows <= limits[j * CORES + b], s[b * tok : (b + 1) * tok, :], LOW))
                at = v_at + h * both + b * tok
                vals.append(kv_refs[v][at : at + tok, :])
        s = jnp.concatenate(parts, axis=0)
        top = jnp.maximum(jnp.max(s, axis=0, keepdims=True), FLOOR).astype(BF16)
        p = jnp.exp2((s - top.astype(F32)) * rate).astype(BF16)
        vt = jnp.concatenate(vals, axis=1)
        vt = jnp.concatenate([vt, jnp.ones((PAD, vt.shape[1]), BF16)], axis=0)
        o = jnp.dot(vt, p, preferred_element_type=F32)
        total = o[size : size + 1, :]
        hi = total.astype(BF16)
        lo = (total - hi.astype(F32)).astype(BF16)
        for b in range(CORES):
            cols = slice(b * tok, (b + 1) * tok)
            store(b, h * size, o[0:size, cols].astype(BF16))
            stats[b] += [top[:, cols].astype(F32), hi[:, cols].astype(F32), lo[:, cols].astype(F32)]
    for b in range(CORES):
        rest = jnp.zeros((PAD - 3 * PER, tok), F32)
        store(b, PER * size, jnp.concatenate(stats[b] + [rest], axis=0).astype(BF16))


def joined(parts, stats, h, rate):
    size = parts[0].shape[0]
    tops = [s[3 * h : 3 * h + 1, :] for s in stats]
    best = functools.reduce(jnp.maximum, tops)
    factors = [jnp.exp2((t - best) * rate) for t in tops]
    total = sum(f * (s[3 * h + 1 : 3 * h + 2, :] + s[3 * h + 2 : 3 * h + 3, :]) for f, s in zip(factors, stats))
    numer = sum(f * part.astype(F32) for f, part in zip(factors, parts))
    return best, total, numer


def add_kernel(n, wide, *refs):
    size = refs[0].shape[1]
    block = PER * size + PAD
    rate = size ** -0.5 * math.log2(math.e)
    for b in range(CORES):
        base = b * block
        stats = [ref[base + PER * size : base + block, :].astype(F32) for ref in refs[:n]]
        out, at = (refs[n], base) if wide else (refs[n + b], 0)
        rows = []
        for h in range(PER):
            parts = [ref[base + h * size : base + (h + 1) * size, :] for ref in refs[:n]]
            best, total, numer = joined(parts, stats, h, rate)
            hi = total.astype(BF16).astype(F32)
            rows += [best, hi, total - hi]
            out[at + h * size : at + (h + 1) * size, :] = numer.astype(BF16)
        rest = jnp.zeros((PAD - 3 * PER, size), F32)
        out[at + PER * size : at + block, :] = jnp.concatenate(rows + [rest], axis=0).astype(BF16)


def combine_kernel(n, *refs):
    parts, out_ref = refs[:n], refs[n]
    size = parts[0].shape[1]
    rate = size ** -0.5 * math.log2(math.e)
    core = lax.rem(lax.axis_index("inner"), CORES)
    for x in range(CORES):
        mine = parts[x::CORES]
        pair = jnp.bitwise_xor(core, x)
        stats = [part[PER * size :, :].astype(F32) for part in mine]
        for h in range(PER):
            _, total, numer = joined([part[h * size : (h + 1) * size, :] for part in mine], stats, h, rate)
            cols = pl.ds(pl.multiple_of((pair * PER + h) * size, size), size)
            out_ref[:, cols] = (numer / total).T.astype(BF16)


def vmem(n=1):
    return [pl.BlockSpec(memory_space=pltpu.VMEM)] * n


def shards(n_out, n_in, queries, keys, values, block_pos):
    tok, width = queries.shape
    size = width // HEADS
    chips = n_in // CORES
    both = CORES * tok
    params = pltpu.CompilerParams(vmem_limit_bytes=40 * 1024 * 1024)

    def along_inner(r, x):
        return [(w * CORES + c, (w ^ r) * CORES + (c ^ x)) for w in range(chips) for c in range(CORES)]

    with jax.named_scope("swap"):
        other = [lax.ppermute(a, "inner", along_inner(0, 1)) for a in (queries, keys, values, block_pos)]
        own = jnp.concatenate([queries, keys, values], axis=0)
    with jax.named_scope("merge"):
        smem = [pl.BlockSpec(memory_space=pltpu.SMEM)]
        q_piece, kv_piece = pl.pallas_call(
            merge_kernel,
            out_shape=(
                jax.ShapeDtypeStruct((PER * both + PAD, size), BF16),
                jax.ShapeDtypeStruct((2 * PER * both + PAD, size), BF16),
            ),
            in_specs=smem * 2 + vmem(4),
            out_specs=tuple(vmem(2)),
            compiler_params=params,
            name="merge",
        )(block_pos, other[3], own, *other[:3])
    half = PER * both + PAD
    block = PER * size + PAD

    def low(r):
        return r & -r

    def high(r):
        return 1 << (r.bit_length() - 1)

    def single(r):
        return r == low(r)

    def over(a, r):
        return lax.ppermute(a, "outer", [(o, o ^ r) for o in range(n_out)])

    with jax.named_scope("exchange"):
        whole = {0: kv_piece}
        for r in range(1, n_out):
            if single(r):
                whole[r] = over(kv_piece, r)
        k_part = {r: a[:half, :] for r, a in whole.items() if r}
        v_part = {r: a[half:, :] for r, a in whole.items() if r}
        for r in range(1, n_out):
            if not single(r):
                k_part[r] = over(k_part[r - high(r)], high(r))
        for r in sorted(range(1, n_out), key=lambda r: r.bit_count()):
            if not single(r):
                v_part[r] = over(v_part[r - low(r)], low(r))
        q_by = {0: q_piece}
        bit = chips // 2
        while bit:
            for r in sorted(q_by):
                q_by[r | bit] = lax.ppermute(q_by[r], "inner", along_inner(bit, 0))
            bit //= 2
    kv, where = [], []
    for r in range(n_out):
        if r in whole:
            where.append((len(kv), 0, len(kv), half))
            kv.append(whole[r])
        else:
            where.append((len(kv), 0, len(kv) + 1, 0))
            kv += [k_part[r], v_part[r]]

    def shapes(wide):
        rows = CORES * block if wide else block
        return (jax.ShapeDtypeStruct((rows, tok), BF16),) * (1 if wide else CORES)

    def attend(r, wide):
        work = 4 * PER * both * n_out * both * size
        with jax.named_scope("attend"):
            return pl.pallas_call(
                functools.partial(attend_kernel, wide, tuple(where)),
                out_shape=shapes(wide),
                in_specs=vmem(1 + len(kv)),
                out_specs=tuple(vmem(len(shapes(wide)))),
                compiler_params=params,
                cost_estimate=pl.CostEstimate(flops=work, bytes_accessed=2**20, transcendentals=work // (4 * size)),
                name="attend",
            )(q_by[r], *kv)

    def add(arrays, wide):
        with jax.named_scope("add"):
            return pl.pallas_call(
                functools.partial(add_kernel, len(arrays), wide),
                out_shape=shapes(wide),
                in_specs=vmem(len(arrays)),
                out_specs=tuple(vmem(len(shapes(wide)))),
                compiler_params=params,
                name="add",
            )(*arrays)

    arrived = {r: [] for r in range(chips)}
    ends = []
    for r in sorted(range(1, chips), key=lambda r: (low(r), -r)):
        last = single(r)
        alone = not (low(r) > 1)
        parts = attend(r, not (last and alone))
        if not alone:
            parts = add([parts[0], *arrived[r]], not last)
        with jax.named_scope("return"):
            if last:
                ends += [lax.ppermute(parts[x], "inner", along_inner(r, x)) for x in range(CORES)]
            else:
                arrived[r - low(r)].append(lax.ppermute(parts[0], "inner", along_inner(low(r), 0)))
    own = attend(0, False)
    with jax.named_scope("return"):
        ends = [own[0], lax.ppermute(own[1], "inner", along_inner(0, 1))] + ends
    with jax.named_scope("combine"):
        return pl.pallas_call(
            functools.partial(combine_kernel, len(ends)),
            out_shape=jax.ShapeDtypeStruct((tok, width), BF16),
            in_specs=vmem(len(ends)),
            out_specs=vmem()[0],
            compiler_params=params,
            name="combine",
        )(*ends)


def solution(mesh):
    n_out, n_in = mesh.shape["outer"], mesh.shape["inner"]
    return jax.shard_map(
        functools.partial(shards, n_out, n_in),
        mesh=mesh,
        in_specs=(
            P(("outer", "inner"), None),
            P(("outer", "inner"), None),
            P(("outer", "inner"), None),
            P(("outer", "inner")),
        ),
        out_specs=P(("outer", "inner"), None),
        check_vma=False,
    )
```

```python
import functools
import math

import jax
import jax.numpy as jnp
from jax import lax
from jax.experimental import pallas as pl
from jax.experimental.pallas import tpu as pltpu
from jax.sharding import PartitionSpec as P

HEADS = 4
CORES = 2
PER = HEADS // CORES
PAD = 16
LOW = -1e30
FLOOR = -1e29
BF16 = jnp.bfloat16
F32 = jnp.float32


def nt_dot(a, b):
    return lax.dot_general(a, b, (((1,), (1,)), ((), ())), preferred_element_type=F32)


def merge_kernel(p0, p1, own, q1, k1, v1, q_out, kv_out):
    tok = q1.shape[0]
    size = q1.shape[1] // HEADS
    q0, k0, v0 = (own.at[i * tok : (i + 1) * tok, :] for i in range(3))
    core = lax.rem(lax.axis_index("inner"), CORES)
    both = CORES * tok
    for b, (q, k, v) in enumerate(((q0, k0, v0), (q1, k1, v1))):
        for j in range(PER):
            cols = pl.ds(pl.multiple_of((core * PER + j) * size, size), size)
            q_out[j * both + b * tok : j * both + (b + 1) * tok, :] = q[:, cols]
            kv_out[j * both + b * tok : j * both + (b + 1) * tok, :] = k[:, cols]
            at = PAD + (PER + j) * both + b * tok
            kv_out[at : at + tok, :] = v[:, cols].astype(F32).T.astype(BF16)
    half = PAD // CORES
    pos = jnp.concatenate([jnp.full((half, size), p[0].astype(F32), F32) for p in (p0, p1)], axis=0).astype(BF16)
    q_out[PER * both :, :] = pos
    kv_out[PER * both : PER * both + PAD, :] = pos


def attend_kernel(wide, where, q_ref, *refs):
    n = 1 + max(w[2] for w in where)
    kv_refs, out_refs = refs[:n], refs[n:]
    size = q_ref.shape[1]
    tok = size
    both = CORES * tok
    half = PAD // CORES
    block = PER * size + PAD
    rate = size ** -0.5 * math.log2(math.e)
    rows = lax.broadcasted_iota(jnp.int32, (tok, both), 0).astype(F32)
    lanes = lax.broadcasted_iota(jnp.int32, (1, tok), 1).astype(F32)

    def start_of(ref, at):
        first = ref[at : at + PAD, :].astype(F32)
        return [first[b * half : b * half + 1, :] * tok for b in range(CORES)]

    def store(b, at, value):
        if wide:
            out_refs[0][b * block + at : b * block + at + value.shape[0], :] = value
        else:
            out_refs[b][at : at + value.shape[0], :] = value

    qpos = jnp.concatenate([s + lanes for s in start_of(q_ref, PER * both)], axis=1)
    limits = []
    for k, k_at, _, _ in where:
        for s in start_of(kv_refs[k], k_at + PER * both):
            limits.append(qpos - jnp.concatenate([s] * CORES, axis=1))
    stats = [[] for _ in range(CORES)]
    for h in range(PER):
        q = q_ref[h * both : (h + 1) * both, :]
        parts, vals = [], []
        for j, (k, k_at, v, v_at) in enumerate(where):
            s = nt_dot(kv_refs[k][k_at + h * both : k_at + (h + 1) * both, :], q)
            for b in range(CORES):
                parts.append(jnp.where(rows <= limits[j * CORES + b], s[b * tok : (b + 1) * tok, :], LOW))
                at = v_at + h * both + b * tok
                vals.append(kv_refs[v][at : at + tok, :])
        s = jnp.concatenate(parts, axis=0)
        top = jnp.maximum(jnp.max(s, axis=0, keepdims=True), FLOOR).astype(BF16)
        p = jnp.exp2((s - top.astype(F32)) * rate).astype(BF16)
        vt = jnp.concatenate(vals, axis=1)
        vt = jnp.concatenate([vt, jnp.ones((PAD, vt.shape[1]), BF16)], axis=0)
        o = jnp.dot(vt, p, preferred_element_type=F32)
        total = o[size : size + 1, :]
        hi = total.astype(BF16)
        lo = (total - hi.astype(F32)).astype(BF16)
        for b in range(CORES):
            cols = slice(b * tok, (b + 1) * tok)
            store(b, h * size, o[0:size, cols].astype(BF16))
            stats[b] += [top[:, cols].astype(F32), hi[:, cols].astype(F32), lo[:, cols].astype(F32)]
    for b in range(CORES):
        rest = jnp.zeros((PAD - 3 * PER, tok), F32)
        store(b, PER * size, jnp.concatenate(stats[b] + [rest], axis=0).astype(BF16))


def joined(parts, stats, h, rate):
    size = parts[0].shape[0]
    tops = [s[3 * h : 3 * h + 1, :] for s in stats]
    best = functools.reduce(jnp.maximum, tops)
    factors = [jnp.exp2((t - best) * rate) for t in tops]
    total = sum(f * (s[3 * h + 1 : 3 * h + 2, :] + s[3 * h + 2 : 3 * h + 3, :]) for f, s in zip(factors, stats))
    numer = sum(f * part.astype(F32) for f, part in zip(factors, parts))
    return best, total, numer


def add_kernel(n, wide, *refs):
    size = refs[0].shape[1]
    block = PER * size + PAD
    rate = size ** -0.5 * math.log2(math.e)
    for b in range(CORES):
        base = b * block
        stats = [ref[base + PER * size : base + block, :].astype(F32) for ref in refs[:n]]
        out, at = (refs[n], base) if wide else (refs[n + b], 0)
        rows = []
        for h in range(PER):
            parts = [ref[base + h * size : base + (h + 1) * size, :] for ref in refs[:n]]
            best, total, numer = joined(parts, stats, h, rate)
            hi = total.astype(BF16).astype(F32)
            rows += [best, hi, total - hi]
            out[at + h * size : at + (h + 1) * size, :] = numer.astype(BF16)
        rest = jnp.zeros((PAD - 3 * PER, size), F32)
        out[at + PER * size : at + block, :] = jnp.concatenate(rows + [rest], axis=0).astype(BF16)


def combine_kernel(n, *refs):
    parts, out_ref = refs[:n], refs[n]
    size = parts[0].shape[1]
    rate = size ** -0.5 * math.log2(math.e)
    core = lax.rem(lax.axis_index("inner"), CORES)
    for x in range(CORES):
        mine = parts[x::CORES]
        pair = jnp.bitwise_xor(core, x)
        stats = [part[PER * size :, :].astype(F32) for part in mine]
        for h in range(PER):
            _, total, numer = joined([part[h * size : (h + 1) * size, :] for part in mine], stats, h, rate)
            cols = pl.ds(pl.multiple_of((pair * PER + h) * size, size), size)
            out_ref[:, cols] = (numer / total).T.astype(BF16)


def vmem(n=1):
    return [pl.BlockSpec(memory_space=pltpu.VMEM)] * n


def shards(n_out, n_in, queries, keys, values, block_pos):
    tok, width = queries.shape
    size = width // HEADS
    chips = n_in // CORES
    both = CORES * tok
    params = pltpu.CompilerParams(vmem_limit_bytes=40 * 1024 * 1024)

    def along_inner(r, x):
        return [(w * CORES + c, (w ^ r) * CORES + (c ^ x)) for w in range(chips) for c in range(CORES)]

    with jax.named_scope("swap"):
        other = [lax.ppermute(a, "inner", along_inner(0, 1)) for a in (queries, keys, values, block_pos)]
        own = jnp.concatenate([queries, keys, values], axis=0)
    with jax.named_scope("merge"):
        smem = [pl.BlockSpec(memory_space=pltpu.SMEM)]
        q_piece, kv_piece = pl.pallas_call(
            merge_kernel,
            out_shape=(
                jax.ShapeDtypeStruct((PER * both + PAD, size), BF16),
                jax.ShapeDtypeStruct((2 * PER * both + PAD, size), BF16),
            ),
            in_specs=smem * 2 + vmem(4),
            out_specs=tuple(vmem(2)),
            compiler_params=params,
            name="merge",
        )(block_pos, other[3], own, *other[:3])
    half = PER * both + PAD
    block = PER * size + PAD

    def low(r):
        return r & -r

    def high(r):
        return 1 << (r.bit_length() - 1)

    def single(r):
        return r == low(r)

    def after(a, b):
        return lax.optimization_barrier((a, b))[0]

    def over(a, r):
        return lax.ppermute(a, "outer", [(o, o ^ r) for o in range(n_out)])

    with jax.named_scope("exchange"):
        whole = {0: kv_piece}
        for r in range(1, n_out):
            if single(r):
                whole[r] = over(kv_piece, r)
        k_part = {r: a[:half, :] for r, a in whole.items() if r}
        v_part = {r: a[half:, :] for r, a in whole.items() if r}
        for r in range(1, n_out):
            if not single(r):
                k_part[r] = over(k_part[r - high(r)], high(r))
        for r in sorted(range(1, n_out), key=lambda r: r.bit_count()):
            if not single(r):
                v_part[r] = over(v_part[r - low(r)], low(r))
        q_by = {0: q_piece}
        for r in reversed(range(1, chips)):
            piece = after(q_piece, whole[1]) if r == 1 else q_piece
            q_by[r] = lax.ppermute(piece, "inner", along_inner(r, 0))
    kv, where = [], []
    for r in range(n_out):
        if r in whole:
            where.append((len(kv), 0, len(kv), half))
            kv.append(whole[r])
        else:
            where.append((len(kv), 0, len(kv) + 1, 0))
            kv += [k_part[r], v_part[r]]

    def shapes(wide):
        rows = CORES * block if wide else block
        return (jax.ShapeDtypeStruct((rows, tok), BF16),) * (1 if wide else CORES)

    def attend(r, wide, done=None):
        q = q_by[r] if done is None else after(q_by[r], done)
        work = 4 * PER * both * n_out * both * size
        with jax.named_scope("attend"):
            return pl.pallas_call(
                functools.partial(attend_kernel, wide, tuple(where)),
                out_shape=shapes(wide),
                in_specs=vmem(1 + len(kv)),
                out_specs=tuple(vmem(len(shapes(wide)))),
                compiler_params=params,
                cost_estimate=pl.CostEstimate(flops=work, bytes_accessed=2**20, transcendentals=work // (4 * size)),
                name="attend",
            )(q, *kv)

    def add(arrays, wide):
        with jax.named_scope("add"):
            return pl.pallas_call(
                functools.partial(add_kernel, len(arrays), wide),
                out_shape=shapes(wide),
                in_specs=vmem(len(arrays)),
                out_specs=tuple(vmem(len(shapes(wide)))),
                compiler_params=params,
                name="add",
            )(*arrays)

    arrived = {r: [] for r in range(chips)}
    ends = []

    def send(r, parts):
        with jax.named_scope("return"):
            if single(r):
                ends.extend(lax.ppermute(parts[x], "inner", along_inner(r, x)) for x in range(CORES))
            else:
                arrived[r - low(r)].append(lax.ppermute(parts[0], "inner", along_inner(low(r), 0)))

    done = q_by[2] if chips > 2 else None
    partial = {}
    for r in reversed(range(2, chips)):
        partial[r] = attend(r, True, done)
        done = partial[r][0]
    own = attend(0, False, done)
    for r in reversed(range(2, chips)):
        parts = partial[r]
        if arrived[r]:
            parts = add([parts[0], *arrived[r]], not single(r))
        done = parts[0]
        send(r, parts)
    with jax.named_scope("return"):
        piece = own[1] if done is None else after(own[1], done)
        across = lax.ppermute(piece, "inner", along_inner(0, 1))
    if chips > 1:
        send(1, attend(1, False, across))
    ends = [own[0], across] + ends
    with jax.named_scope("combine"):
        return pl.pallas_call(
            functools.partial(combine_kernel, len(ends)),
            out_shape=jax.ShapeDtypeStruct((tok, width), BF16),
            in_specs=vmem(len(ends)),
            out_specs=vmem()[0],
            compiler_params=params,
            name="combine",
        )(*ends)


def solution(mesh):
    n_out, n_in = mesh.shape["outer"], mesh.shape["inner"]
    return jax.shard_map(
        functools.partial(shards, n_out, n_in),
        mesh=mesh,
        in_specs=(
            P(("outer", "inner"), None),
            P(("outer", "inner"), None),
            P(("outer", "inner"), None),
            P(("outer", "inner")),
        ),
        out_specs=P(("outer", "inner"), None),
        check_vma=False,
    )
```

```python
import functools
import math

import jax
import jax.numpy as jnp
from jax import lax
from jax.experimental import pallas as pl
from jax.experimental.pallas import tpu as pltpu
from jax.sharding import PartitionSpec as P

HEADS = 4
CORES = 2
PER = HEADS // CORES
PAD = 16
LOW = -1e30
FLOOR = -1e29
BF16 = jnp.bfloat16
F32 = jnp.float32


def nt_dot(a, b):
    return lax.dot_general(a, b, (((1,), (1,)), ((), ())), preferred_element_type=F32)


def merge_kernel(p0, p1, own, q1, k1, v1, q_out, kv_out):
    tok = q1.shape[0]
    size = q1.shape[1] // HEADS
    q0, k0, v0 = (own.at[i * tok : (i + 1) * tok, :] for i in range(3))
    core = lax.rem(lax.axis_index("inner"), CORES)
    both = CORES * tok
    for b, (q, k, v) in enumerate(((q0, k0, v0), (q1, k1, v1))):
        for j in range(PER):
            cols = pl.ds(pl.multiple_of((core * PER + j) * size, size), size)
            q_out[j * both + b * tok : j * both + (b + 1) * tok, :] = q[:, cols]
            kv_out[j * both + b * tok : j * both + (b + 1) * tok, :] = k[:, cols]
            at = PAD + (PER + j) * both + b * tok
            kv_out[at : at + tok, :] = v[:, cols].astype(F32).T.astype(BF16)
    half = PAD // CORES
    pos = jnp.concatenate([jnp.full((half, size), p[0].astype(F32), F32) for p in (p0, p1)], axis=0).astype(BF16)
    q_out[PER * both :, :] = pos
    kv_out[PER * both : PER * both + PAD, :] = pos


def attend_kernel(wide, where, q_ref, *refs):
    n = 1 + max(w[2] for w in where)
    kv_refs, out_refs = refs[:n], refs[n:]
    size = q_ref.shape[1]
    tok = size
    both = CORES * tok
    half = PAD // CORES
    block = PER * size + PAD
    rate = size ** -0.5 * math.log2(math.e)
    rows = lax.broadcasted_iota(jnp.int32, (tok, both), 0).astype(F32)
    lanes = lax.broadcasted_iota(jnp.int32, (1, tok), 1).astype(F32)

    def start_of(ref, at):
        first = ref[at : at + PAD, :].astype(F32)
        return [first[b * half : b * half + 1, :] * tok for b in range(CORES)]

    def store(b, at, value):
        if wide:
            out_refs[0][b * block + at : b * block + at + value.shape[0], :] = value
        else:
            out_refs[b][at : at + value.shape[0], :] = value

    qpos = jnp.concatenate([s + lanes for s in start_of(q_ref, PER * both)], axis=1)
    limits = []
    for k, k_at, _, _ in where:
        for s in start_of(kv_refs[k], k_at + PER * both):
            limits.append(qpos - jnp.concatenate([s] * CORES, axis=1))
    stats = [[] for _ in range(CORES)]
    for h in range(PER):
        q = q_ref[h * both : (h + 1) * both, :]
        parts, vals = [], []
        for j, (k, k_at, v, v_at) in enumerate(where):
            s = nt_dot(kv_refs[k][k_at + h * both : k_at + (h + 1) * both, :], q)
            for b in range(CORES):
                parts.append(jnp.where(rows <= limits[j * CORES + b], s[b * tok : (b + 1) * tok, :], LOW))
                at = v_at + h * both + b * tok
                vals.append(kv_refs[v][at : at + tok, :])
        s = jnp.concatenate(parts, axis=0)
        top = jnp.maximum(jnp.max(s, axis=0, keepdims=True), FLOOR).astype(BF16)
        p = jnp.exp2((s - top.astype(F32)) * rate).astype(BF16)
        vt = jnp.concatenate(vals, axis=1)
        vt = jnp.concatenate([vt, jnp.ones((PAD, vt.shape[1]), BF16)], axis=0)
        o = jnp.dot(vt, p, preferred_element_type=F32)
        total = o[size : size + 1, :]
        hi = total.astype(BF16)
        lo = (total - hi.astype(F32)).astype(BF16)
        for b in range(CORES):
            cols = slice(b * tok, (b + 1) * tok)
            store(b, h * size, o[0:size, cols].astype(BF16))
            stats[b] += [top[:, cols].astype(F32), hi[:, cols].astype(F32), lo[:, cols].astype(F32)]
    for b in range(CORES):
        rest = jnp.zeros((PAD - 3 * PER, tok), F32)
        store(b, PER * size, jnp.concatenate(stats[b] + [rest], axis=0).astype(BF16))


def joined(parts, stats, h, rate):
    size = parts[0].shape[0]
    tops = [s[3 * h : 3 * h + 1, :] for s in stats]
    best = functools.reduce(jnp.maximum, tops)
    factors = [jnp.exp2((t - best) * rate) for t in tops]
    total = sum(f * (s[3 * h + 1 : 3 * h + 2, :] + s[3 * h + 2 : 3 * h + 3, :]) for f, s in zip(factors, stats))
    numer = sum(f * part.astype(F32) for f, part in zip(factors, parts))
    return best, total, numer


def add_kernel(n, wide, *refs):
    size = refs[0].shape[1]
    block = PER * size + PAD
    rate = size ** -0.5 * math.log2(math.e)
    for b in range(CORES):
        base = b * block
        stats = [ref[base + PER * size : base + block, :].astype(F32) for ref in refs[:n]]
        out, at = (refs[n], base) if wide else (refs[n + b], 0)
        rows = []
        for h in range(PER):
            parts = [ref[base + h * size : base + (h + 1) * size, :] for ref in refs[:n]]
            best, total, numer = joined(parts, stats, h, rate)
            hi = total.astype(BF16).astype(F32)
            rows += [best, hi, total - hi]
            out[at + h * size : at + (h + 1) * size, :] = numer.astype(BF16)
        rest = jnp.zeros((PAD - 3 * PER, size), F32)
        out[at + PER * size : at + block, :] = jnp.concatenate(rows + [rest], axis=0).astype(BF16)


def combine_kernel(n, *refs):
    parts, out_ref = refs[:n], refs[n]
    size = parts[0].shape[1]
    rate = size ** -0.5 * math.log2(math.e)
    core = lax.rem(lax.axis_index("inner"), CORES)
    for x in range(CORES):
        mine = parts[x::CORES]
        pair = jnp.bitwise_xor(core, x)
        stats = [part[PER * size :, :].astype(F32) for part in mine]
        for h in range(PER):
            _, total, numer = joined([part[h * size : (h + 1) * size, :] for part in mine], stats, h, rate)
            cols = pl.ds(pl.multiple_of((pair * PER + h) * size, size), size)
            out_ref[:, cols] = (numer / total).T.astype(BF16)


def vmem(n=1):
    return [pl.BlockSpec(memory_space=pltpu.VMEM)] * n


def shards(n_out, n_in, queries, keys, values, block_pos):
    tok, width = queries.shape
    size = width // HEADS
    chips = n_in // CORES
    both = CORES * tok
    params = pltpu.CompilerParams(vmem_limit_bytes=40 * 1024 * 1024)

    def along_inner(r, x):
        return [(w * CORES + c, (w ^ r) * CORES + (c ^ x)) for w in range(chips) for c in range(CORES)]

    with jax.named_scope("swap"):
        other = [lax.ppermute(a, "inner", along_inner(0, 1)) for a in (queries, keys, values, block_pos)]
        own = jnp.concatenate([queries, keys, values], axis=0)
    with jax.named_scope("merge"):
        smem = [pl.BlockSpec(memory_space=pltpu.SMEM)]
        q_piece, kv_piece = pl.pallas_call(
            merge_kernel,
            out_shape=(
                jax.ShapeDtypeStruct((PER * both + PAD, size), BF16),
                jax.ShapeDtypeStruct((2 * PER * both + PAD, size), BF16),
            ),
            in_specs=smem * 2 + vmem(4),
            out_specs=tuple(vmem(2)),
            compiler_params=params,
            name="merge",
        )(block_pos, other[3], own, *other[:3])
    half = PER * both + PAD
    block = PER * size + PAD

    def low(r):
        return r & -r

    def single(r):
        return r == low(r)

    def after(a, b):
        return lax.optimization_barrier((a, b))[0]

    with jax.named_scope("exchange"):
        kv = [kv_piece] + [lax.ppermute(kv_piece, "outer", [(o, o ^ r) for o in range(n_out)]) for r in range(1, n_out)]
        q_by = {0: q_piece}
        for r in reversed(range(1, chips)):
            piece = after(q_piece, kv[1]) if r == 1 else q_piece
            q_by[r] = lax.ppermute(piece, "inner", along_inner(r, 0))
    where = tuple((r, 0, r, half) for r in range(n_out))

    def shapes(wide):
        rows = CORES * block if wide else block
        return (jax.ShapeDtypeStruct((rows, tok), BF16),) * (1 if wide else CORES)

    def attend(r, wide, done=None):
        q = q_by[r] if done is None else after(q_by[r], done)
        work = 4 * PER * both * n_out * both * size
        with jax.named_scope("attend"):
            return pl.pallas_call(
                functools.partial(attend_kernel, wide, where),
                out_shape=shapes(wide),
                in_specs=vmem(1 + len(kv)),
                out_specs=tuple(vmem(len(shapes(wide)))),
                compiler_params=params,
                cost_estimate=pl.CostEstimate(flops=work, bytes_accessed=2**20, transcendentals=work // (4 * size)),
                name="attend",
            )(q, *kv)

    def add(arrays, wide):
        with jax.named_scope("add"):
            return pl.pallas_call(
                functools.partial(add_kernel, len(arrays), wide),
                out_shape=shapes(wide),
                in_specs=vmem(len(arrays)),
                out_specs=tuple(vmem(len(shapes(wide)))),
                compiler_params=params,
                name="add",
            )(*arrays)

    arrived = {r: [] for r in range(chips)}
    ends = []

    def send(r, parts):
        with jax.named_scope("return"):
            if single(r):
                ends.extend(lax.ppermute(parts[x], "inner", along_inner(r, x)) for x in range(CORES))
            else:
                arrived[r - low(r)].append(lax.ppermute(parts[0], "inner", along_inner(low(r), 0)))

    done = (q_by[2], q_by[1]) if chips > 2 else None
    partial = {}
    for r in reversed(range(2, chips)):
        partial[r] = attend(r, True, done)
        done = partial[r][0]
    own = attend(0, False, done)
    for r in reversed(range(2, chips)):
        parts = partial[r]
        if arrived[r]:
            parts = add([parts[0], *arrived[r]], not single(r))
        done = parts[0]
        send(r, parts)
    with jax.named_scope("return"):
        piece = own[1] if done is None else after(own[1], done)
        across = lax.ppermute(piece, "inner", along_inner(0, 1))
    if chips > 1:
        send(1, attend(1, False, across))
    ends = [own[0], across] + ends
    with jax.named_scope("combine"):
        return pl.pallas_call(
            functools.partial(combine_kernel, len(ends)),
            out_shape=jax.ShapeDtypeStruct((tok, width), BF16),
            in_specs=vmem(len(ends)),
            out_specs=vmem()[0],
            compiler_params=params,
            name="combine",
        )(*ends)


def solution(mesh):
    n_out, n_in = mesh.shape["outer"], mesh.shape["inner"]
    return jax.shard_map(
        functools.partial(shards, n_out, n_in),
        mesh=mesh,
        in_specs=(
            P(("outer", "inner"), None),
            P(("outer", "inner"), None),
            P(("outer", "inner"), None),
            P(("outer", "inner")),
        ),
        out_specs=P(("outer", "inner"), None),
        check_vma=False,
    )
```

```python
import functools
import math

import jax
import jax.numpy as jnp
from jax import lax
from jax.experimental import pallas as pl
from jax.experimental.pallas import tpu as pltpu
from jax.sharding import PartitionSpec as P

HEADS = 4
CORES = 2
PER = HEADS // CORES
PAD = 16
LOW = -1e30
FLOOR = -1e29
BF16 = jnp.bfloat16
F32 = jnp.float32


def nt_dot(a, b):
    return lax.dot_general(a, b, (((1,), (1,)), ((), ())), preferred_element_type=F32)


def place(own, other, out, at, turned=False):
    tok = own.shape[0]
    size = own.shape[1] // HEADS
    core = lax.rem(lax.axis_index("inner"), CORES)
    for b, ref in enumerate((own, other)):
        for j in range(PER):
            piece = ref[:, pl.ds(pl.multiple_of((core * PER + j) * size, size), size)]
            if turned:
                piece = piece.astype(F32).T.astype(BF16)
            row = at + j * CORES * tok + b * tok
            out[row : row + tok, :] = piece


def starts(p0, p1, size):
    half = PAD // CORES
    return jnp.concatenate([jnp.full((half, size), p[0].astype(F32), F32) for p in (p0, p1)], axis=0).astype(BF16)


def merge_q_kernel(p0, p1, own, q1, out):
    tok = q1.shape[0]
    rows = PER * CORES * tok
    place(own.at[0:tok, :], q1, out, 0)
    out[rows:, :] = starts(p0, p1, out.shape[1])


def merge_kv_kernel(p0, p1, own, k1, v1, out):
    tok = k1.shape[0]
    rows = PER * CORES * tok
    place(own.at[tok : 2 * tok, :], k1, out, 0)
    out[rows : rows + PAD, :] = starts(p0, p1, out.shape[1])
    place(own.at[2 * tok : 3 * tok, :], v1, out, rows + PAD, turned=True)


def attend_kernel(wide, where, q_ref, *refs):
    n = 1 + max(w[2] for w in where)
    kv_refs, out_refs = refs[:n], refs[n:]
    size = q_ref.shape[1]
    tok = size
    both = CORES * tok
    half = PAD // CORES
    block = PER * size + PAD
    rate = size ** -0.5 * math.log2(math.e)
    rows = lax.broadcasted_iota(jnp.int32, (tok, both), 0).astype(F32)
    lanes = lax.broadcasted_iota(jnp.int32, (1, tok), 1).astype(F32)

    def start_of(ref, at):
        first = ref[at : at + PAD, :].astype(F32)
        return [first[b * half : b * half + 1, :] * tok for b in range(CORES)]

    def store(b, at, value):
        if wide:
            out_refs[0][b * block + at : b * block + at + value.shape[0], :] = value
        else:
            out_refs[b][at : at + value.shape[0], :] = value

    qpos = jnp.concatenate([s + lanes for s in start_of(q_ref, PER * both)], axis=1)
    limits = []
    for k, k_at, _, _ in where:
        for s in start_of(kv_refs[k], k_at + PER * both):
            limits.append(qpos - jnp.concatenate([s] * CORES, axis=1))
    stats = [[] for _ in range(CORES)]
    for h in range(PER):
        q = q_ref[h * both : (h + 1) * both, :]
        parts, vals = [], []
        for j, (k, k_at, v, v_at) in enumerate(where):
            s = nt_dot(kv_refs[k][k_at + h * both : k_at + (h + 1) * both, :], q)
            for b in range(CORES):
                parts.append(jnp.where(rows <= limits[j * CORES + b], s[b * tok : (b + 1) * tok, :], LOW))
                at = v_at + h * both + b * tok
                vals.append(kv_refs[v][at : at + tok, :])
        s = jnp.concatenate(parts, axis=0)
        top = jnp.maximum(jnp.max(s, axis=0, keepdims=True), FLOOR).astype(BF16)
        p = jnp.exp2((s - top.astype(F32)) * rate).astype(BF16)
        vt = jnp.concatenate(vals, axis=1)
        vt = jnp.concatenate([vt, jnp.ones((PAD, vt.shape[1]), BF16)], axis=0)
        o = jnp.dot(vt, p, preferred_element_type=F32)
        total = o[size : size + 1, :]
        hi = total.astype(BF16)
        lo = (total - hi.astype(F32)).astype(BF16)
        for b in range(CORES):
            cols = slice(b * tok, (b + 1) * tok)
            store(b, h * size, o[0:size, cols].astype(BF16))
            stats[b] += [top[:, cols].astype(F32), hi[:, cols].astype(F32), lo[:, cols].astype(F32)]
    for b in range(CORES):
        rest = jnp.zeros((PAD - 3 * PER, tok), F32)
        store(b, PER * size, jnp.concatenate(stats[b] + [rest], axis=0).astype(BF16))


def joined(parts, stats, h, rate):
    size = parts[0].shape[0]
    tops = [s[3 * h : 3 * h + 1, :] for s in stats]
    best = functools.reduce(jnp.maximum, tops)
    factors = [jnp.exp2((t - best) * rate) for t in tops]
    total = sum(f * (s[3 * h + 1 : 3 * h + 2, :] + s[3 * h + 2 : 3 * h + 3, :]) for f, s in zip(factors, stats))
    numer = sum(f * part.astype(F32) for f, part in zip(factors, parts))
    return best, total, numer


def add_kernel(n, wide, *refs):
    size = refs[0].shape[1]
    block = PER * size + PAD
    rate = size ** -0.5 * math.log2(math.e)
    for b in range(CORES):
        base = b * block
        stats = [ref[base + PER * size : base + block, :].astype(F32) for ref in refs[:n]]
        out, at = (refs[n], base) if wide else (refs[n + b], 0)
        rows = []
        for h in range(PER):
            parts = [ref[base + h * size : base + (h + 1) * size, :] for ref in refs[:n]]
            best, total, numer = joined(parts, stats, h, rate)
            hi = total.astype(BF16).astype(F32)
            rows += [best, hi, total - hi]
            out[at + h * size : at + (h + 1) * size, :] = numer.astype(BF16)
        rest = jnp.zeros((PAD - 3 * PER, size), F32)
        out[at + PER * size : at + block, :] = jnp.concatenate(rows + [rest], axis=0).astype(BF16)


def combine_kernel(n, *refs):
    parts, out_ref = refs[:n], refs[n]
    size = parts[0].shape[1]
    rate = size ** -0.5 * math.log2(math.e)
    core = lax.rem(lax.axis_index("inner"), CORES)
    for x in range(CORES):
        mine = parts[x::CORES]
        pair = jnp.bitwise_xor(core, x)
        stats = [part[PER * size :, :].astype(F32) for part in mine]
        for h in range(PER):
            _, total, numer = joined([part[h * size : (h + 1) * size, :] for part in mine], stats, h, rate)
            cols = pl.ds(pl.multiple_of((pair * PER + h) * size, size), size)
            out_ref[:, cols] = (numer / total).T.astype(BF16)


def vmem(n=1):
    return [pl.BlockSpec(memory_space=pltpu.VMEM)] * n


def shards(n_out, n_in, queries, keys, values, block_pos):
    tok, width = queries.shape
    size = width // HEADS
    chips = n_in // CORES
    both = CORES * tok
    params = pltpu.CompilerParams(vmem_limit_bytes=40 * 1024 * 1024)

    def along_inner(r, x):
        return [(w * CORES + c, (w ^ r) * CORES + (c ^ x)) for w in range(chips) for c in range(CORES)]

    def after(a, b):
        return lax.optimization_barrier((a, b))[0]

    with jax.named_scope("swap"):
        other = [lax.ppermute(a, "inner", along_inner(0, 1)) for a in (queries, keys, values, block_pos)]
        own = jnp.concatenate([queries, keys, values], axis=0)
    with jax.named_scope("merge"):
        smem = [pl.BlockSpec(memory_space=pltpu.SMEM)]
        q_piece = pl.pallas_call(
            merge_q_kernel,
            out_shape=jax.ShapeDtypeStruct((PER * both + PAD, size), BF16),
            in_specs=smem * 2 + vmem(2),
            out_specs=vmem()[0],
            compiler_params=params,
            name="merge_q",
        )(block_pos, other[3], own, other[0])
        kv_piece = pl.pallas_call(
            merge_kv_kernel,
            out_shape=jax.ShapeDtypeStruct((2 * PER * both + PAD, size), BF16),
            in_specs=smem * 2 + vmem(3),
            out_specs=vmem()[0],
            compiler_params=params,
            name="merge_kv",
        )(block_pos, other[3], own, after(other[1], q_piece), other[2])
    half = PER * both + PAD
    block = PER * size + PAD

    def low(r):
        return r & -r

    def single(r):
        return r == low(r)

    with jax.named_scope("exchange"):
        kv = [kv_piece] + [lax.ppermute(kv_piece, "outer", [(o, o ^ r) for o in range(n_out)]) for r in range(1, n_out)]
        q_by = {0: q_piece}
        bit = chips // 2
        while bit:
            for r in sorted(q_by):
                q_by[r | bit] = lax.ppermute(q_by[r], "inner", along_inner(bit, 0))
            bit //= 2
    where = tuple((r, 0, r, half) for r in range(n_out))

    def shapes(wide):
        rows = CORES * block if wide else block
        return (jax.ShapeDtypeStruct((rows, tok), BF16),) * (1 if wide else CORES)

    def attend(r, wide, done=None):
        q = q_by[r] if done is None else after(q_by[r], done)
        work = 4 * PER * both * n_out * both * size
        with jax.named_scope("attend"):
            return pl.pallas_call(
                functools.partial(attend_kernel, wide, where),
                out_shape=shapes(wide),
                in_specs=vmem(1 + len(kv)),
                out_specs=tuple(vmem(len(shapes(wide)))),
                compiler_params=params,
                cost_estimate=pl.CostEstimate(flops=work, bytes_accessed=2**20, transcendentals=work // (4 * size)),
                name="attend",
            )(q, *kv)

    def add(arrays, wide):
        with jax.named_scope("add"):
            return pl.pallas_call(
                functools.partial(add_kernel, len(arrays), wide),
                out_shape=shapes(wide),
                in_specs=vmem(len(arrays)),
                out_specs=tuple(vmem(len(shapes(wide)))),
                compiler_params=params,
                name="add",
            )(*arrays)

    arrived = {r: [] for r in range(chips)}
    ends = []

    def send(r, parts):
        with jax.named_scope("return"):
            if single(r):
                ends.extend(lax.ppermute(parts[x], "inner", along_inner(r, x)) for x in range(CORES))
            else:
                arrived[r - low(r)].append(lax.ppermute(parts[0], "inner", along_inner(low(r), 0)))

    done = None
    partial = {}
    for r in reversed(range(1, chips)):
        partial[r] = attend(r, r > 1, done)
        done = partial[r][0]
    own = attend(0, False, done)
    for r in reversed(range(1, chips)):
        parts = partial[r]
        if arrived[r]:
            parts = add([parts[0], *arrived[r]], not single(r))
        send(r, parts)
    with jax.named_scope("return"):
        ends = [own[0], lax.ppermute(own[1], "inner", along_inner(0, 1))] + ends
    with jax.named_scope("combine"):
        return pl.pallas_call(
            functools.partial(combine_kernel, len(ends)),
            out_shape=jax.ShapeDtypeStruct((tok, width), BF16),
            in_specs=vmem(len(ends)),
            out_specs=vmem()[0],
            compiler_params=params,
            name="combine",
        )(*ends)


def solution(mesh):
    n_out, n_in = mesh.shape["outer"], mesh.shape["inner"]
    return jax.shard_map(
        functools.partial(shards, n_out, n_in),
        mesh=mesh,
        in_specs=(
            P(("outer", "inner"), None),
            P(("outer", "inner"), None),
            P(("outer", "inner"), None),
            P(("outer", "inner")),
        ),
        out_specs=P(("outer", "inner"), None),
        check_vma=False,
    )
```

```python
import functools
import math

import jax
import jax.numpy as jnp
from jax import lax
from jax.experimental import pallas as pl
from jax.experimental.pallas import tpu as pltpu
from jax.sharding import PartitionSpec as P

HEADS = 4
CORES = 2
PER = HEADS // CORES
PAD = 16
LOW = -1e30
FLOOR = -1e29
BF16 = jnp.bfloat16
F32 = jnp.float32


def nt_dot(a, b):
    return lax.dot_general(a, b, (((1,), (1,)), ((), ())), preferred_element_type=F32)


def place(own, other, out, at, turned=False):
    tok = own.shape[0]
    size = own.shape[1] // HEADS
    core = lax.rem(lax.axis_index("inner"), CORES)
    for b, ref in enumerate((own, other)):
        for j in range(PER):
            piece = ref[:, pl.ds(pl.multiple_of((core * PER + j) * size, size), size)]
            if turned:
                piece = piece.astype(F32).T.astype(BF16)
            row = at + j * CORES * tok + b * tok
            out[row : row + tok, :] = piece


def starts(p0, p1, size):
    half = PAD // CORES
    return jnp.concatenate([jnp.full((half, size), p[0].astype(F32), F32) for p in (p0, p1)], axis=0).astype(BF16)


def merge_q_kernel(p0, p1, own, q1, out):
    tok = q1.shape[0]
    rows = PER * CORES * tok
    place(own.at[0:tok, :], q1, out, 0)
    out[rows:, :] = starts(p0, p1, out.shape[1])


def merge_kv_kernel(p0, p1, own, k1, v1, out):
    tok = k1.shape[0]
    rows = PER * CORES * tok
    place(own.at[tok : 2 * tok, :], k1, out, 0)
    out[rows : rows + PAD, :] = starts(p0, p1, out.shape[1])
    place(own.at[2 * tok : 3 * tok, :], v1, out, rows + PAD, turned=True)


def attend_kernel(wide, same, q_ref, *refs):
    nk = len(refs) - (1 if wide else CORES)
    kv_refs, out_refs = refs[:nk], refs[nk:]
    size = q_ref.shape[1]
    tok = size
    both = CORES * tok
    half = PAD // CORES
    block = PER * size + PAD
    rate = size ** -0.5 * math.log2(math.e)
    at_or_before = lax.broadcasted_iota(jnp.int32, (tok, tok), 0) <= lax.broadcasted_iota(jnp.int32, (tok, tok), 1)

    def block_of(ref, at):
        first = ref[at : at + PAD, :].astype(F32)
        return [first[b * half : b * half + 1, :] for b in range(CORES)]

    def store(b, at, value):
        if wide:
            out_refs[0][b * block + at : b * block + at + value.shape[0], :] = value
        else:
            out_refs[b][at : at + value.shape[0], :] = value

    q_block = jnp.concatenate(block_of(q_ref, PER * both), axis=1)
    kept = [
        jnp.concatenate([p] * CORES, axis=1) <= q_block for ref in kv_refs for p in block_of(ref, PER * both)
    ]
    stats = [[] for _ in range(CORES)]
    for h in range(PER):
        q = q_ref[h * both : (h + 1) * both, :]
        scores, vals = [], []
        for j, ref in enumerate(kv_refs):
            s = nt_dot(ref[h * both : (h + 1) * both, :], q)
            for b in range(CORES):
                part = s[b * tok : (b + 1) * tok, :]
                if same and j == 0:
                    cols = [part[:, c * tok : (c + 1) * tok] for c in range(CORES)]
                    cols[b] = jnp.where(at_or_before, cols[b], LOW)
                    part = jnp.concatenate(cols, axis=1)
                scores.append(part)
                at = PAD + (PER + h) * both + b * tok
                vals.append(ref[at : at + tok, :])
        tops = [jnp.where(k, jnp.max(s, axis=0, keepdims=True), FLOOR) for k, s in zip(kept, scores)]
        top = jnp.maximum(functools.reduce(jnp.maximum, tops), FLOOR).astype(BF16)
        shift = top.astype(F32)
        p = jnp.concatenate(
            [jnp.exp2((s - jnp.where(k, shift, -LOW)) * rate).astype(BF16) for k, s in zip(kept, scores)], axis=0
        )
        vt = jnp.concatenate(vals, axis=1)
        vt = jnp.concatenate([vt, jnp.ones((PAD, vt.shape[1]), BF16)], axis=0)
        o = jnp.dot(vt, p, preferred_element_type=F32)
        total = o[size : size + 1, :]
        hi = total.astype(BF16)
        lo = (total - hi.astype(F32)).astype(BF16)
        for b in range(CORES):
            cols = slice(b * tok, (b + 1) * tok)
            store(b, h * size, o[0:size, cols].astype(BF16))
            stats[b] += [shift[:, cols], hi[:, cols].astype(F32), lo[:, cols].astype(F32)]
    for b in range(CORES):
        rest = jnp.zeros((PAD - 3 * PER, tok), F32)
        store(b, PER * size, jnp.concatenate(stats[b] + [rest], axis=0).astype(BF16))


def joined(parts, stats, h, rate):
    size = parts[0].shape[0]
    tops = [s[3 * h : 3 * h + 1, :] for s in stats]
    best = functools.reduce(jnp.maximum, tops)
    factors = [jnp.exp2((t - best) * rate) for t in tops]
    total = sum(f * (s[3 * h + 1 : 3 * h + 2, :] + s[3 * h + 2 : 3 * h + 3, :]) for f, s in zip(factors, stats))
    numer = sum(f * part.astype(F32) for f, part in zip(factors, parts))
    return best, total, numer


def add_kernel(n, wide, *refs):
    size = refs[0].shape[1]
    block = PER * size + PAD
    rate = size ** -0.5 * math.log2(math.e)
    for b in range(CORES):
        base = b * block
        stats = [ref[base + PER * size : base + block, :].astype(F32) for ref in refs[:n]]
        out, at = (refs[n], base) if wide else (refs[n + b], 0)
        rows = []
        for h in range(PER):
            parts = [ref[base + h * size : base + (h + 1) * size, :] for ref in refs[:n]]
            best, total, numer = joined(parts, stats, h, rate)
            hi = total.astype(BF16).astype(F32)
            rows += [best, hi, total - hi]
            out[at + h * size : at + (h + 1) * size, :] = numer.astype(BF16)
        rest = jnp.zeros((PAD - 3 * PER, size), F32)
        out[at + PER * size : at + block, :] = jnp.concatenate(rows + [rest], axis=0).astype(BF16)


def combine_kernel(n, *refs):
    parts, out_ref = refs[:n], refs[n]
    size = parts[0].shape[1]
    rate = size ** -0.5 * math.log2(math.e)
    core = lax.rem(lax.axis_index("inner"), CORES)
    for x in range(CORES):
        mine = parts[x::CORES]
        pair = jnp.bitwise_xor(core, x)
        stats = [part[PER * size :, :].astype(F32) for part in mine]
        for h in range(PER):
            _, total, numer = joined([part[h * size : (h + 1) * size, :] for part in mine], stats, h, rate)
            cols = pl.ds(pl.multiple_of((pair * PER + h) * size, size), size)
            out_ref[:, cols] = (numer * (1.0 / total)).T.astype(BF16)


def vmem(n=1):
    return [pl.BlockSpec(memory_space=pltpu.VMEM)] * n


def shards(n_out, n_in, queries, keys, values, block_pos):
    tok, width = queries.shape
    size = width // HEADS
    chips = n_in // CORES
    both = CORES * tok
    params = pltpu.CompilerParams(vmem_limit_bytes=40 * 1024 * 1024)

    def along_inner(r, x):
        return [(w * CORES + c, (w ^ r) * CORES + (c ^ x)) for w in range(chips) for c in range(CORES)]

    def after(a, b):
        return lax.optimization_barrier((a, b))[0]

    with jax.named_scope("swap"):
        other = [lax.ppermute(a, "inner", along_inner(0, 1)) for a in (queries, keys, values, block_pos)]
        own = jnp.concatenate([queries, keys, values], axis=0)
    with jax.named_scope("merge"):
        smem = [pl.BlockSpec(memory_space=pltpu.SMEM)]
        q_piece = pl.pallas_call(
            merge_q_kernel,
            out_shape=jax.ShapeDtypeStruct((PER * both + PAD, size), BF16),
            in_specs=smem * 2 + vmem(2),
            out_specs=vmem()[0],
            compiler_params=params,
            name="merge_q",
        )(block_pos, other[3], own, other[0])
        kv_piece = pl.pallas_call(
            merge_kv_kernel,
            out_shape=jax.ShapeDtypeStruct((2 * PER * both + PAD, size), BF16),
            in_specs=smem * 2 + vmem(3),
            out_specs=vmem()[0],
            compiler_params=params,
            name="merge_kv",
        )(block_pos, other[3], own, after(other[1], q_piece), other[2])
    block = PER * size + PAD

    def low(r):
        return r & -r

    def single(r):
        return r == low(r)

    with jax.named_scope("exchange"):
        kv = [kv_piece] + [lax.ppermute(kv_piece, "outer", [(o, o ^ r) for o in range(n_out)]) for r in range(1, n_out)]
        q_by = {0: q_piece}
        bit = chips // 2
        while bit:
            for r in sorted(q_by):
                q_by[r | bit] = lax.ppermute(q_by[r], "inner", along_inner(bit, 0))
            bit //= 2
    def shapes(wide):
        rows = CORES * block if wide else block
        return (jax.ShapeDtypeStruct((rows, tok), BF16),) * (1 if wide else CORES)

    def attend(r, wide, done=None):
        q = q_by[r] if done is None else after(q_by[r], done)
        work = 4 * PER * both * n_out * both * size
        with jax.named_scope("attend"):
            return pl.pallas_call(
                functools.partial(attend_kernel, wide, r == 0),
                out_shape=shapes(wide),
                in_specs=vmem(1 + len(kv)),
                out_specs=tuple(vmem(len(shapes(wide)))),
                compiler_params=params,
                cost_estimate=pl.CostEstimate(flops=work, bytes_accessed=2**20, transcendentals=work // (4 * size)),
                name="attend",
            )(q, *kv)

    def add(arrays, wide):
        with jax.named_scope("add"):
            return pl.pallas_call(
                functools.partial(add_kernel, len(arrays), wide),
                out_shape=shapes(wide),
                in_specs=vmem(len(arrays)),
                out_specs=tuple(vmem(len(shapes(wide)))),
                compiler_params=params,
                name="add",
            )(*arrays)

    arrived = {r: [] for r in range(chips)}
    ends = []

    def send(r, parts):
        with jax.named_scope("return"):
            if single(r):
                ends.extend(lax.ppermute(parts[x], "inner", along_inner(r, x)) for x in range(CORES))
            else:
                arrived[r - low(r)].append(lax.ppermute(parts[0], "inner", along_inner(low(r), 0)))

    done = None
    partial = {}
    for r in reversed(range(1, chips)):
        partial[r] = attend(r, r > 1, done)
        done = partial[r][0]
    own = attend(0, False, done)
    for r in reversed(range(1, chips)):
        parts = partial[r]
        if arrived[r]:
            parts = add([parts[0], *arrived[r]], not single(r))
        send(r, parts)
    with jax.named_scope("return"):
        ends = [own[0], lax.ppermute(own[1], "inner", along_inner(0, 1))] + ends
    with jax.named_scope("combine"):
        return pl.pallas_call(
            functools.partial(combine_kernel, len(ends)),
            out_shape=jax.ShapeDtypeStruct((tok, width), BF16),
            in_specs=vmem(len(ends)),
            out_specs=vmem()[0],
            compiler_params=params,
            name="combine",
        )(*ends)


def solution(mesh):
    n_out, n_in = mesh.shape["outer"], mesh.shape["inner"]
    return jax.shard_map(
        functools.partial(shards, n_out, n_in),
        mesh=mesh,
        in_specs=(
            P(("outer", "inner"), None),
            P(("outer", "inner"), None),
            P(("outer", "inner"), None),
            P(("outer", "inner")),
        ),
        out_specs=P(("outer", "inner"), None),
        check_vma=False,
    )
```

```python
import functools
import math

import jax
import jax.numpy as jnp
from jax import lax
from jax.experimental import pallas as pl
from jax.experimental.pallas import tpu as pltpu
from jax.sharding import PartitionSpec as P

HEADS = 4
CORES = 2
PER = HEADS // CORES
PAD = 16
LOW = -1e30
FLOOR = -1e29
BF16 = jnp.bfloat16
F32 = jnp.float32


def nt_dot(a, b):
    return lax.dot_general(a, b, (((1,), (1,)), ((), ())), preferred_element_type=F32)


def place(own, other, out, at, turned=False):
    tok = own.shape[0]
    size = own.shape[1] // HEADS
    core = lax.rem(lax.axis_index("inner"), CORES)
    for b, ref in enumerate((own, other)):
        for j in range(PER):
            piece = ref[:, pl.ds(pl.multiple_of((core * PER + j) * size, size), size)]
            if turned:
                piece = piece.astype(F32).T.astype(BF16)
            row = at + j * CORES * tok + b * tok
            out[row : row + tok, :] = piece


def starts(p0, p1, size):
    half = PAD // CORES
    return jnp.concatenate([jnp.full((half, size), p[0].astype(F32), F32) for p in (p0, p1)], axis=0).astype(BF16)


def merge_q_kernel(p0, p1, own, q1, out):
    tok = q1.shape[0]
    rows = PER * CORES * tok
    place(own.at[0:tok, :], q1, out, 0)
    out[rows:, :] = starts(p0, p1, out.shape[1])


def merge_kv_kernel(p0, p1, own, k1, v1, k_out, v_out):
    tok = k1.shape[0]
    rows = PER * CORES * tok
    place(own.at[tok : 2 * tok, :], k1, k_out, 0)
    k_out[rows:, :] = starts(p0, p1, k_out.shape[1])
    place(own.at[2 * tok : 3 * tok, :], v1, v_out, 0, turned=True)


def score_kernel(same, q_ref, *refs):
    k_refs, (p_ref, top_ref) = refs[:-2], refs[-2:]
    size = q_ref.shape[1]
    tok = size
    both = CORES * tok
    half = PAD // CORES
    rate = size ** -0.5 * math.log2(math.e)
    at_or_before = lax.broadcasted_iota(jnp.int32, (tok, tok), 0) <= lax.broadcasted_iota(jnp.int32, (tok, tok), 1)

    def block_of(ref):
        first = ref[PER * both :, :].astype(F32)
        return [first[b * half : b * half + 1, :] for b in range(CORES)]

    q_block = jnp.concatenate(block_of(q_ref), axis=1)
    kept = [jnp.concatenate([p] * CORES, axis=1) <= q_block for ref in k_refs for p in block_of(ref)]
    for h in range(PER):
        q = q_ref[h * both : (h + 1) * both, :]
        scores = []
        for j, ref in enumerate(k_refs):
            s = nt_dot(ref[h * both : (h + 1) * both, :], q)
            for b in range(CORES):
                part = s[b * tok : (b + 1) * tok, :]
                if same and j == 0:
                    cols = [part[:, c * tok : (c + 1) * tok] for c in range(CORES)]
                    cols[b] = jnp.where(at_or_before, cols[b], LOW)
                    part = jnp.concatenate(cols, axis=1)
                scores.append(part)
        tops = [jnp.where(k, jnp.max(s, axis=0, keepdims=True), FLOOR) for k, s in zip(kept, scores)]
        top = jnp.maximum(functools.reduce(jnp.maximum, tops), FLOOR).astype(BF16).astype(F32)
        for i, (k, s) in enumerate(zip(kept, scores)):
            p_ref[h, i * tok : (i + 1) * tok, :] = jnp.exp2((s - jnp.where(k, top, -LOW)) * rate).astype(BF16)
        top_ref[h * 8 : (h + 1) * 8, :] = jnp.broadcast_to(top, (8, both))


def apply_kernel(wide, p_ref, top_ref, *refs):
    nv = len(refs) - (1 if wide else CORES)
    v_refs, out_refs = refs[:nv], refs[nv:]
    size = v_refs[0].shape[1]
    tok = size
    both = CORES * tok
    block = PER * size + PAD

    def store(b, at, value):
        if wide:
            out_refs[0][b * block + at : b * block + at + value.shape[0], :] = value
        else:
            out_refs[b][at : at + value.shape[0], :] = value

    stats = [[] for _ in range(CORES)]
    for h in range(PER):
        vals = [ref[h * both + b * tok : h * both + (b + 1) * tok, :] for ref in v_refs for b in range(CORES)]
        vt = jnp.concatenate(vals, axis=1)
        vt = jnp.concatenate([vt, jnp.ones((PAD, vt.shape[1]), BF16)], axis=0)
        o = jnp.dot(vt, p_ref[h], preferred_element_type=F32)
        total = o[size : size + 1, :]
        hi = total.astype(BF16).astype(F32)
        top = top_ref[h * 8 : h * 8 + 1, :]
        for b in range(CORES):
            cols = slice(b * tok, (b + 1) * tok)
            store(b, h * size, o[0:size, cols].astype(BF16))
            stats[b] += [top[:, cols], hi[:, cols], (total - hi)[:, cols]]
    for b in range(CORES):
        rest = jnp.zeros((PAD - 3 * PER, tok), F32)
        store(b, PER * size, jnp.concatenate(stats[b] + [rest], axis=0).astype(BF16))


def joined(parts, stats, h, rate):
    size = parts[0].shape[0]
    tops = [s[3 * h : 3 * h + 1, :] for s in stats]
    best = functools.reduce(jnp.maximum, tops)
    factors = [jnp.exp2((t - best) * rate) for t in tops]
    total = sum(f * (s[3 * h + 1 : 3 * h + 2, :] + s[3 * h + 2 : 3 * h + 3, :]) for f, s in zip(factors, stats))
    numer = sum(f * part.astype(F32) for f, part in zip(factors, parts))
    return best, total, numer


def add_kernel(n, wide, *refs):
    size = refs[0].shape[1]
    block = PER * size + PAD
    rate = size ** -0.5 * math.log2(math.e)
    for b in range(CORES):
        base = b * block
        stats = [ref[base + PER * size : base + block, :].astype(F32) for ref in refs[:n]]
        out, at = (refs[n], base) if wide else (refs[n + b], 0)
        rows = []
        for h in range(PER):
            parts = [ref[base + h * size : base + (h + 1) * size, :] for ref in refs[:n]]
            best, total, numer = joined(parts, stats, h, rate)
            hi = total.astype(BF16).astype(F32)
            rows += [best, hi, total - hi]
            out[at + h * size : at + (h + 1) * size, :] = numer.astype(BF16)
        rest = jnp.zeros((PAD - 3 * PER, size), F32)
        out[at + PER * size : at + block, :] = jnp.concatenate(rows + [rest], axis=0).astype(BF16)


def combine_kernel(n, *refs):
    parts, out_ref = refs[:n], refs[n]
    size = parts[0].shape[1]
    rate = size ** -0.5 * math.log2(math.e)
    core = lax.rem(lax.axis_index("inner"), CORES)
    for x in range(CORES):
        mine = parts[x::CORES]
        pair = jnp.bitwise_xor(core, x)
        stats = [part[PER * size :, :].astype(F32) for part in mine]
        for h in range(PER):
            _, total, numer = joined([part[h * size : (h + 1) * size, :] for part in mine], stats, h, rate)
            cols = pl.ds(pl.multiple_of((pair * PER + h) * size, size), size)
            out_ref[:, cols] = (numer * (1.0 / total)).T.astype(BF16)


def vmem(n=1):
    return [pl.BlockSpec(memory_space=pltpu.VMEM)] * n


def shards(n_out, n_in, queries, keys, values, block_pos):
    tok, width = queries.shape
    size = width // HEADS
    chips = n_in // CORES
    both = CORES * tok
    params = pltpu.CompilerParams(vmem_limit_bytes=40 * 1024 * 1024)

    def along_inner(r, x):
        return [(w * CORES + c, (w ^ r) * CORES + (c ^ x)) for w in range(chips) for c in range(CORES)]

    def after(a, b):
        return lax.optimization_barrier((a, b))[0]

    with jax.named_scope("swap"):
        other = [lax.ppermute(a, "inner", along_inner(0, 1)) for a in (queries, keys, values, block_pos)]
        own = jnp.concatenate([queries, keys, values], axis=0)
    with jax.named_scope("merge"):
        smem = [pl.BlockSpec(memory_space=pltpu.SMEM)]
        q_piece = pl.pallas_call(
            merge_q_kernel,
            out_shape=jax.ShapeDtypeStruct((PER * both + PAD, size), BF16),
            in_specs=smem * 2 + vmem(2),
            out_specs=vmem()[0],
            compiler_params=params,
            name="merge_q",
        )(block_pos, other[3], own, other[0])
        k_piece, v_piece = pl.pallas_call(
            merge_kv_kernel,
            out_shape=(
                jax.ShapeDtypeStruct((PER * both + PAD, size), BF16),
                jax.ShapeDtypeStruct((PER * both, size), BF16),
            ),
            in_specs=smem * 2 + vmem(3),
            out_specs=tuple(vmem(2)),
            compiler_params=params,
            name="merge_kv",
        )(block_pos, other[3], own, after(other[1], q_piece), other[2])
    block = PER * size + PAD

    def low(r):
        return r & -r

    def high(r):
        return 1 << (r.bit_length() - 1)

    def single(r):
        return r == low(r)

    def over(a, r):
        return lax.ppermute(a, "outer", [(o, o ^ r) for o in range(n_out)])

    with jax.named_scope("exchange"):
        k_by, v_by = {0: k_piece}, {0: v_piece}
        for r in range(1, n_out):
            k_by[r] = over(k_by[r - high(r)], high(r))
        for r in sorted(range(1, n_out), key=lambda r: r.bit_count()):
            v_by[r] = over(v_by[r - low(r)], low(r))
        ks, vs = [k_by[r] for r in range(n_out)], [v_by[r] for r in range(n_out)]
        q_by = {0: q_piece}
        bit = chips // 2
        while bit:
            for r in sorted(q_by):
                q_by[r | bit] = lax.ppermute(q_by[r], "inner", along_inner(bit, 0))
            bit //= 2
    def shapes(wide):
        rows = CORES * block if wide else block
        return (jax.ShapeDtypeStruct((rows, tok), BF16),) * (1 if wide else CORES)

    work = 2 * PER * both * n_out * both * size

    def score(r, done):
        with jax.named_scope("score"):
            return pl.pallas_call(
                functools.partial(score_kernel, r == 0),
                out_shape=(
                    jax.ShapeDtypeStruct((PER, n_out * both, both), BF16),
                    jax.ShapeDtypeStruct((PER * 8, both), F32),
                ),
                in_specs=vmem(1 + n_out),
                out_specs=tuple(vmem(2)),
                compiler_params=params,
                cost_estimate=pl.CostEstimate(flops=work, bytes_accessed=2**20, transcendentals=work // (2 * size)),
                name="score",
            )(after(q_by[r], done), *ks)

    def apply(r, wide, done):
        with jax.named_scope("apply"):
            weights, tops = weights_by[r]
            return pl.pallas_call(
                functools.partial(apply_kernel, wide),
                out_shape=shapes(wide),
                in_specs=vmem(2 + n_out),
                out_specs=tuple(vmem(len(shapes(wide)))),
                compiler_params=params,
                cost_estimate=pl.CostEstimate(flops=work, bytes_accessed=2**20, transcendentals=0),
                name="apply",
            )(weights, tops if done is None else after(tops, done), *vs)

    def add(arrays, wide):
        with jax.named_scope("add"):
            return pl.pallas_call(
                functools.partial(add_kernel, len(arrays), wide),
                out_shape=shapes(wide),
                in_specs=vmem(len(arrays)),
                out_specs=tuple(vmem(len(shapes(wide)))),
                compiler_params=params,
                name="add",
            )(*arrays)

    arrived = {r: [] for r in range(chips)}
    ends = []

    def send(r, parts):
        with jax.named_scope("return"):
            if single(r):
                ends.extend(lax.ppermute(parts[x], "inner", along_inner(r, x)) for x in range(CORES))
            else:
                arrived[r - low(r)].append(lax.ppermute(parts[0], "inner", along_inner(low(r), 0)))

    weights_by = {}
    done = [v_by[r] for r in range(1, n_out) if single(r)]
    for r in range(chips):
        weights_by[r] = score(r, done)
        done = weights_by[r][1]
    done = None
    partial = {}
    for r in reversed(range(1, chips)):
        partial[r] = apply(r, r > 1, done)
        done = partial[r][0]
    own = apply(0, False, done)
    for r in reversed(range(1, chips)):
        parts = partial[r]
        if arrived[r]:
            parts = add([parts[0], *arrived[r]], not single(r))
        send(r, parts)
    with jax.named_scope("return"):
        ends = [own[0], lax.ppermute(own[1], "inner", along_inner(0, 1))] + ends
    with jax.named_scope("combine"):
        return pl.pallas_call(
            functools.partial(combine_kernel, len(ends)),
            out_shape=jax.ShapeDtypeStruct((tok, width), BF16),
            in_specs=vmem(len(ends)),
            out_specs=vmem()[0],
            compiler_params=params,
            name="combine",
        )(*ends)


def solution(mesh):
    n_out, n_in = mesh.shape["outer"], mesh.shape["inner"]
    return jax.shard_map(
        functools.partial(shards, n_out, n_in),
        mesh=mesh,
        in_specs=(
            P(("outer", "inner"), None),
            P(("outer", "inner"), None),
            P(("outer", "inner"), None),
            P(("outer", "inner")),
        ),
        out_specs=P(("outer", "inner"), None),
        check_vma=False,
    )
```

```python
import functools
import math

import jax
import jax.numpy as jnp
from jax import lax
from jax.experimental import pallas as pl
from jax.experimental.pallas import tpu as pltpu
from jax.sharding import PartitionSpec as P

HEADS = 4
CORES = 2
PER = HEADS // CORES
PAD = 16
LOW = -1e30
FLOOR = -1e29
BF16 = jnp.bfloat16
F32 = jnp.float32


def nt_dot(a, b):
    return lax.dot_general(a, b, (((1,), (1,)), ((), ())), preferred_element_type=F32)


def place(own, other, out, at, turned=False):
    tok = own.shape[0]
    size = own.shape[1] // HEADS
    core = lax.rem(lax.axis_index("inner"), CORES)
    for b, ref in enumerate((own, other)):
        for j in range(PER):
            piece = ref[:, pl.ds(pl.multiple_of((core * PER + j) * size, size), size)]
            if turned:
                piece = piece.astype(F32).T.astype(BF16)
            row = at + j * CORES * tok + b * tok
            out[row : row + tok, :] = piece


def starts(p0, p1, size):
    half = PAD // CORES
    return jnp.concatenate([jnp.full((half, size), p[0].astype(F32), F32) for p in (p0, p1)], axis=0).astype(BF16)


def merge_kernel(p0, p1, own, q1, k1, v1, q_out, k_out, v_out):
    tok = q1.shape[0]
    rows = PER * CORES * tok
    pos = starts(p0, p1, q_out.shape[1])
    place(own.at[0:tok, :], q1, q_out, 0)
    q_out[rows:, :] = pos
    place(own.at[tok : 2 * tok, :], k1, k_out, 0)
    k_out[rows:, :] = pos
    place(own.at[2 * tok : 3 * tok, :], v1, v_out, 0, turned=True)


def score_kernel(same, q_ref, *refs):
    k_refs, (p_ref, top_ref) = refs[:-2], refs[-2:]
    size = q_ref.shape[1]
    tok = size
    both = CORES * tok
    half = PAD // CORES
    rate = size ** -0.5 * math.log2(math.e)
    at_or_before = lax.broadcasted_iota(jnp.int32, (tok, tok), 0) <= lax.broadcasted_iota(jnp.int32, (tok, tok), 1)

    def block_of(ref):
        first = ref[PER * both :, :].astype(F32)
        return [first[b * half : b * half + 1, :] for b in range(CORES)]

    q_block = jnp.concatenate(block_of(q_ref), axis=1)
    kept = [jnp.concatenate([p] * CORES, axis=1) <= q_block for ref in k_refs for p in block_of(ref)]
    for h in range(PER):
        q = q_ref[h * both : (h + 1) * both, :]
        scores = []
        for j, ref in enumerate(k_refs):
            s = nt_dot(ref[h * both : (h + 1) * both, :], q)
            for b in range(CORES):
                part = s[b * tok : (b + 1) * tok, :]
                if same and j == 0:
                    cols = [part[:, c * tok : (c + 1) * tok] for c in range(CORES)]
                    cols[b] = jnp.where(at_or_before, cols[b], LOW)
                    part = jnp.concatenate(cols, axis=1)
                scores.append(part)
        tops = [jnp.where(k, jnp.max(s, axis=0, keepdims=True), FLOOR) for k, s in zip(kept, scores)]
        top = jnp.maximum(functools.reduce(jnp.maximum, tops), FLOOR).astype(BF16).astype(F32)
        for i, (k, s) in enumerate(zip(kept, scores)):
            p_ref[h, i * tok : (i + 1) * tok, :] = jnp.exp2((s - jnp.where(k, top, -LOW)) * rate).astype(BF16)
        top_ref[h * 8 : (h + 1) * 8, :] = jnp.broadcast_to(top, (8, both))


def apply_kernel(wide, p_ref, top_ref, *refs):
    nv = len(refs) - (1 if wide else CORES)
    v_refs, out_refs = refs[:nv], refs[nv:]
    size = v_refs[0].shape[1]
    tok = size
    both = CORES * tok
    block = PER * size + PAD

    def store(b, at, value):
        if wide:
            out_refs[0][b * block + at : b * block + at + value.shape[0], :] = value
        else:
            out_refs[b][at : at + value.shape[0], :] = value

    stats = [[] for _ in range(CORES)]
    for h in range(PER):
        vals = [ref[h * both + b * tok : h * both + (b + 1) * tok, :] for ref in v_refs for b in range(CORES)]
        vt = jnp.concatenate(vals, axis=1)
        vt = jnp.concatenate([vt, jnp.ones((PAD, vt.shape[1]), BF16)], axis=0)
        o = jnp.dot(vt, p_ref[h], preferred_element_type=F32)
        total = o[size : size + 1, :]
        hi = total.astype(BF16).astype(F32)
        top = top_ref[h * 8 : h * 8 + 1, :]
        for b in range(CORES):
            cols = slice(b * tok, (b + 1) * tok)
            store(b, h * size, o[0:size, cols].astype(BF16))
            stats[b] += [top[:, cols], hi[:, cols], (total - hi)[:, cols]]
    for b in range(CORES):
        rest = jnp.zeros((PAD - 3 * PER, tok), F32)
        store(b, PER * size, jnp.concatenate(stats[b] + [rest], axis=0).astype(BF16))


def joined(parts, stats, h, rate):
    size = parts[0].shape[0]
    tops = [s[3 * h : 3 * h + 1, :] for s in stats]
    best = functools.reduce(jnp.maximum, tops)
    factors = [jnp.exp2((t - best) * rate) for t in tops]
    total = sum(f * (s[3 * h + 1 : 3 * h + 2, :] + s[3 * h + 2 : 3 * h + 3, :]) for f, s in zip(factors, stats))
    numer = sum(f * part.astype(F32) for f, part in zip(factors, parts))
    return best, total, numer


def add_kernel(n, wide, *refs):
    size = refs[0].shape[1]
    block = PER * size + PAD
    rate = size ** -0.5 * math.log2(math.e)
    for b in range(CORES):
        base = b * block
        stats = [ref[base + PER * size : base + block, :].astype(F32) for ref in refs[:n]]
        out, at = (refs[n], base) if wide else (refs[n + b], 0)
        rows = []
        for h in range(PER):
            parts = [ref[base + h * size : base + (h + 1) * size, :] for ref in refs[:n]]
            best, total, numer = joined(parts, stats, h, rate)
            hi = total.astype(BF16).astype(F32)
            rows += [best, hi, total - hi]
            out[at + h * size : at + (h + 1) * size, :] = numer.astype(BF16)
        rest = jnp.zeros((PAD - 3 * PER, size), F32)
        out[at + PER * size : at + block, :] = jnp.concatenate(rows + [rest], axis=0).astype(BF16)


def combine_kernel(n, *refs):
    parts, out_ref = refs[:n], refs[n]
    size = parts[0].shape[1]
    rate = size ** -0.5 * math.log2(math.e)
    core = lax.rem(lax.axis_index("inner"), CORES)
    for x in range(CORES):
        mine = parts[x::CORES]
        pair = jnp.bitwise_xor(core, x)
        stats = [part[PER * size :, :].astype(F32) for part in mine]
        for h in range(PER):
            _, total, numer = joined([part[h * size : (h + 1) * size, :] for part in mine], stats, h, rate)
            cols = pl.ds(pl.multiple_of((pair * PER + h) * size, size), size)
            out_ref[:, cols] = (numer * (1.0 / total)).T.astype(BF16)


def vmem(n=1):
    return [pl.BlockSpec(memory_space=pltpu.VMEM)] * n


def shards(n_out, n_in, queries, keys, values, block_pos):
    tok, width = queries.shape
    size = width // HEADS
    chips = n_in // CORES
    both = CORES * tok
    params = pltpu.CompilerParams(vmem_limit_bytes=40 * 1024 * 1024)

    def along_inner(r, x):
        return [(w * CORES + c, (w ^ r) * CORES + (c ^ x)) for w in range(chips) for c in range(CORES)]

    def after(a, b):
        return lax.optimization_barrier((a, b))[0]

    with jax.named_scope("swap"):
        other = [lax.ppermute(a, "inner", along_inner(0, 1)) for a in (queries, keys, values, block_pos)]
        own = jnp.concatenate([queries, keys, values], axis=0)
    with jax.named_scope("merge"):
        smem = [pl.BlockSpec(memory_space=pltpu.SMEM)]
        piece = jax.ShapeDtypeStruct((PER * both + PAD, size), BF16)
        q_piece, k_piece, v_piece = pl.pallas_call(
            merge_kernel,
            out_shape=(piece, piece, jax.ShapeDtypeStruct((PER * both, size), BF16)),
            in_specs=smem * 2 + vmem(4),
            out_specs=tuple(vmem(3)),
            compiler_params=params,
            name="merge",
        )(block_pos, other[3], own, *other[:3])
    block = PER * size + PAD

    def low(r):
        return r & -r

    def high(r):
        return 1 << (r.bit_length() - 1)

    def single(r):
        return r == low(r)

    def over(a, r):
        return lax.ppermute(a, "outer", [(o, o ^ r) for o in range(n_out)])

    with jax.named_scope("exchange"):
        k_by, v_by = {0: k_piece}, {0: v_piece}
        for r in range(1, n_out):
            k_by[r] = over(k_by[r - high(r)], high(r))
        for r in sorted(range(1, n_out), key=lambda r: r.bit_count()):
            v_by[r] = over(v_by[r - low(r)], low(r))
        ks, vs = [k_by[r] for r in range(n_out)], [v_by[r] for r in range(n_out)]
        passed = v_by[n_out // 2] if n_out > 1 else v_piece
        q_by = {0: q_piece}
        bit = chips // 2
        while bit:
            for r in sorted(q_by):
                piece = q_by[r] if bit == chips // 2 else after(q_by[r], passed)
                q_by[r | bit] = lax.ppermute(piece, "inner", along_inner(bit, 0))
            bit //= 2

    def shapes(wide):
        rows = CORES * block if wide else block
        return (jax.ShapeDtypeStruct((rows, tok), BF16),) * (1 if wide else CORES)

    work = 2 * PER * both * n_out * both * size

    def score(r, done):
        with jax.named_scope("score"):
            return pl.pallas_call(
                functools.partial(score_kernel, r == 0),
                out_shape=(
                    jax.ShapeDtypeStruct((PER, n_out * both, both), BF16),
                    jax.ShapeDtypeStruct((PER * 8, both), F32),
                ),
                in_specs=vmem(1 + n_out),
                out_specs=tuple(vmem(2)),
                compiler_params=params,
                cost_estimate=pl.CostEstimate(flops=work, bytes_accessed=2**20, transcendentals=work // (2 * size)),
                name="score",
            )(after(q_by[r], done), *ks)

    def apply(r, wide, done):
        with jax.named_scope("apply"):
            weights, tops = weights_by[r]
            return pl.pallas_call(
                functools.partial(apply_kernel, wide),
                out_shape=shapes(wide),
                in_specs=vmem(2 + n_out),
                out_specs=tuple(vmem(len(shapes(wide)))),
                compiler_params=params,
                cost_estimate=pl.CostEstimate(flops=work, bytes_accessed=2**20, transcendentals=0),
                name="apply",
            )(weights, tops if done is None else after(tops, done), *vs)

    def add(arrays, wide):
        with jax.named_scope("add"):
            return pl.pallas_call(
                functools.partial(add_kernel, len(arrays), wide),
                out_shape=shapes(wide),
                in_specs=vmem(len(arrays)),
                out_specs=tuple(vmem(len(shapes(wide)))),
                compiler_params=params,
                name="add",
            )(*arrays)

    arrived = {r: [] for r in range(chips)}
    ends = []

    def send(r, parts):
        with jax.named_scope("return"):
            if single(r):
                ends.extend(lax.ppermute(parts[x], "inner", along_inner(r, x)) for x in range(CORES))
            else:
                arrived[r - low(r)].append(lax.ppermute(parts[0], "inner", along_inner(low(r), 0)))

    weights_by = {}
    done = passed
    for r in range(chips):
        weights_by[r] = score(r, done)
        done = weights_by[r][1]
    done = None
    partial = {}
    for r in reversed(range(chips)):
        partial[r] = apply(r, r > 1, done)
        done = partial[r][0]
    for r in reversed(range(2, chips)):
        parts = partial[r]
        if arrived[r]:
            parts = add([parts[0], *arrived[r]], not single(r))
            done = parts[0]
        send(r, parts)
    with jax.named_scope("return"):
        across = lax.ppermute(after(partial[0][1], done), "inner", along_inner(0, 1))
    if chips > 1:
        send(1, [after(part, across) for part in partial[1]])
    ends = [partial[0][0], across] + ends
    with jax.named_scope("combine"):
        return pl.pallas_call(
            functools.partial(combine_kernel, len(ends)),
            out_shape=jax.ShapeDtypeStruct((tok, width), BF16),
            in_specs=vmem(len(ends)),
            out_specs=vmem()[0],
            compiler_params=params,
            name="combine",
        )(*ends)


def solution(mesh):
    n_out, n_in = mesh.shape["outer"], mesh.shape["inner"]
    return jax.shard_map(
        functools.partial(shards, n_out, n_in),
        mesh=mesh,
        in_specs=(
            P(("outer", "inner"), None),
            P(("outer", "inner"), None),
            P(("outer", "inner"), None),
            P(("outer", "inner")),
        ),
        out_specs=P(("outer", "inner"), None),
        check_vma=False,
    )
```

```python
import functools
import math

import jax
import jax.numpy as jnp
from jax import lax
from jax.experimental import pallas as pl
from jax.experimental.pallas import tpu as pltpu
from jax.sharding import PartitionSpec as P

HEADS = 4
CORES = 2
PER = HEADS // CORES
PAD = 16
LOW = -1e30
FLOOR = -1e29
BF16 = jnp.bfloat16
F32 = jnp.float32


def nt_dot(a, b):
    return lax.dot_general(a, b, (((1,), (1,)), ((), ())), preferred_element_type=F32)


def place(own, other, out, at, turned=False):
    tok = own.shape[0]
    size = own.shape[1] // HEADS
    core = lax.rem(lax.axis_index("inner"), CORES)
    for b, ref in enumerate((own, other)):
        for j in range(PER):
            piece = ref[:, pl.ds(pl.multiple_of((core * PER + j) * size, size), size)]
            if turned:
                piece = piece.astype(F32).T.astype(BF16)
            row = at + j * CORES * tok + b * tok
            out[row : row + tok, :] = piece


def starts(p0, p1, size):
    half = PAD // CORES
    return jnp.concatenate([jnp.full((half, size), p[0].astype(F32), F32) for p in (p0, p1)], axis=0).astype(BF16)


def merge_kernel(p0, p1, own, q1, k1, v1, q_out, k_out, v_out):
    tok = q1.shape[0]
    rows = PER * CORES * tok
    pos = starts(p0, p1, q_out.shape[1])
    place(own.at[0:tok, :], q1, q_out, 0)
    q_out[rows:, :] = pos
    place(own.at[tok : 2 * tok, :], k1, k_out, 0)
    k_out[rows:, :] = pos
    place(own.at[2 * tok : 3 * tok, :], v1, v_out, 0, turned=True)


def score_kernel(same, q_ref, *refs):
    k_refs, (p_ref, top_ref) = refs[:-2], refs[-2:]
    size = q_ref.shape[1]
    tok = size
    both = CORES * tok
    half = PAD // CORES
    rate = size ** -0.5 * math.log2(math.e)
    at_or_before = lax.broadcasted_iota(jnp.int32, (tok, tok), 0) <= lax.broadcasted_iota(jnp.int32, (tok, tok), 1)

    def block_of(ref):
        first = ref[PER * both :, :].astype(F32)
        return [first[b * half : b * half + 1, :] for b in range(CORES)]

    q_block = jnp.concatenate(block_of(q_ref), axis=1)
    kept = [jnp.concatenate([p] * CORES, axis=1) <= q_block for ref in k_refs for p in block_of(ref)]
    for h in range(PER):
        q = q_ref[h * both : (h + 1) * both, :]
        scores = []
        for j, ref in enumerate(k_refs):
            s = nt_dot(ref[h * both : (h + 1) * both, :], q)
            for b in range(CORES):
                part = s[b * tok : (b + 1) * tok, :]
                if same and j == 0:
                    cols = [part[:, c * tok : (c + 1) * tok] for c in range(CORES)]
                    cols[b] = jnp.where(at_or_before, cols[b], LOW)
                    part = jnp.concatenate(cols, axis=1)
                scores.append(part)
        tops = [jnp.where(k, jnp.max(s, axis=0, keepdims=True), FLOOR) for k, s in zip(kept, scores)]
        top = jnp.maximum(functools.reduce(jnp.maximum, tops), FLOOR).astype(BF16).astype(F32)
        for i, (k, s) in enumerate(zip(kept, scores)):
            p_ref[h, i * tok : (i + 1) * tok, :] = jnp.exp2((s - jnp.where(k, top, -LOW)) * rate).astype(BF16)
        top_ref[h * 8 : (h + 1) * 8, :] = jnp.broadcast_to(top, (8, both))


def apply_kernel(wide, p_ref, top_ref, *refs):
    nv = len(refs) - (1 if wide else CORES)
    v_refs, out_refs = refs[:nv], refs[nv:]
    size = v_refs[0].shape[1]
    tok = size
    both = CORES * tok
    block = PER * size + PAD

    def store(b, at, value):
        if wide:
            out_refs[0][b * block + at : b * block + at + value.shape[0], :] = value
        else:
            out_refs[b][at : at + value.shape[0], :] = value

    stats = [[] for _ in range(CORES)]
    for h in range(PER):
        vals = [ref[h * both + b * tok : h * both + (b + 1) * tok, :] for ref in v_refs for b in range(CORES)]
        vt = jnp.concatenate(vals, axis=1)
        vt = jnp.concatenate([vt, jnp.ones((PAD, vt.shape[1]), BF16)], axis=0)
        o = jnp.dot(vt, p_ref[h], preferred_element_type=F32)
        total = o[size : size + 1, :]
        hi = total.astype(BF16).astype(F32)
        top = top_ref[h * 8 : h * 8 + 1, :]
        for b in range(CORES):
            cols = slice(b * tok, (b + 1) * tok)
            store(b, h * size, o[0:size, cols].astype(BF16))
            stats[b] += [top[:, cols], hi[:, cols], (total - hi)[:, cols]]
    for b in range(CORES):
        rest = jnp.zeros((PAD - 3 * PER, tok), F32)
        store(b, PER * size, jnp.concatenate(stats[b] + [rest], axis=0).astype(BF16))


def joined(parts, stats, h, rate):
    size = parts[0].shape[0]
    tops = [s[3 * h : 3 * h + 1, :] for s in stats]
    best = functools.reduce(jnp.maximum, tops)
    factors = [jnp.exp2((t - best) * rate) for t in tops]
    total = sum(f * (s[3 * h + 1 : 3 * h + 2, :] + s[3 * h + 2 : 3 * h + 3, :]) for f, s in zip(factors, stats))
    numer = sum(f * part.astype(F32) for f, part in zip(factors, parts))
    return best, total, numer


def add_kernel(n, wide, *refs):
    size = refs[0].shape[1]
    block = PER * size + PAD
    rate = size ** -0.5 * math.log2(math.e)
    for b in range(CORES):
        base = b * block
        stats = [ref[base + PER * size : base + block, :].astype(F32) for ref in refs[:n]]
        out, at = (refs[n], base) if wide else (refs[n + b], 0)
        rows = []
        for h in range(PER):
            parts = [ref[base + h * size : base + (h + 1) * size, :] for ref in refs[:n]]
            best, total, numer = joined(parts, stats, h, rate)
            hi = total.astype(BF16).astype(F32)
            rows += [best, hi, total - hi]
            out[at + h * size : at + (h + 1) * size, :] = numer.astype(BF16)
        rest = jnp.zeros((PAD - 3 * PER, size), F32)
        out[at + PER * size : at + block, :] = jnp.concatenate(rows + [rest], axis=0).astype(BF16)


def combine_kernel(n, *refs):
    parts, out_ref = refs[:n], refs[n]
    size = parts[0].shape[1]
    rate = size ** -0.5 * math.log2(math.e)
    core = lax.rem(lax.axis_index("inner"), CORES)
    for x in range(CORES):
        mine = parts[x::CORES]
        pair = jnp.bitwise_xor(core, x)
        stats = [part[PER * size :, :].astype(F32) for part in mine]
        for h in range(PER):
            _, total, numer = joined([part[h * size : (h + 1) * size, :] for part in mine], stats, h, rate)
            cols = pl.ds(pl.multiple_of((pair * PER + h) * size, size), size)
            out_ref[:, cols] = (numer * (1.0 / total)).T.astype(BF16)


def vmem(n=1):
    return [pl.BlockSpec(memory_space=pltpu.VMEM)] * n


def shards(n_out, n_in, queries, keys, values, block_pos):
    tok, width = queries.shape
    size = width // HEADS
    chips = n_in // CORES
    both = CORES * tok
    params = pltpu.CompilerParams(vmem_limit_bytes=40 * 1024 * 1024)

    def along_inner(r, x):
        return [(w * CORES + c, (w ^ r) * CORES + (c ^ x)) for w in range(chips) for c in range(CORES)]

    def after(a, b):
        return lax.optimization_barrier((a, b))[0]

    with jax.named_scope("swap"):
        other = [lax.ppermute(a, "inner", along_inner(0, 1)) for a in (queries, keys, values, block_pos)]
        own = jnp.concatenate([queries, keys, values], axis=0)
    with jax.named_scope("merge"):
        smem = [pl.BlockSpec(memory_space=pltpu.SMEM)]
        piece = jax.ShapeDtypeStruct((PER * both + PAD, size), BF16)
        q_piece, k_piece, v_piece = pl.pallas_call(
            merge_kernel,
            out_shape=(piece, piece, jax.ShapeDtypeStruct((PER * both, size), BF16)),
            in_specs=smem * 2 + vmem(4),
            out_specs=tuple(vmem(3)),
            compiler_params=params,
            name="merge",
        )(block_pos, other[3], own, *other[:3])
    block = PER * size + PAD

    def low(r):
        return r & -r

    def high(r):
        return 1 << (r.bit_length() - 1)

    def single(r):
        return r == low(r)

    def over(a, r):
        return lax.ppermute(a, "outer", [(o, o ^ r) for o in range(n_out)])

    with jax.named_scope("exchange"):
        k_by, v_by = {0: k_piece}, {0: v_piece}
        for r in range(1, n_out):
            k_by[r] = over(k_by[r - high(r)], high(r))
        for r in sorted(range(1, n_out), key=lambda r: r.bit_count()):
            v_by[r] = over(v_by[r - low(r)], low(r))
        ks, vs = [k_by[r] for r in range(n_out)], [v_by[r] for r in range(n_out)]
        passed = v_by[n_out // 2] if n_out > 1 else v_piece
        q_by = {0: q_piece}
        bit = chips // 2
        while bit:
            for r in sorted(q_by):
                piece = q_by[r]
                if r:
                    piece = after(piece, passed)
                elif bit == 1:
                    piece = after(piece, k_by[n_out - 1])
                q_by[r | bit] = lax.ppermute(piece, "inner", along_inner(bit, 0))
            bit //= 2

    def shapes(wide):
        rows = CORES * block if wide else block
        return (jax.ShapeDtypeStruct((rows, tok), BF16),) * (1 if wide else CORES)

    work = 2 * PER * both * n_out * both * size

    def score(r, done):
        with jax.named_scope("score"):
            return pl.pallas_call(
                functools.partial(score_kernel, r == 0),
                out_shape=(
                    jax.ShapeDtypeStruct((PER, n_out * both, both), BF16),
                    jax.ShapeDtypeStruct((PER * 8, both), F32),
                ),
                in_specs=vmem(1 + n_out),
                out_specs=tuple(vmem(2)),
                compiler_params=params,
                cost_estimate=pl.CostEstimate(flops=work, bytes_accessed=2**20, transcendentals=work // (2 * size)),
                name="score",
            )(after(q_by[r], done), *ks)

    def apply(r, wide, done):
        with jax.named_scope("apply"):
            weights, tops = weights_by[r]
            return pl.pallas_call(
                functools.partial(apply_kernel, wide),
                out_shape=shapes(wide),
                in_specs=vmem(2 + n_out),
                out_specs=tuple(vmem(len(shapes(wide)))),
                compiler_params=params,
                cost_estimate=pl.CostEstimate(flops=work, bytes_accessed=2**20, transcendentals=0),
                name="apply",
            )(weights, tops if done is None else after(tops, done), *vs)

    def add(arrays, wide):
        with jax.named_scope("add"):
            return pl.pallas_call(
                functools.partial(add_kernel, len(arrays), wide),
                out_shape=shapes(wide),
                in_specs=vmem(len(arrays)),
                out_specs=tuple(vmem(len(shapes(wide)))),
                compiler_params=params,
                name="add",
            )(*arrays)

    arrived = {r: [] for r in range(chips)}
    ends = []

    def send(r, parts):
        with jax.named_scope("return"):
            if single(r):
                ends.extend(lax.ppermute(parts[x], "inner", along_inner(r, x)) for x in range(CORES))
            else:
                arrived[r - low(r)].append(lax.ppermute(parts[0], "inner", along_inner(low(r), 0)))

    weights_by = {}
    done = [v_by[r] for r in range(1, n_out) if single(r)]
    for r in sorted(range(chips), key=lambda r: (r == 1, r)):
        weights_by[r] = score(r, done)
        done = weights_by[r][1]
    done = None
    partial = {}
    for r in reversed(range(chips)):
        partial[r] = apply(r, r > 1, done)
        done = partial[r][0]
    for r in reversed(range(1, chips)):
        parts = partial[r]
        if arrived[r]:
            parts = add([parts[0], *arrived[r]], not single(r))
        send(r, parts)
    with jax.named_scope("return"):
        ends = [partial[0][0], lax.ppermute(partial[0][1], "inner", along_inner(0, 1))] + ends
    with jax.named_scope("combine"):
        return pl.pallas_call(
            functools.partial(combine_kernel, len(ends)),
            out_shape=jax.ShapeDtypeStruct((tok, width), BF16),
            in_specs=vmem(len(ends)),
            out_specs=vmem()[0],
            compiler_params=params,
            name="combine",
        )(*ends)


def solution(mesh):
    n_out, n_in = mesh.shape["outer"], mesh.shape["inner"]
    return jax.shard_map(
        functools.partial(shards, n_out, n_in),
        mesh=mesh,
        in_specs=(
            P(("outer", "inner"), None),
            P(("outer", "inner"), None),
            P(("outer", "inner"), None),
            P(("outer", "inner")),
        ),
        out_specs=P(("outer", "inner"), None),
        check_vma=False,
    )
```

```python
import functools
import math

import jax
import jax.numpy as jnp
from jax import lax
from jax.experimental import pallas as pl
from jax.experimental.pallas import tpu as pltpu
from jax.sharding import PartitionSpec as P

HEADS = 4
CORES = 2
PER = HEADS // CORES
PAD = 16
LOW = -1e30
FLOOR = -1e29
BF16 = jnp.bfloat16
F32 = jnp.float32


def nt_dot(a, b):
    return lax.dot_general(a, b, (((1,), (1,)), ((), ())), preferred_element_type=F32)


def place(own, other, out, at, turned=False):
    tok = own.shape[0]
    size = own.shape[1] // HEADS
    core = lax.rem(lax.axis_index("inner"), CORES)
    for b, ref in enumerate((own, other)):
        for j in range(PER):
            piece = ref[:, pl.ds(pl.multiple_of((core * PER + j) * size, size), size)]
            if turned:
                piece = piece.astype(F32).T.astype(BF16)
            row = at + j * CORES * tok + b * tok
            out[row : row + tok, :] = piece


def starts(p0, p1, size):
    half = PAD // CORES
    return jnp.concatenate([jnp.full((half, size), p[0].astype(F32), F32) for p in (p0, p1)], axis=0).astype(BF16)


def merge_kernel(p0, p1, own, q1, k1, v1, q_out, kv_out):
    tok = q1.shape[0]
    rows = PER * CORES * tok
    pos = starts(p0, p1, q_out.shape[1])
    place(own.at[0:tok, :], q1, q_out, 0)
    q_out[rows:, :] = pos
    place(own.at[tok : 2 * tok, :], k1, kv_out, 0)
    kv_out[rows : rows + PAD, :] = pos
    place(own.at[2 * tok : 3 * tok, :], v1, kv_out, rows + PAD, turned=True)


def score_kernel(same, q_ref, *refs):
    k_refs, (p_ref, top_ref) = refs[:-2], refs[-2:]
    size = q_ref.shape[1]
    tok = size
    both = CORES * tok
    half = PAD // CORES
    rate = size ** -0.5 * math.log2(math.e)
    at_or_before = lax.broadcasted_iota(jnp.int32, (tok, tok), 0) <= lax.broadcasted_iota(jnp.int32, (tok, tok), 1)

    def block_of(ref):
        first = ref[PER * both : PER * both + PAD, :].astype(F32)
        return [first[b * half : b * half + 1, :] for b in range(CORES)]

    q_block = jnp.concatenate(block_of(q_ref), axis=1)
    kept = [jnp.concatenate([p] * CORES, axis=1) <= q_block for ref in k_refs for p in block_of(ref)]
    for h in range(PER):
        q = q_ref[h * both : (h + 1) * both, :]
        scores = []
        for j, ref in enumerate(k_refs):
            s = nt_dot(ref[h * both : (h + 1) * both, :], q)
            for b in range(CORES):
                part = s[b * tok : (b + 1) * tok, :]
                if same and j == 0:
                    cols = [part[:, c * tok : (c + 1) * tok] for c in range(CORES)]
                    cols[b] = jnp.where(at_or_before, cols[b], LOW)
                    part = jnp.concatenate(cols, axis=1)
                scores.append(part)
        tops = [jnp.where(k, jnp.max(s, axis=0, keepdims=True), FLOOR) for k, s in zip(kept, scores)]
        top = jnp.maximum(functools.reduce(jnp.maximum, tops), FLOOR).astype(BF16).astype(F32)
        for i, (k, s) in enumerate(zip(kept, scores)):
            p_ref[h, i * tok : (i + 1) * tok, :] = jnp.exp2((s - jnp.where(k, top, -LOW)) * rate).astype(BF16)
        top_ref[h * 8 : (h + 1) * 8, :] = jnp.broadcast_to(top, (8, both))


def apply_kernel(wide, rows, p_ref, top_ref, *refs):
    nv = len(refs) - (1 if wide else CORES)
    v_refs, out_refs = refs[:nv], refs[nv:]
    size = v_refs[0].shape[1]
    tok = size
    both = CORES * tok
    block = PER * size + PAD

    def store(b, at, value):
        if wide:
            out_refs[0][b * block + at : b * block + at + value.shape[0], :] = value
        else:
            out_refs[b][at : at + value.shape[0], :] = value

    stats = [[] for _ in range(CORES)]
    for h in range(PER):
        vals = []
        for ref, row in zip(v_refs, rows):
            for b in range(CORES):
                at = row + h * both + b * tok
                vals.append(ref[at : at + tok, :])
        vt = jnp.concatenate(vals, axis=1)
        vt = jnp.concatenate([vt, jnp.ones((PAD, vt.shape[1]), BF16)], axis=0)
        o = jnp.dot(vt, p_ref[h], preferred_element_type=F32)
        total = o[size : size + 1, :]
        hi = total.astype(BF16).astype(F32)
        top = top_ref[h * 8 : h * 8 + 1, :]
        for b in range(CORES):
            cols = slice(b * tok, (b + 1) * tok)
            store(b, h * size, o[0:size, cols].astype(BF16))
            stats[b] += [top[:, cols], hi[:, cols], (total - hi)[:, cols]]
    for b in range(CORES):
        rest = jnp.zeros((PAD - 3 * PER, tok), F32)
        store(b, PER * size, jnp.concatenate(stats[b] + [rest], axis=0).astype(BF16))


def joined(parts, stats, h, rate):
    size = parts[0].shape[0]
    tops = [s[3 * h : 3 * h + 1, :] for s in stats]
    best = functools.reduce(jnp.maximum, tops)
    factors = [jnp.exp2((t - best) * rate) for t in tops]
    total = sum(f * (s[3 * h + 1 : 3 * h + 2, :] + s[3 * h + 2 : 3 * h + 3, :]) for f, s in zip(factors, stats))
    numer = sum(f * part.astype(F32) for f, part in zip(factors, parts))
    return best, total, numer


def add_kernel(n, wide, *refs):
    size = refs[0].shape[1]
    block = PER * size + PAD
    rate = size ** -0.5 * math.log2(math.e)
    for b in range(CORES):
        base = b * block
        stats = [ref[base + PER * size : base + block, :].astype(F32) for ref in refs[:n]]
        out, at = (refs[n], base) if wide else (refs[n + b], 0)
        rows = []
        for h in range(PER):
            parts = [ref[base + h * size : base + (h + 1) * size, :] for ref in refs[:n]]
            best, total, numer = joined(parts, stats, h, rate)
            hi = total.astype(BF16).astype(F32)
            rows += [best, hi, total - hi]
            out[at + h * size : at + (h + 1) * size, :] = numer.astype(BF16)
        rest = jnp.zeros((PAD - 3 * PER, size), F32)
        out[at + PER * size : at + block, :] = jnp.concatenate(rows + [rest], axis=0).astype(BF16)


def combine_kernel(n, *refs):
    parts, out_ref = refs[:n], refs[n]
    size = parts[0].shape[1]
    rate = size ** -0.5 * math.log2(math.e)
    core = lax.rem(lax.axis_index("inner"), CORES)
    for x in range(CORES):
        mine = parts[x::CORES]
        pair = jnp.bitwise_xor(core, x)
        stats = [part[PER * size :, :].astype(F32) for part in mine]
        for h in range(PER):
            _, total, numer = joined([part[h * size : (h + 1) * size, :] for part in mine], stats, h, rate)
            cols = pl.ds(pl.multiple_of((pair * PER + h) * size, size), size)
            out_ref[:, cols] = (numer * (1.0 / total)).T.astype(BF16)


def vmem(n=1):
    return [pl.BlockSpec(memory_space=pltpu.VMEM)] * n


def shards(n_out, n_in, queries, keys, values, block_pos):
    tok, width = queries.shape
    size = width // HEADS
    chips = n_in // CORES
    both = CORES * tok
    params = pltpu.CompilerParams(vmem_limit_bytes=40 * 1024 * 1024)

    def along_inner(r, x):
        return [(w * CORES + c, (w ^ r) * CORES + (c ^ x)) for w in range(chips) for c in range(CORES)]

    def after(a, b):
        return lax.optimization_barrier((a, b))[0]

    with jax.named_scope("swap"):
        other = [lax.ppermute(a, "inner", along_inner(0, 1)) for a in (queries, keys, values, block_pos)]
        own = jnp.concatenate([queries, keys, values], axis=0)
    with jax.named_scope("merge"):
        smem = [pl.BlockSpec(memory_space=pltpu.SMEM)]
        q_piece, kv_piece = pl.pallas_call(
            merge_kernel,
            out_shape=(
                jax.ShapeDtypeStruct((PER * both + PAD, size), BF16),
                jax.ShapeDtypeStruct((2 * PER * both + PAD, size), BF16),
            ),
            in_specs=smem * 2 + vmem(4),
            out_specs=tuple(vmem(2)),
            compiler_params=params,
            name="merge",
        )(block_pos, other[3], own, *other[:3])
    half = PER * both + PAD
    block = PER * size + PAD

    def low(r):
        return r & -r

    def high(r):
        return 1 << (r.bit_length() - 1)

    def single(r):
        return r == low(r)

    def over(a, r):
        return lax.ppermute(a, "outer", [(o, o ^ r) for o in range(n_out)])

    with jax.named_scope("exchange"):
        whole = {r: over(kv_piece, r) if r else kv_piece for r in range(n_out) if single(r)}
        q_by = {0: q_piece}
        bit = chips // 2
        while bit:
            for r in sorted(q_by):
                piece = after(q_by[r], list(whole.values())[1:]) if r else q_piece
                q_by[r | bit] = lax.ppermute(piece, "inner", along_inner(bit, 0))
            bit //= 2
        k_by = {r: a[:half, :] for r, a in whole.items() if r}
        v_by = {r: a[half:, :] for r, a in whole.items() if r}
        if chips > 1:
            k_by = {r: after(a, q_by[1]) for r, a in k_by.items()}
        for r in range(1, n_out):
            if not single(r):
                k_by[r] = over(k_by[r - high(r)], high(r))
        for r in sorted(range(1, n_out), key=lambda r: r.bit_count()):
            if not single(r):
                v_by[r] = over(v_by[r - low(r)], low(r))
        ks = [whole[r] if r in whole else k_by[r] for r in range(n_out)]
        vs = [whole[r] if r in whole else v_by[r] for r in range(n_out)]
        rows = tuple(half if r in whole else 0 for r in range(n_out))

    def shapes(wide):
        rows = CORES * block if wide else block
        return (jax.ShapeDtypeStruct((rows, tok), BF16),) * (1 if wide else CORES)

    work = 2 * PER * both * n_out * both * size

    def score(r, done):
        with jax.named_scope("score"):
            return pl.pallas_call(
                functools.partial(score_kernel, r == 0),
                out_shape=(
                    jax.ShapeDtypeStruct((PER, n_out * both, both), BF16),
                    jax.ShapeDtypeStruct((PER * 8, both), F32),
                ),
                in_specs=vmem(1 + n_out),
                out_specs=tuple(vmem(2)),
                compiler_params=params,
                cost_estimate=pl.CostEstimate(flops=work, bytes_accessed=2**20, transcendentals=work // (2 * size)),
                name="score",
            )(q_by[r] if done is None else after(q_by[r], done), *ks)

    def apply(r, wide, done):
        with jax.named_scope("apply"):
            weights, tops = weights_by[r]
            return pl.pallas_call(
                functools.partial(apply_kernel, wide, rows),
                out_shape=shapes(wide),
                in_specs=vmem(2 + n_out),
                out_specs=tuple(vmem(len(shapes(wide)))),
                compiler_params=params,
                cost_estimate=pl.CostEstimate(flops=work, bytes_accessed=2**20, transcendentals=0),
                name="apply",
            )(weights, tops if done is None else after(tops, done), *vs)

    def add(arrays, wide):
        with jax.named_scope("add"):
            return pl.pallas_call(
                functools.partial(add_kernel, len(arrays), wide),
                out_shape=shapes(wide),
                in_specs=vmem(len(arrays)),
                out_specs=tuple(vmem(len(shapes(wide)))),
                compiler_params=params,
                name="add",
            )(*arrays)

    arrived = {r: [] for r in range(chips)}
    ends = []

    def send(r, parts):
        with jax.named_scope("return"):
            if single(r):
                ends.extend(lax.ppermute(parts[x], "inner", along_inner(r, x)) for x in range(CORES))
            else:
                arrived[r - low(r)].append(lax.ppermute(parts[0], "inner", along_inner(low(r), 0)))

    weights_by = {}
    done = None
    for r in range(chips):
        weights_by[r] = score(r, done)
        done = weights_by[r][1]
    done = None
    partial = {}
    for r in reversed(range(chips)):
        partial[r] = apply(r, r > 1, done)
        done = partial[r][0]
    for r in reversed(range(1, chips)):
        parts = partial[r]
        if arrived[r]:
            parts = add([parts[0], *arrived[r]], not single(r))
        send(r, parts)
    with jax.named_scope("return"):
        ends = [partial[0][0], lax.ppermute(partial[0][1], "inner", along_inner(0, 1))] + ends
    with jax.named_scope("combine"):
        return pl.pallas_call(
            functools.partial(combine_kernel, len(ends)),
            out_shape=jax.ShapeDtypeStruct((tok, width), BF16),
            in_specs=vmem(len(ends)),
            out_specs=vmem()[0],
            compiler_params=params,
            name="combine",
        )(*ends)


def solution(mesh):
    n_out, n_in = mesh.shape["outer"], mesh.shape["inner"]
    return jax.shard_map(
        functools.partial(shards, n_out, n_in),
        mesh=mesh,
        in_specs=(
            P(("outer", "inner"), None),
            P(("outer", "inner"), None),
            P(("outer", "inner"), None),
            P(("outer", "inner")),
        ),
        out_specs=P(("outer", "inner"), None),
        check_vma=False,
    )
```

```python
import functools
import math

import jax
import jax.numpy as jnp
from jax import lax
from jax.experimental import pallas as pl
from jax.experimental.pallas import tpu as pltpu
from jax.sharding import PartitionSpec as P

HEADS = 4
CORES = 2
PER = HEADS // CORES
PAD = 16
LOW = -1e30
FLOOR = -1e29
BF16 = jnp.bfloat16
F32 = jnp.float32


def nt_dot(a, b):
    return lax.dot_general(a, b, (((1,), (1,)), ((), ())), preferred_element_type=F32)


def place(own, other, out, at, turned=False):
    tok = own.shape[0]
    size = own.shape[1] // HEADS
    core = lax.rem(lax.axis_index("inner"), CORES)
    for b, ref in enumerate((own, other)):
        for j in range(PER):
            piece = ref[:, pl.ds(pl.multiple_of((core * PER + j) * size, size), size)]
            if turned:
                piece = piece.astype(F32).T.astype(BF16)
            row = at + j * CORES * tok + b * tok
            out[row : row + tok, :] = piece


def starts(p0, p1, size):
    half = PAD // CORES
    return jnp.concatenate([jnp.full((half, size), p[0].astype(F32), F32) for p in (p0, p1)], axis=0).astype(BF16)


def merge_kernel(p0, p1, own, q1, k1, v1, q_out, kv_out):
    tok = q1.shape[0]
    rows = PER * CORES * tok
    pos = starts(p0, p1, q_out.shape[1])
    place(own.at[0:tok, :], q1, q_out, 0)
    q_out[rows:, :] = pos
    place(own.at[tok : 2 * tok, :], k1, kv_out, 0)
    kv_out[rows : rows + PAD, :] = pos
    place(own.at[2 * tok : 3 * tok, :], v1, kv_out, rows + PAD, turned=True)


def score_kernel(same, q_ref, *refs):
    k_refs, (p_ref, top_ref) = refs[:-2], refs[-2:]
    size = q_ref.shape[1]
    tok = size
    both = CORES * tok
    half = PAD // CORES
    rate = size ** -0.5 * math.log2(math.e)
    at_or_before = lax.broadcasted_iota(jnp.int32, (tok, tok), 0) <= lax.broadcasted_iota(jnp.int32, (tok, tok), 1)

    def block_of(ref):
        first = ref[PER * both : PER * both + PAD, :].astype(F32)
        return [first[b * half : b * half + 1, :] for b in range(CORES)]

    q_block = jnp.concatenate(block_of(q_ref), axis=1)
    kept = [jnp.concatenate([p] * CORES, axis=1) <= q_block for ref in k_refs for p in block_of(ref)]
    for h in range(PER):
        q = q_ref[h * both : (h + 1) * both, :]
        scores = []
        for j, ref in enumerate(k_refs):
            s = nt_dot(ref[h * both : (h + 1) * both, :], q)
            for b in range(CORES):
                part = s[b * tok : (b + 1) * tok, :]
                if same and j == 0:
                    cols = [part[:, c * tok : (c + 1) * tok] for c in range(CORES)]
                    cols[b] = jnp.where(at_or_before, cols[b], LOW)
                    part = jnp.concatenate(cols, axis=1)
                scores.append(part)
        tops = [jnp.where(k, jnp.max(s, axis=0, keepdims=True), FLOOR) for k, s in zip(kept, scores)]
        top = jnp.maximum(functools.reduce(jnp.maximum, tops), FLOOR).astype(BF16).astype(F32)
        for i, (k, s) in enumerate(zip(kept, scores)):
            p_ref[h, i * tok : (i + 1) * tok, :] = jnp.exp2((s - jnp.where(k, top, -LOW)) * rate).astype(BF16)
        top_ref[h * 8 : (h + 1) * 8, :] = jnp.broadcast_to(top, (8, both))


def apply_kernel(wide, rows, p_ref, top_ref, *refs):
    nv = len(refs) - (1 if wide else CORES)
    v_refs, out_refs = refs[:nv], refs[nv:]
    size = v_refs[0].shape[1]
    tok = size
    both = CORES * tok
    block = PER * size + PAD

    def store(b, at, value):
        if wide:
            out_refs[0][b * block + at : b * block + at + value.shape[0], :] = value
        else:
            out_refs[b][at : at + value.shape[0], :] = value

    stats = [[] for _ in range(CORES)]
    for h in range(PER):
        vals = []
        for ref, row in zip(v_refs, rows):
            for b in range(CORES):
                at = row + h * both + b * tok
                vals.append(ref[at : at + tok, :])
        vt = jnp.concatenate(vals, axis=1)
        vt = jnp.concatenate([vt, jnp.ones((PAD, vt.shape[1]), BF16)], axis=0)
        o = jnp.dot(vt, p_ref[h], preferred_element_type=F32)
        total = o[size : size + 1, :]
        hi = total.astype(BF16).astype(F32)
        top = top_ref[h * 8 : h * 8 + 1, :]
        for b in range(CORES):
            cols = slice(b * tok, (b + 1) * tok)
            store(b, h * size, o[0:size, cols].astype(BF16))
            stats[b] += [top[:, cols], hi[:, cols], (total - hi)[:, cols]]
    for b in range(CORES):
        rest = jnp.zeros((PAD - 3 * PER, tok), F32)
        store(b, PER * size, jnp.concatenate(stats[b] + [rest], axis=0).astype(BF16))


def joined(parts, stats, h, rate):
    size = parts[0].shape[0]
    tops = [s[3 * h : 3 * h + 1, :] for s in stats]
    best = functools.reduce(jnp.maximum, tops)
    factors = [jnp.exp2((t - best) * rate) for t in tops]
    total = sum(f * (s[3 * h + 1 : 3 * h + 2, :] + s[3 * h + 2 : 3 * h + 3, :]) for f, s in zip(factors, stats))
    numer = sum(f * part.astype(F32) for f, part in zip(factors, parts))
    return best, total, numer


def add_kernel(n, wide, *refs):
    size = refs[0].shape[1]
    block = PER * size + PAD
    rate = size ** -0.5 * math.log2(math.e)
    for b in range(CORES):
        base = b * block
        stats = [ref[base + PER * size : base + block, :].astype(F32) for ref in refs[:n]]
        out, at = (refs[n], base) if wide else (refs[n + b], 0)
        rows = []
        for h in range(PER):
            parts = [ref[base + h * size : base + (h + 1) * size, :] for ref in refs[:n]]
            best, total, numer = joined(parts, stats, h, rate)
            hi = total.astype(BF16).astype(F32)
            rows += [best, hi, total - hi]
            out[at + h * size : at + (h + 1) * size, :] = numer.astype(BF16)
        rest = jnp.zeros((PAD - 3 * PER, size), F32)
        out[at + PER * size : at + block, :] = jnp.concatenate(rows + [rest], axis=0).astype(BF16)


def combine_kernel(n, *refs):
    parts, out_ref = refs[:n], refs[n]
    size = parts[0].shape[1]
    rate = size ** -0.5 * math.log2(math.e)
    core = lax.rem(lax.axis_index("inner"), CORES)
    for x in range(CORES):
        mine = parts[x::CORES]
        pair = jnp.bitwise_xor(core, x)
        stats = [part[PER * size :, :].astype(F32) for part in mine]
        for h in range(PER):
            _, total, numer = joined([part[h * size : (h + 1) * size, :] for part in mine], stats, h, rate)
            cols = pl.ds(pl.multiple_of((pair * PER + h) * size, size), size)
            out_ref[:, cols] = (numer * (1.0 / total)).T.astype(BF16)


def vmem(n=1):
    return [pl.BlockSpec(memory_space=pltpu.VMEM)] * n


def shards(n_out, n_in, queries, keys, values, block_pos):
    tok, width = queries.shape
    size = width // HEADS
    chips = n_in // CORES
    both = CORES * tok
    params = pltpu.CompilerParams(vmem_limit_bytes=40 * 1024 * 1024)

    def along_inner(r, x):
        return [(w * CORES + c, (w ^ r) * CORES + (c ^ x)) for w in range(chips) for c in range(CORES)]

    def after(a, b):
        return lax.optimization_barrier((a, b))[0]

    with jax.named_scope("swap"):
        other = [lax.ppermute(a, "inner", along_inner(0, 1)) for a in (queries, keys, values, block_pos)]
        own = jnp.concatenate([queries, keys, values], axis=0)
    with jax.named_scope("merge"):
        smem = [pl.BlockSpec(memory_space=pltpu.SMEM)]
        q_piece, kv_piece = pl.pallas_call(
            merge_kernel,
            out_shape=(
                jax.ShapeDtypeStruct((PER * both + PAD, size), BF16),
                jax.ShapeDtypeStruct((2 * PER * both + PAD, size), BF16),
            ),
            in_specs=smem * 2 + vmem(4),
            out_specs=tuple(vmem(2)),
            compiler_params=params,
            name="merge",
        )(block_pos, other[3], own, *other[:3])
    half = PER * both + PAD
    block = PER * size + PAD

    def low(r):
        return r & -r

    def high(r):
        return 1 << (r.bit_length() - 1)

    def single(r):
        return r == low(r)

    def over(a, r):
        return lax.ppermute(a, "outer", [(o, o ^ r) for o in range(n_out)])

    with jax.named_scope("exchange"):
        whole = {r: over(kv_piece, r) if r else kv_piece for r in range(n_out) if single(r)}
        q_by = {0: q_piece}
        for r in reversed(range(1, chips)):
            q_by[r] = lax.ppermute(q_piece, "inner", along_inner(r, 0))
        k_by = {r: a[:half, :] for r, a in whole.items() if r}
        v_by = {r: a[half:, :] for r, a in whole.items() if r}
        if chips > 1:
            k_by = {r: after(a, q_by[1]) for r, a in k_by.items()}
        for r in range(1, n_out):
            if not single(r):
                k_by[r] = over(k_by[r - high(r)], high(r))
        for r in sorted(range(1, n_out), key=lambda r: r.bit_count()):
            if not single(r):
                v_by[r] = over(v_by[r - low(r)], low(r))
        ks = [whole[r] if r in whole else k_by[r] for r in range(n_out)]
        vs = [whole[r] if r in whole else v_by[r] for r in range(n_out)]
        rows = tuple(half if r in whole else 0 for r in range(n_out))

    def shapes(wide):
        rows = CORES * block if wide else block
        return (jax.ShapeDtypeStruct((rows, tok), BF16),) * (1 if wide else CORES)

    work = 2 * PER * both * n_out * both * size

    def score(r, done):
        with jax.named_scope("score"):
            return pl.pallas_call(
                functools.partial(score_kernel, r == 0),
                out_shape=(
                    jax.ShapeDtypeStruct((PER, n_out * both, both), BF16),
                    jax.ShapeDtypeStruct((PER * 8, both), F32),
                ),
                in_specs=vmem(1 + n_out),
                out_specs=tuple(vmem(2)),
                compiler_params=params,
                cost_estimate=pl.CostEstimate(flops=work, bytes_accessed=2**20, transcendentals=work // (2 * size)),
                name="score",
            )(q_by[r] if done is None else after(q_by[r], done), *ks)

    def apply(r, wide):
        with jax.named_scope("apply"):
            return pl.pallas_call(
                functools.partial(apply_kernel, wide, rows),
                out_shape=shapes(wide),
                in_specs=vmem(2 + n_out),
                out_specs=tuple(vmem(len(shapes(wide)))),
                compiler_params=params,
                cost_estimate=pl.CostEstimate(flops=work, bytes_accessed=2**20, transcendentals=0),
                name="apply",
            )(*weights_by[r], *vs)

    def add(arrays, wide):
        with jax.named_scope("add"):
            return pl.pallas_call(
                functools.partial(add_kernel, len(arrays), wide),
                out_shape=shapes(wide),
                in_specs=vmem(len(arrays)),
                out_specs=tuple(vmem(len(shapes(wide)))),
                compiler_params=params,
                name="add",
            )(*arrays)

    arrived = {r: [] for r in range(chips)}
    ends = []

    def send(r, parts):
        with jax.named_scope("return"):
            if single(r):
                ends.extend(lax.ppermute(parts[x], "inner", along_inner(r, x)) for x in range(CORES))
            else:
                arrived[r - low(r)].append(lax.ppermute(parts[0], "inner", along_inner(low(r), 0)))

    done = None
    weights_by, partial = {}, {}
    for r in reversed(range(chips)):
        weights_by[r] = score(r, done)
        partial[r] = apply(r, r > 1)
        done = partial[r][0]
    for r in reversed(range(1, chips)):
        parts = partial[r]
        if arrived[r]:
            parts = add([parts[0], *arrived[r]], not single(r))
        send(r, parts)
    with jax.named_scope("return"):
        ends = [partial[0][0], lax.ppermute(partial[0][1], "inner", along_inner(0, 1))] + ends
    with jax.named_scope("combine"):
        return pl.pallas_call(
            functools.partial(combine_kernel, len(ends)),
            out_shape=jax.ShapeDtypeStruct((tok, width), BF16),
            in_specs=vmem(len(ends)),
            out_specs=vmem()[0],
            compiler_params=params,
            name="combine",
        )(*ends)


def solution(mesh):
    n_out, n_in = mesh.shape["outer"], mesh.shape["inner"]
    return jax.shard_map(
        functools.partial(shards, n_out, n_in),
        mesh=mesh,
        in_specs=(
            P(("outer", "inner"), None),
            P(("outer", "inner"), None),
            P(("outer", "inner"), None),
            P(("outer", "inner")),
        ),
        out_specs=P(("outer", "inner"), None),
        check_vma=False,
    )
```

```python
import functools
import math

import jax
import jax.numpy as jnp
from jax import lax
from jax.experimental import pallas as pl
from jax.experimental.pallas import tpu as pltpu
from jax.sharding import PartitionSpec as P

HEADS = 4
CORES = 2
PER = HEADS // CORES
PAD = 16
LOW = -1e30
FLOOR = -1e29
BF16 = jnp.bfloat16
F32 = jnp.float32


def nt_dot(a, b):
    return lax.dot_general(a, b, (((1,), (1,)), ((), ())), preferred_element_type=F32)


def place(own, other, out, at, turned=False):
    tok = own.shape[0]
    size = own.shape[1] // HEADS
    core = lax.rem(lax.axis_index("inner"), CORES)
    for b, ref in enumerate((own, other)):
        for j in range(PER):
            piece = ref[:, pl.ds(pl.multiple_of((core * PER + j) * size, size), size)]
            if turned:
                piece = piece.astype(F32).T.astype(BF16)
            row = at + j * CORES * tok + b * tok
            out[row : row + tok, :] = piece


def starts(p0, p1, size):
    half = PAD // CORES
    return jnp.concatenate([jnp.full((half, size), p[0].astype(F32), F32) for p in (p0, p1)], axis=0).astype(BF16)


def merge_kernel(p0, p1, own, q1, k1, v1, q_out, kv_out):
    tok = q1.shape[0]
    rows = PER * CORES * tok
    pos = starts(p0, p1, q_out.shape[1])
    place(own.at[0:tok, :], q1, q_out, 0)
    q_out[rows:, :] = pos
    place(own.at[tok : 2 * tok, :], k1, kv_out, 0)
    kv_out[rows : rows + PAD, :] = pos
    place(own.at[2 * tok : 3 * tok, :], v1, kv_out, rows + PAD, turned=True)


def score_kernel(same, q_ref, *refs):
    k_refs, (p_ref, top_ref) = refs[:-2], refs[-2:]
    size = q_ref.shape[1]
    tok = size
    both = CORES * tok
    half = PAD // CORES
    rate = size ** -0.5 * math.log2(math.e)
    at_or_before = lax.broadcasted_iota(jnp.int32, (tok, tok), 0) <= lax.broadcasted_iota(jnp.int32, (tok, tok), 1)

    def block_of(ref):
        first = ref[PER * both : PER * both + PAD, :].astype(F32)
        return [first[b * half : b * half + 1, :] for b in range(CORES)]

    q_block = jnp.concatenate(block_of(q_ref), axis=1)
    kept = [jnp.concatenate([p] * CORES, axis=1) <= q_block for ref in k_refs for p in block_of(ref)]
    for h in range(PER):
        q = q_ref[h * both : (h + 1) * both, :]
        scores = []
        for j, ref in enumerate(k_refs):
            s = nt_dot(ref[h * both : (h + 1) * both, :], q)
            for b in range(CORES):
                part = s[b * tok : (b + 1) * tok, :]
                if same and j == 0:
                    cols = [part[:, c * tok : (c + 1) * tok] for c in range(CORES)]
                    cols[b] = jnp.where(at_or_before, cols[b], LOW)
                    part = jnp.concatenate(cols, axis=1)
                scores.append(part)
        tops = [jnp.where(k, jnp.max(s, axis=0, keepdims=True), FLOOR) for k, s in zip(kept, scores)]
        top = jnp.maximum(functools.reduce(jnp.maximum, tops), FLOOR).astype(BF16).astype(F32)
        for i, (k, s) in enumerate(zip(kept, scores)):
            p_ref[h, i * tok : (i + 1) * tok, :] = jnp.exp2((s - jnp.where(k, top, -LOW)) * rate).astype(BF16)
        top_ref[h * 8 : (h + 1) * 8, :] = jnp.broadcast_to(top, (8, both))


def apply_kernel(wide, rows, p_ref, top_ref, *refs):
    nv = len(refs) - (1 if wide else CORES)
    v_refs, out_refs = refs[:nv], refs[nv:]
    size = v_refs[0].shape[1]
    tok = size
    both = CORES * tok
    block = PER * size + PAD

    def store(b, at, value):
        if wide:
            out_refs[0][b * block + at : b * block + at + value.shape[0], :] = value
        else:
            out_refs[b][at : at + value.shape[0], :] = value

    stats = [[] for _ in range(CORES)]
    for h in range(PER):
        vals = []
        for ref, row in zip(v_refs, rows):
            for b in range(CORES):
                at = row + h * both + b * tok
                vals.append(ref[at : at + tok, :])
        vt = jnp.concatenate(vals, axis=1)
        vt = jnp.concatenate([vt, jnp.ones((PAD, vt.shape[1]), BF16)], axis=0)
        o = jnp.dot(vt, p_ref[h], preferred_element_type=F32)
        total = o[size : size + 1, :]
        hi = total.astype(BF16).astype(F32)
        top = top_ref[h * 8 : h * 8 + 1, :]
        for b in range(CORES):
            cols = slice(b * tok, (b + 1) * tok)
            store(b, h * size, o[0:size, cols].astype(BF16))
            stats[b] += [top[:, cols], hi[:, cols], (total - hi)[:, cols]]
    for b in range(CORES):
        rest = jnp.zeros((PAD - 3 * PER, tok), F32)
        store(b, PER * size, jnp.concatenate(stats[b] + [rest], axis=0).astype(BF16))


def joined(parts, stats, h, rate):
    size = parts[0].shape[0]
    tops = [s[3 * h : 3 * h + 1, :] for s in stats]
    best = functools.reduce(jnp.maximum, tops)
    factors = [jnp.exp2((t - best) * rate) for t in tops]
    total = sum(f * (s[3 * h + 1 : 3 * h + 2, :] + s[3 * h + 2 : 3 * h + 3, :]) for f, s in zip(factors, stats))
    numer = sum(f * part.astype(F32) for f, part in zip(factors, parts))
    return best, total, numer


def add_kernel(n, wide, *refs):
    size = refs[0].shape[1]
    block = PER * size + PAD
    rate = size ** -0.5 * math.log2(math.e)
    for b in range(CORES):
        base = b * block
        stats = [ref[base + PER * size : base + block, :].astype(F32) for ref in refs[:n]]
        out, at = (refs[n], base) if wide else (refs[n + b], 0)
        rows = []
        for h in range(PER):
            parts = [ref[base + h * size : base + (h + 1) * size, :] for ref in refs[:n]]
            best, total, numer = joined(parts, stats, h, rate)
            hi = total.astype(BF16).astype(F32)
            rows += [best, hi, total - hi]
            out[at + h * size : at + (h + 1) * size, :] = numer.astype(BF16)
        rest = jnp.zeros((PAD - 3 * PER, size), F32)
        out[at + PER * size : at + block, :] = jnp.concatenate(rows + [rest], axis=0).astype(BF16)


def combine_kernel(n, *refs):
    parts, out_ref = refs[:n], refs[n]
    size = parts[0].shape[1]
    rate = size ** -0.5 * math.log2(math.e)
    core = lax.rem(lax.axis_index("inner"), CORES)
    for x in range(CORES):
        mine = parts[x::CORES]
        pair = jnp.bitwise_xor(core, x)
        stats = [part[PER * size :, :].astype(F32) for part in mine]
        for h in range(PER):
            _, total, numer = joined([part[h * size : (h + 1) * size, :] for part in mine], stats, h, rate)
            cols = pl.ds(pl.multiple_of((pair * PER + h) * size, size), size)
            out_ref[:, cols] = (numer * (1.0 / total)).T.astype(BF16)


def vmem(n=1):
    return [pl.BlockSpec(memory_space=pltpu.VMEM)] * n


def shards(n_out, n_in, queries, keys, values, block_pos):
    tok, width = queries.shape
    size = width // HEADS
    chips = n_in // CORES
    both = CORES * tok
    params = pltpu.CompilerParams(vmem_limit_bytes=40 * 1024 * 1024)

    def along_inner(r, x):
        return [(w * CORES + c, (w ^ r) * CORES + (c ^ x)) for w in range(chips) for c in range(CORES)]

    def after(a, b):
        return lax.optimization_barrier((a, b))[0]

    with jax.named_scope("swap"):
        other = [lax.ppermute(a, "inner", along_inner(0, 1)) for a in (queries, keys, values, block_pos)]
        own = jnp.concatenate([queries, keys, values], axis=0)
    with jax.named_scope("merge"):
        smem = [pl.BlockSpec(memory_space=pltpu.SMEM)]
        q_piece, kv_piece = pl.pallas_call(
            merge_kernel,
            out_shape=(
                jax.ShapeDtypeStruct((PER * both + PAD, size), BF16),
                jax.ShapeDtypeStruct((2 * PER * both + PAD, size), BF16),
            ),
            in_specs=smem * 2 + vmem(4),
            out_specs=tuple(vmem(2)),
            compiler_params=params,
            name="merge",
        )(block_pos, other[3], own, *other[:3])
    half = PER * both + PAD
    block = PER * size + PAD

    def low(r):
        return r & -r

    def high(r):
        return 1 << (r.bit_length() - 1)

    def single(r):
        return r == low(r)

    def over(a, r):
        return lax.ppermute(a, "outer", [(o, o ^ r) for o in range(n_out)])

    with jax.named_scope("exchange"):
        whole = {r: over(kv_piece, r) if r else kv_piece for r in range(n_out) if single(r)}
        q_by = {0: q_piece}
        for r in reversed(range(1, chips)):
            q_by[r] = lax.ppermute(q_piece, "inner", along_inner(r, 0))
        k_by = {r: a[:half, :] for r, a in whole.items() if r}
        v_by = {r: a[half:, :] for r, a in whole.items() if r}
        if chips > 1:
            k_by = {r: after(a, q_by[1]) for r, a in k_by.items()}
        for r in range(1, n_out):
            if not single(r):
                k_by[r] = over(k_by[r - high(r)], high(r))
        for r in sorted(range(1, n_out), key=lambda r: r.bit_count()):
            if not single(r):
                v_by[r] = over(v_by[r - low(r)], low(r))
        ks = [whole[r] if r in whole else k_by[r] for r in range(n_out)]
        vs = [whole[r] if r in whole else v_by[r] for r in range(n_out)]
        rows = tuple(half if r in whole else 0 for r in range(n_out))

    def shapes(wide):
        rows = CORES * block if wide else block
        return (jax.ShapeDtypeStruct((rows, tok), BF16),) * (1 if wide else CORES)

    work = 2 * PER * both * n_out * both * size

    def score(r, done):
        with jax.named_scope("score"):
            return pl.pallas_call(
                functools.partial(score_kernel, r == 0),
                out_shape=(
                    jax.ShapeDtypeStruct((PER, n_out * both, both), BF16),
                    jax.ShapeDtypeStruct((PER * 8, both), F32),
                ),
                in_specs=vmem(1 + n_out),
                out_specs=tuple(vmem(2)),
                compiler_params=params,
                cost_estimate=pl.CostEstimate(flops=work, bytes_accessed=2**20, transcendentals=work // (2 * size)),
                name="score",
            )(q_by[r] if done is None else after(q_by[r], done), *ks)

    def apply(r, wide):
        with jax.named_scope("apply"):
            return pl.pallas_call(
                functools.partial(apply_kernel, wide, rows),
                out_shape=shapes(wide),
                in_specs=vmem(2 + n_out),
                out_specs=tuple(vmem(len(shapes(wide)))),
                compiler_params=params,
                cost_estimate=pl.CostEstimate(flops=work, bytes_accessed=2**20, transcendentals=0),
                name="apply",
            )(*weights_by[r], *vs)

    def add(arrays, wide):
        with jax.named_scope("add"):
            return pl.pallas_call(
                functools.partial(add_kernel, len(arrays), wide),
                out_shape=shapes(wide),
                in_specs=vmem(len(arrays)),
                out_specs=tuple(vmem(len(shapes(wide)))),
                compiler_params=params,
                name="add",
            )(*arrays)

    arrived = {r: [] for r in range(chips)}
    ends = []

    def send(r, parts):
        with jax.named_scope("return"):
            if single(r):
                ends.extend(lax.ppermute(parts[x], "inner", along_inner(r, x)) for x in range(CORES))
            else:
                arrived[r - low(r)].append(lax.ppermute(parts[0], "inner", along_inner(low(r), 0)))

    def both_kernels(r, done):
        weights_by[r] = score(r, done)
        partial[r] = apply(r, r > 1)
        return partial[r][0]

    done = None
    weights_by, partial = {}, {}
    for r in reversed(range(1, chips)):
        done = both_kernels(r, done)
    for r in reversed(range(1, chips)):
        parts = partial[r]
        if arrived[r]:
            parts = add([parts[0], *arrived[r]], not single(r))
            done = parts[0]
        if r == 1:
            parts = [parts[0], after(parts[1], done)]
        send(r, parts)
    both_kernels(0, done)
    with jax.named_scope("return"):
        ends = [partial[0][0], lax.ppermute(partial[0][1], "inner", along_inner(0, 1))] + ends
    with jax.named_scope("combine"):
        return pl.pallas_call(
            functools.partial(combine_kernel, len(ends)),
            out_shape=jax.ShapeDtypeStruct((tok, width), BF16),
            in_specs=vmem(len(ends)),
            out_specs=vmem()[0],
            compiler_params=params,
            name="combine",
        )(*ends)


def solution(mesh):
    n_out, n_in = mesh.shape["outer"], mesh.shape["inner"]
    return jax.shard_map(
        functools.partial(shards, n_out, n_in),
        mesh=mesh,
        in_specs=(
            P(("outer", "inner"), None),
            P(("outer", "inner"), None),
            P(("outer", "inner"), None),
            P(("outer", "inner")),
        ),
        out_specs=P(("outer", "inner"), None),
        check_vma=False,
    )
```

```python
import functools
import math

import jax
import jax.numpy as jnp
from jax import lax
from jax.experimental import pallas as pl
from jax.experimental.pallas import tpu as pltpu
from jax.sharding import PartitionSpec as P

HEADS = 4
CORES = 2
PER = HEADS // CORES
PAD = 16
LOW = -1e30
FLOOR = -1e29
BF16 = jnp.bfloat16
F32 = jnp.float32


def nt_dot(a, b):
    return lax.dot_general(a, b, (((1,), (1,)), ((), ())), preferred_element_type=F32)


def place(own, other, out, at, turned=False):
    tok = own.shape[0]
    size = own.shape[1] // HEADS
    core = lax.rem(lax.axis_index("inner"), CORES)
    for b, ref in enumerate((own, other)):
        for j in range(PER):
            piece = ref[:, pl.ds(pl.multiple_of((core * PER + j) * size, size), size)]
            if turned:
                piece = piece.astype(F32).T.astype(BF16)
            row = at + j * CORES * tok + b * tok
            out[row : row + tok, :] = piece


def starts(p0, p1, size):
    half = PAD // CORES
    return jnp.concatenate([jnp.full((half, size), p[0].astype(F32), F32) for p in (p0, p1)], axis=0).astype(BF16)


def merge_kernel(p0, p1, own, q1, k1, v1, q_out, kv_out):
    tok = q1.shape[0]
    rows = PER * CORES * tok
    pos = starts(p0, p1, q_out.shape[1])
    place(own.at[0:tok, :], q1, q_out, 0)
    q_out[rows:, :] = pos
    place(own.at[tok : 2 * tok, :], k1, kv_out, 0)
    kv_out[rows : rows + PAD, :] = pos
    place(own.at[2 * tok : 3 * tok, :], v1, kv_out, rows + PAD, turned=True)


def score_kernel(same, q_ref, *refs):
    k_refs, (p_ref, top_ref) = refs[:-2], refs[-2:]
    size = q_ref.shape[1]
    tok = size
    both = CORES * tok
    half = PAD // CORES
    rate = size ** -0.5 * math.log2(math.e)
    at_or_before = lax.broadcasted_iota(jnp.int32, (tok, tok), 0) <= lax.broadcasted_iota(jnp.int32, (tok, tok), 1)

    def block_of(ref):
        first = ref[PER * both : PER * both + PAD, :].astype(F32)
        return [first[b * half : b * half + 1, :] for b in range(CORES)]

    q_block = jnp.concatenate(block_of(q_ref), axis=1)
    kept = [jnp.concatenate([p] * CORES, axis=1) <= q_block for ref in k_refs for p in block_of(ref)]
    for h in range(PER):
        q = q_ref[h * both : (h + 1) * both, :]
        scores = []
        for j, ref in enumerate(k_refs):
            s = nt_dot(ref[h * both : (h + 1) * both, :], q)
            for b in range(CORES):
                part = s[b * tok : (b + 1) * tok, :]
                if same and j == 0:
                    cols = [part[:, c * tok : (c + 1) * tok] for c in range(CORES)]
                    cols[b] = jnp.where(at_or_before, cols[b], LOW)
                    part = jnp.concatenate(cols, axis=1)
                scores.append(part)
        tops = [jnp.where(k, jnp.max(s, axis=0, keepdims=True), FLOOR) for k, s in zip(kept, scores)]
        top = jnp.maximum(functools.reduce(jnp.maximum, tops), FLOOR).astype(BF16).astype(F32)
        for i, (k, s) in enumerate(zip(kept, scores)):
            p_ref[h, i * tok : (i + 1) * tok, :] = jnp.exp2((s - jnp.where(k, top, -LOW)) * rate).astype(BF16)
        top_ref[h * 8 : (h + 1) * 8, :] = jnp.broadcast_to(top, (8, both))


def apply_kernel(wide, rows, p_ref, top_ref, *refs):
    nv = len(refs) - (1 if wide else CORES)
    v_refs, out_refs = refs[:nv], refs[nv:]
    size = v_refs[0].shape[1]
    tok = size
    both = CORES * tok
    block = PER * size + PAD

    def store(b, at, value):
        if wide:
            out_refs[0][b * block + at : b * block + at + value.shape[0], :] = value
        else:
            out_refs[b][at : at + value.shape[0], :] = value

    stats = [[] for _ in range(CORES)]
    for h in range(PER):
        vals = []
        for ref, row in zip(v_refs, rows):
            for b in range(CORES):
                at = row + h * both + b * tok
                vals.append(ref[at : at + tok, :])
        vt = jnp.concatenate(vals, axis=1)
        vt = jnp.concatenate([vt, jnp.ones((PAD, vt.shape[1]), BF16)], axis=0)
        o = jnp.dot(vt, p_ref[h], preferred_element_type=F32)
        total = o[size : size + 1, :]
        hi = total.astype(BF16).astype(F32)
        top = top_ref[h * 8 : h * 8 + 1, :]
        for b in range(CORES):
            cols = slice(b * tok, (b + 1) * tok)
            store(b, h * size, o[0:size, cols].astype(BF16))
            stats[b] += [top[:, cols], hi[:, cols], (total - hi)[:, cols]]
    for b in range(CORES):
        rest = jnp.zeros((PAD - 3 * PER, tok), F32)
        store(b, PER * size, jnp.concatenate(stats[b] + [rest], axis=0).astype(BF16))


def joined(parts, stats, h, rate):
    size = parts[0].shape[0]
    tops = [s[3 * h : 3 * h + 1, :] for s in stats]
    best = functools.reduce(jnp.maximum, tops)
    factors = [jnp.exp2((t - best) * rate) for t in tops]
    total = sum(f * (s[3 * h + 1 : 3 * h + 2, :] + s[3 * h + 2 : 3 * h + 3, :]) for f, s in zip(factors, stats))
    numer = sum(f * part.astype(F32) for f, part in zip(factors, parts))
    return best, total, numer


def add_kernel(n, wide, *refs):
    size = refs[0].shape[1]
    block = PER * size + PAD
    rate = size ** -0.5 * math.log2(math.e)
    for b in range(CORES):
        base = b * block
        stats = [ref[base + PER * size : base + block, :].astype(F32) for ref in refs[:n]]
        out, at = (refs[n], base) if wide else (refs[n + b], 0)
        rows = []
        for h in range(PER):
            parts = [ref[base + h * size : base + (h + 1) * size, :] for ref in refs[:n]]
            best, total, numer = joined(parts, stats, h, rate)
            hi = total.astype(BF16).astype(F32)
            rows += [best, hi, total - hi]
            out[at + h * size : at + (h + 1) * size, :] = numer.astype(BF16)
        rest = jnp.zeros((PAD - 3 * PER, size), F32)
        out[at + PER * size : at + block, :] = jnp.concatenate(rows + [rest], axis=0).astype(BF16)


def combine_kernel(n, *refs):
    parts, out_ref = refs[:n], refs[n]
    size = parts[0].shape[1]
    rate = size ** -0.5 * math.log2(math.e)
    core = lax.rem(lax.axis_index("inner"), CORES)
    for x in range(CORES):
        mine = parts[x::CORES]
        pair = jnp.bitwise_xor(core, x)
        stats = [part[PER * size :, :].astype(F32) for part in mine]
        for h in range(PER):
            _, total, numer = joined([part[h * size : (h + 1) * size, :] for part in mine], stats, h, rate)
            cols = pl.ds(pl.multiple_of((pair * PER + h) * size, size), size)
            out_ref[:, cols] = (numer * (1.0 / total)).T.astype(BF16)


def vmem(n=1):
    return [pl.BlockSpec(memory_space=pltpu.VMEM)] * n


def shards(n_out, n_in, queries, keys, values, block_pos):
    tok, width = queries.shape
    size = width // HEADS
    chips = n_in // CORES
    both = CORES * tok
    params = pltpu.CompilerParams(vmem_limit_bytes=40 * 1024 * 1024)

    def along_inner(r, x):
        return [(w * CORES + c, (w ^ r) * CORES + (c ^ x)) for w in range(chips) for c in range(CORES)]

    def after(a, b):
        return lax.optimization_barrier((a, b))[0]

    with jax.named_scope("swap"):
        other = [lax.ppermute(a, "inner", along_inner(0, 1)) for a in (queries, keys, values, block_pos)]
        own = jnp.concatenate([queries, keys, values], axis=0)
    with jax.named_scope("merge"):
        smem = [pl.BlockSpec(memory_space=pltpu.SMEM)]
        q_piece, kv_piece = pl.pallas_call(
            merge_kernel,
            out_shape=(
                jax.ShapeDtypeStruct((PER * both + PAD, size), BF16),
                jax.ShapeDtypeStruct((2 * PER * both + PAD, size), BF16),
            ),
            in_specs=smem * 2 + vmem(4),
            out_specs=tuple(vmem(2)),
            compiler_params=params,
            name="merge",
        )(block_pos, other[3], own, *other[:3])
    half = PER * both + PAD
    block = PER * size + PAD

    def low(r):
        return r & -r

    def high(r):
        return 1 << (r.bit_length() - 1)

    def single(r):
        return r == low(r)

    def over(a, r):
        return lax.ppermute(a, "outer", [(o, o ^ r) for o in range(n_out)])

    with jax.named_scope("exchange"):
        whole = {r: over(kv_piece, r) if r else kv_piece for r in range(n_out) if single(r) and r != 1}
        k_by = {r: a[:half, :] for r, a in whole.items()}
        v_by = {r: a[half:, :] for r, a in whole.items()}
        if n_out > 1:
            k_by[1], v_by[1] = over(k_by[0], 1), over(v_by[0], 1)
        q_by = {0: q_piece}
        for r in reversed(range(1, chips)):
            q_by[r] = lax.ppermute(q_piece, "inner", along_inner(r, 0))
        for r in sorted(range(1, n_out), key=lambda r: r.bit_count()):
            if not single(r):
                k = k_by[r - high(r)]
                k_by[r] = over(after(k, q_by[1]) if chips > 1 else k, high(r))
                v_by[r] = over(v_by[r - low(r)], low(r))
        ks = [whole[r] if r in whole else k_by[r] for r in range(n_out)]
        vs = [whole[r] if r in whole else v_by[r] for r in range(n_out)]
        rows = tuple(half if r in whole else 0 for r in range(n_out))

    def shapes(wide):
        rows = CORES * block if wide else block
        return (jax.ShapeDtypeStruct((rows, tok), BF16),) * (1 if wide else CORES)

    work = 2 * PER * both * n_out * both * size

    def score(r, done):
        with jax.named_scope("score"):
            return pl.pallas_call(
                functools.partial(score_kernel, r == 0),
                out_shape=(
                    jax.ShapeDtypeStruct((PER, n_out * both, both), BF16),
                    jax.ShapeDtypeStruct((PER * 8, both), F32),
                ),
                in_specs=vmem(1 + n_out),
                out_specs=tuple(vmem(2)),
                compiler_params=params,
                cost_estimate=pl.CostEstimate(flops=work, bytes_accessed=2**20, transcendentals=work // (2 * size)),
                name="score",
            )(q_by[r] if done is None else after(q_by[r], done), *ks)

    def apply(r, wide):
        with jax.named_scope("apply"):
            return pl.pallas_call(
                functools.partial(apply_kernel, wide, rows),
                out_shape=shapes(wide),
                in_specs=vmem(2 + n_out),
                out_specs=tuple(vmem(len(shapes(wide)))),
                compiler_params=params,
                cost_estimate=pl.CostEstimate(flops=work, bytes_accessed=2**20, transcendentals=0),
                name="apply",
            )(*weights_by[r], *vs)

    def add(arrays, wide):
        with jax.named_scope("add"):
            return pl.pallas_call(
                functools.partial(add_kernel, len(arrays), wide),
                out_shape=shapes(wide),
                in_specs=vmem(len(arrays)),
                out_specs=tuple(vmem(len(shapes(wide)))),
                compiler_params=params,
                name="add",
            )(*arrays)

    arrived = {r: [] for r in range(chips)}
    ends = []

    def send(r, parts):
        with jax.named_scope("return"):
            if single(r):
                ends.extend(lax.ppermute(parts[x], "inner", along_inner(r, x)) for x in range(CORES))
            else:
                arrived[r - low(r)].append(lax.ppermute(parts[0], "inner", along_inner(low(r), 0)))

    def both_kernels(r, done):
        weights_by[r] = score(r, done)
        partial[r] = apply(r, r > 1)
        return partial[r][0]

    done = None
    weights_by, partial = {}, {}
    for r in reversed(range(1, chips)):
        done = both_kernels(r, done)
    for r in reversed(range(1, chips)):
        parts = partial[r]
        if arrived[r]:
            parts = add([parts[0], *arrived[r]], not single(r))
            done = parts[0]
        if r == 1:
            parts = [parts[0], after(parts[1], done)]
        send(r, parts)
    both_kernels(0, done)
    with jax.named_scope("return"):
        ends = [partial[0][0], lax.ppermute(partial[0][1], "inner", along_inner(0, 1))] + ends
    with jax.named_scope("combine"):
        return pl.pallas_call(
            functools.partial(combine_kernel, len(ends)),
            out_shape=jax.ShapeDtypeStruct((tok, width), BF16),
            in_specs=vmem(len(ends)),
            out_specs=vmem()[0],
            compiler_params=params,
            name="combine",
        )(*ends)


def solution(mesh):
    n_out, n_in = mesh.shape["outer"], mesh.shape["inner"]
    return jax.shard_map(
        functools.partial(shards, n_out, n_in),
        mesh=mesh,
        in_specs=(
            P(("outer", "inner"), None),
            P(("outer", "inner"), None),
            P(("outer", "inner"), None),
            P(("outer", "inner")),
        ),
        out_specs=P(("outer", "inner"), None),
        check_vma=False,
    )
```

```python
import functools
import math

import jax
import jax.numpy as jnp
from jax import lax
from jax.experimental import pallas as pl
from jax.experimental.pallas import tpu as pltpu
from jax.sharding import PartitionSpec as P

HEADS = 4
CORES = 2
PER = HEADS // CORES
PAD = 16
LOW = -1e30
FLOOR = -1e29
BF16 = jnp.bfloat16
F32 = jnp.float32


def nt_dot(a, b):
    return lax.dot_general(a, b, (((1,), (1,)), ((), ())), preferred_element_type=F32)


def place(own, other, out, at, turned=False):
    tok = own.shape[0]
    size = own.shape[1] // HEADS
    core = lax.rem(lax.axis_index("inner"), CORES)
    for b, ref in enumerate((own, other)):
        for j in range(PER):
            piece = ref[:, pl.ds(pl.multiple_of((core * PER + j) * size, size), size)]
            if turned:
                piece = piece.astype(F32).T.astype(BF16)
            row = at + j * CORES * tok + b * tok
            out[row : row + tok, :] = piece


def starts(p0, p1, size):
    half = PAD // CORES
    return jnp.concatenate([jnp.full((half, size), p[0].astype(F32), F32) for p in (p0, p1)], axis=0).astype(BF16)


def merge_kernel(p0, p1, own, q1, k1, v1, q_out, kv_out):
    tok = q1.shape[0]
    rows = PER * CORES * tok
    pos = starts(p0, p1, q_out.shape[1])
    place(own.at[0:tok, :], q1, q_out, 0)
    q_out[rows:, :] = pos
    place(own.at[tok : 2 * tok, :], k1, kv_out, 0)
    kv_out[rows : rows + PAD, :] = pos
    place(own.at[2 * tok : 3 * tok, :], v1, kv_out, rows + PAD, turned=True)


def score_kernel(same, q_ref, *refs):
    k_refs, (p_ref, top_ref) = refs[:-2], refs[-2:]
    size = q_ref.shape[1]
    tok = size
    both = CORES * tok
    half = PAD // CORES
    rate = size ** -0.5 * math.log2(math.e)
    at_or_before = lax.broadcasted_iota(jnp.int32, (tok, tok), 0) <= lax.broadcasted_iota(jnp.int32, (tok, tok), 1)

    def block_of(ref):
        first = ref[PER * both : PER * both + PAD, :].astype(F32)
        return [first[b * half : b * half + 1, :] for b in range(CORES)]

    q_block = jnp.concatenate(block_of(q_ref), axis=1)
    kept = [jnp.concatenate([p] * CORES, axis=1) <= q_block for ref in k_refs for p in block_of(ref)]
    for h in range(PER):
        q = q_ref[h * both : (h + 1) * both, :]
        scores = []
        for j, ref in enumerate(k_refs):
            s = nt_dot(ref[h * both : (h + 1) * both, :], q)
            for b in range(CORES):
                part = s[b * tok : (b + 1) * tok, :]
                if same and j == 0:
                    cols = [part[:, c * tok : (c + 1) * tok] for c in range(CORES)]
                    cols[b] = jnp.where(at_or_before, cols[b], LOW)
                    part = jnp.concatenate(cols, axis=1)
                scores.append(part)
        tops = [jnp.where(k, jnp.max(s, axis=0, keepdims=True), FLOOR) for k, s in zip(kept, scores)]
        top = jnp.maximum(functools.reduce(jnp.maximum, tops), FLOOR).astype(BF16).astype(F32)
        for i, (k, s) in enumerate(zip(kept, scores)):
            p_ref[h, i * tok : (i + 1) * tok, :] = jnp.exp2((s - jnp.where(k, top, -LOW)) * rate).astype(BF16)
        top_ref[h * 8 : (h + 1) * 8, :] = jnp.broadcast_to(top, (8, both))


def apply_kernel(wide, row, p_ref, top_ref, *refs):
    nv = len(refs) - (1 if wide else CORES)
    v_refs, out_refs = refs[:nv], refs[nv:]
    size = v_refs[0].shape[1]
    tok = size
    both = CORES * tok
    block = PER * size + PAD

    def store(b, at, value):
        if wide:
            out_refs[0][b * block + at : b * block + at + value.shape[0], :] = value
        else:
            out_refs[b][at : at + value.shape[0], :] = value

    stats = [[] for _ in range(CORES)]
    for h in range(PER):
        vals = []
        for ref in v_refs:
            for b in range(CORES):
                at = row + h * both + b * tok
                vals.append(ref[at : at + tok, :])
        vt = jnp.concatenate(vals, axis=1)
        vt = jnp.concatenate([vt, jnp.ones((PAD, vt.shape[1]), BF16)], axis=0)
        o = jnp.dot(vt, p_ref[h], preferred_element_type=F32)
        total = o[size : size + 1, :]
        hi = total.astype(BF16).astype(F32)
        top = top_ref[h * 8 : h * 8 + 1, :]
        for b in range(CORES):
            cols = slice(b * tok, (b + 1) * tok)
            store(b, h * size, o[0:size, cols].astype(BF16))
            stats[b] += [top[:, cols], hi[:, cols], (total - hi)[:, cols]]
    for b in range(CORES):
        rest = jnp.zeros((PAD - 3 * PER, tok), F32)
        store(b, PER * size, jnp.concatenate(stats[b] + [rest], axis=0).astype(BF16))


def joined(parts, stats, h, rate):
    size = parts[0].shape[0]
    tops = [s[3 * h : 3 * h + 1, :] for s in stats]
    best = functools.reduce(jnp.maximum, tops)
    factors = [jnp.exp2((t - best) * rate) for t in tops]
    total = sum(f * (s[3 * h + 1 : 3 * h + 2, :] + s[3 * h + 2 : 3 * h + 3, :]) for f, s in zip(factors, stats))
    numer = sum(f * part.astype(F32) for f, part in zip(factors, parts))
    return best, total, numer


def add_kernel(n, wide, *refs):
    size = refs[0].shape[1]
    block = PER * size + PAD
    rate = size ** -0.5 * math.log2(math.e)
    for b in range(CORES):
        base = b * block
        stats = [ref[base + PER * size : base + block, :].astype(F32) for ref in refs[:n]]
        out, at = (refs[n], base) if wide else (refs[n + b], 0)
        rows = []
        for h in range(PER):
            parts = [ref[base + h * size : base + (h + 1) * size, :] for ref in refs[:n]]
            best, total, numer = joined(parts, stats, h, rate)
            hi = total.astype(BF16).astype(F32)
            rows += [best, hi, total - hi]
            out[at + h * size : at + (h + 1) * size, :] = numer.astype(BF16)
        rest = jnp.zeros((PAD - 3 * PER, size), F32)
        out[at + PER * size : at + block, :] = jnp.concatenate(rows + [rest], axis=0).astype(BF16)


def combine_kernel(n, *refs):
    parts, out_ref = refs[:n], refs[n]
    size = parts[0].shape[1]
    rate = size ** -0.5 * math.log2(math.e)
    core = lax.rem(lax.axis_index("inner"), CORES)
    for x in range(CORES):
        mine = parts[x::CORES]
        pair = jnp.bitwise_xor(core, x)
        stats = [part[PER * size :, :].astype(F32) for part in mine]
        for h in range(PER):
            _, total, numer = joined([part[h * size : (h + 1) * size, :] for part in mine], stats, h, rate)
            cols = pl.ds(pl.multiple_of((pair * PER + h) * size, size), size)
            out_ref[:, cols] = (numer * (1.0 / total)).T.astype(BF16)


def vmem(n=1):
    return [pl.BlockSpec(memory_space=pltpu.VMEM)] * n


def shards(n_out, n_in, queries, keys, values, block_pos):
    tok, width = queries.shape
    size = width // HEADS
    chips = n_in // CORES
    both = CORES * tok
    params = pltpu.CompilerParams(vmem_limit_bytes=40 * 1024 * 1024)

    def along_inner(r, x):
        return [(w * CORES + c, (w ^ r) * CORES + (c ^ x)) for w in range(chips) for c in range(CORES)]

    def after(a, b):
        return lax.optimization_barrier((a, b))[0]

    with jax.named_scope("swap"):
        other = [lax.ppermute(a, "inner", along_inner(0, 1)) for a in (queries, keys, values, block_pos)]
        own = jnp.concatenate([queries, keys, values], axis=0)
    with jax.named_scope("merge"):
        smem = [pl.BlockSpec(memory_space=pltpu.SMEM)]
        q_piece, kv_piece = pl.pallas_call(
            merge_kernel,
            out_shape=(
                jax.ShapeDtypeStruct((PER * both + PAD, size), BF16),
                jax.ShapeDtypeStruct((2 * PER * both + PAD, size), BF16),
            ),
            in_specs=smem * 2 + vmem(4),
            out_specs=tuple(vmem(2)),
            compiler_params=params,
            name="merge",
        )(block_pos, other[3], own, *other[:3])
    half = PER * both + PAD
    block = PER * size + PAD

    def low(r):
        return r & -r

    def single(r):
        return r == low(r)

    def over(a, step):
        bits = n_out.bit_length() - 1
        flip = [1 << (step + c) % bits for c in range(CORES)]
        pairs = [
            (o * n_in + w * CORES + c, (o ^ flip[c]) * n_in + w * CORES + c)
            for o in range(n_out)
            for w in range(chips)
            for c in range(CORES)
        ]
        return lax.ppermute(a, ("outer", "inner"), pairs)

    with jax.named_scope("exchange"):
        kv = [kv_piece]
        for step in range(n_out.bit_length() - 1):
            kv += [over(a, step) for a in kv]
        q_by = {0: q_piece}
        for r in reversed(range(1, chips)):
            q_by[r] = lax.ppermute(q_piece, "inner", along_inner(r, 0))

    def shapes(wide):
        rows = CORES * block if wide else block
        return (jax.ShapeDtypeStruct((rows, tok), BF16),) * (1 if wide else CORES)

    work = 2 * PER * both * n_out * both * size

    def score(r, done):
        with jax.named_scope("score"):
            return pl.pallas_call(
                functools.partial(score_kernel, r == 0),
                out_shape=(
                    jax.ShapeDtypeStruct((PER, n_out * both, both), BF16),
                    jax.ShapeDtypeStruct((PER * 8, both), F32),
                ),
                in_specs=vmem(1 + n_out),
                out_specs=tuple(vmem(2)),
                compiler_params=params,
                cost_estimate=pl.CostEstimate(flops=work, bytes_accessed=2**20, transcendentals=work // (2 * size)),
                name="score",
            )(q_by[r] if done is None else after(q_by[r], done), *kv)

    def apply(r, wide):
        with jax.named_scope("apply"):
            return pl.pallas_call(
                functools.partial(apply_kernel, wide, half),
                out_shape=shapes(wide),
                in_specs=vmem(2 + n_out),
                out_specs=tuple(vmem(len(shapes(wide)))),
                compiler_params=params,
                cost_estimate=pl.CostEstimate(flops=work, bytes_accessed=2**20, transcendentals=0),
                name="apply",
            )(*weights_by[r], *kv)

    def add(arrays, wide):
        with jax.named_scope("add"):
            return pl.pallas_call(
                functools.partial(add_kernel, len(arrays), wide),
                out_shape=shapes(wide),
                in_specs=vmem(len(arrays)),
                out_specs=tuple(vmem(len(shapes(wide)))),
                compiler_params=params,
                name="add",
            )(*arrays)

    arrived = {r: [] for r in range(chips)}
    ends = []

    def send(r, parts):
        with jax.named_scope("return"):
            if single(r):
                ends.extend(lax.ppermute(parts[x], "inner", along_inner(r, x)) for x in range(CORES))
            else:
                arrived[r - low(r)].append(lax.ppermute(parts[0], "inner", along_inner(low(r), 0)))

    def both_kernels(r, done):
        weights_by[r] = score(r, done)
        partial[r] = apply(r, r > 1)
        return partial[r][0]

    done = None
    weights_by, partial = {}, {}
    for r in reversed(range(1, chips)):
        done = both_kernels(r, done)
    for r in reversed(range(1, chips)):
        parts = partial[r]
        if arrived[r]:
            parts = add([parts[0], *arrived[r]], not single(r))
            done = parts[0]
        if r == 1:
            parts = [parts[0], after(parts[1], done)]
        send(r, parts)
    both_kernels(0, done)
    with jax.named_scope("return"):
        ends = [partial[0][0], lax.ppermute(partial[0][1], "inner", along_inner(0, 1))] + ends
    with jax.named_scope("combine"):
        return pl.pallas_call(
            functools.partial(combine_kernel, len(ends)),
            out_shape=jax.ShapeDtypeStruct((tok, width), BF16),
            in_specs=vmem(len(ends)),
            out_specs=vmem()[0],
            compiler_params=params,
            name="combine",
        )(*ends)


def solution(mesh):
    n_out, n_in = mesh.shape["outer"], mesh.shape["inner"]
    return jax.shard_map(
        functools.partial(shards, n_out, n_in),
        mesh=mesh,
        in_specs=(
            P(("outer", "inner"), None),
            P(("outer", "inner"), None),
            P(("outer", "inner"), None),
            P(("outer", "inner")),
        ),
        out_specs=P(("outer", "inner"), None),
        check_vma=False,
    )
```

```python
import functools
import math

import jax
import jax.numpy as jnp
from jax import lax
from jax.experimental import pallas as pl
from jax.experimental.pallas import tpu as pltpu
from jax.sharding import PartitionSpec as P

HEADS = 4
CORES = 2
PER = HEADS // CORES
PAD = 16
LOW = -1e30
FLOOR = -1e29
BF16 = jnp.bfloat16
F32 = jnp.float32


def nt_dot(a, b):
    return lax.dot_general(a, b, (((1,), (1,)), ((), ())), preferred_element_type=F32)


def place(own, other, out, at, turned=False):
    tok = own.shape[0]
    size = own.shape[1] // HEADS
    core = lax.rem(lax.axis_index("inner"), CORES)
    for b, ref in enumerate((own, other)):
        for j in range(PER):
            piece = ref[:, pl.ds(pl.multiple_of((core * PER + j) * size, size), size)]
            if turned:
                piece = piece.astype(F32).T.astype(BF16)
            row = at + j * CORES * tok + b * tok
            out[row : row + tok, :] = piece


def starts(p0, p1, size):
    half = PAD // CORES
    return jnp.concatenate([jnp.full((half, size), p[0].astype(F32), F32) for p in (p0, p1)], axis=0).astype(BF16)


def merge_kernel(p0, p1, own, q1, k1, v1, q_out, kv_out):
    tok = q1.shape[0]
    rows = PER * CORES * tok
    pos = starts(p0, p1, q_out.shape[1])
    place(own.at[0:tok, :], q1, q_out, 0)
    q_out[rows:, :] = pos
    place(own.at[tok : 2 * tok, :], k1, kv_out, 0)
    kv_out[rows : rows + PAD, :] = pos
    place(own.at[2 * tok : 3 * tok, :], v1, kv_out, rows + PAD, turned=True)


def score_kernel(same, q_ref, *refs):
    k_refs, (p_ref, top_ref) = refs[:-2], refs[-2:]
    size = q_ref.shape[1]
    tok = size
    both = CORES * tok
    half = PAD // CORES
    rate = size ** -0.5 * math.log2(math.e)
    at_or_before = lax.broadcasted_iota(jnp.int32, (tok, tok), 0) <= lax.broadcasted_iota(jnp.int32, (tok, tok), 1)

    def block_of(ref):
        first = ref[PER * both : PER * both + PAD, :].astype(F32)
        return [first[b * half : b * half + 1, :] for b in range(CORES)]

    q_block = jnp.concatenate(block_of(q_ref), axis=1)
    kept = [jnp.concatenate([p] * CORES, axis=1) <= q_block for ref in k_refs for p in block_of(ref)]
    for h in range(PER):
        q = q_ref[h * both : (h + 1) * both, :]
        scores = []
        for j, ref in enumerate(k_refs):
            s = nt_dot(ref[h * both : (h + 1) * both, :], q)
            for b in range(CORES):
                part = s[b * tok : (b + 1) * tok, :]
                if same and j == 0:
                    cols = [part[:, c * tok : (c + 1) * tok] for c in range(CORES)]
                    cols[b] = jnp.where(at_or_before, cols[b], LOW)
                    part = jnp.concatenate(cols, axis=1)
                scores.append(part)
        tops = [jnp.where(k, jnp.max(s, axis=0, keepdims=True), FLOOR) for k, s in zip(kept, scores)]
        top = jnp.maximum(functools.reduce(jnp.maximum, tops), FLOOR).astype(BF16).astype(F32)
        for i, (k, s) in enumerate(zip(kept, scores)):
            p_ref[h, i * tok : (i + 1) * tok, :] = jnp.exp2((s - jnp.where(k, top, -LOW)) * rate).astype(BF16)
        top_ref[h * 8 : (h + 1) * 8, :] = jnp.broadcast_to(top, (8, both))


def apply_kernel(wide, rows, p_ref, top_ref, *refs):
    nv = len(refs) - (1 if wide else CORES)
    v_refs, out_refs = refs[:nv], refs[nv:]
    size = v_refs[0].shape[1]
    tok = size
    both = CORES * tok
    block = PER * size + PAD

    def store(b, at, value):
        if wide:
            out_refs[0][b * block + at : b * block + at + value.shape[0], :] = value
        else:
            out_refs[b][at : at + value.shape[0], :] = value

    stats = [[] for _ in range(CORES)]
    for h in range(PER):
        vals = []
        for ref, row in zip(v_refs, rows):
            for b in range(CORES):
                at = row + h * both + b * tok
                vals.append(ref[at : at + tok, :])
        vt = jnp.concatenate(vals, axis=1)
        vt = jnp.concatenate([vt, jnp.ones((PAD, vt.shape[1]), BF16)], axis=0)
        o = jnp.dot(vt, p_ref[h], preferred_element_type=F32)
        total = o[size : size + 1, :]
        hi = total.astype(BF16).astype(F32)
        top = top_ref[h * 8 : h * 8 + 1, :]
        for b in range(CORES):
            cols = slice(b * tok, (b + 1) * tok)
            store(b, h * size, o[0:size, cols].astype(BF16))
            stats[b] += [top[:, cols], hi[:, cols], (total - hi)[:, cols]]
    for b in range(CORES):
        rest = jnp.zeros((PAD - 3 * PER, tok), F32)
        store(b, PER * size, jnp.concatenate(stats[b] + [rest], axis=0).astype(BF16))


def joined(parts, stats, h, rate):
    size = parts[0].shape[0]
    tops = [s[3 * h : 3 * h + 1, :] for s in stats]
    best = functools.reduce(jnp.maximum, tops)
    factors = [jnp.exp2((t - best) * rate) for t in tops]
    total = sum(f * (s[3 * h + 1 : 3 * h + 2, :] + s[3 * h + 2 : 3 * h + 3, :]) for f, s in zip(factors, stats))
    numer = sum(f * part.astype(F32) for f, part in zip(factors, parts))
    return best, total, numer


def add_kernel(n, wide, *refs):
    size = refs[0].shape[1]
    block = PER * size + PAD
    rate = size ** -0.5 * math.log2(math.e)
    for b in range(CORES):
        base = b * block
        stats = [ref[base + PER * size : base + block, :].astype(F32) for ref in refs[:n]]
        out, at = (refs[n], base) if wide else (refs[n + b], 0)
        rows = []
        for h in range(PER):
            parts = [ref[base + h * size : base + (h + 1) * size, :] for ref in refs[:n]]
            best, total, numer = joined(parts, stats, h, rate)
            hi = total.astype(BF16).astype(F32)
            rows += [best, hi, total - hi]
            out[at + h * size : at + (h + 1) * size, :] = numer.astype(BF16)
        rest = jnp.zeros((PAD - 3 * PER, size), F32)
        out[at + PER * size : at + block, :] = jnp.concatenate(rows + [rest], axis=0).astype(BF16)


def combine_kernel(n, *refs):
    parts, out_ref = refs[:n], refs[n]
    size = parts[0].shape[1]
    rate = size ** -0.5 * math.log2(math.e)
    core = lax.rem(lax.axis_index("inner"), CORES)
    for x in range(CORES):
        mine = parts[x::CORES]
        pair = jnp.bitwise_xor(core, x)
        stats = [part[PER * size :, :].astype(F32) for part in mine]
        for h in range(PER):
            _, total, numer = joined([part[h * size : (h + 1) * size, :] for part in mine], stats, h, rate)
            cols = pl.ds(pl.multiple_of((pair * PER + h) * size, size), size)
            out_ref[:, cols] = (numer * (1.0 / total)).T.astype(BF16)


def vmem(n=1):
    return [pl.BlockSpec(memory_space=pltpu.VMEM)] * n


def shards(n_out, n_in, queries, keys, values, block_pos):
    tok, width = queries.shape
    size = width // HEADS
    chips = n_in // CORES
    both = CORES * tok
    params = pltpu.CompilerParams(vmem_limit_bytes=40 * 1024 * 1024)

    def along_inner(r, x):
        return [(w * CORES + c, (w ^ r) * CORES + (c ^ x)) for w in range(chips) for c in range(CORES)]

    def after(a, b):
        return lax.optimization_barrier((a, b))[0]

    with jax.named_scope("swap"):
        other = [lax.ppermute(a, "inner", along_inner(0, 1)) for a in (queries, keys, values, block_pos)]
        own = jnp.concatenate([queries, keys, values], axis=0)
    with jax.named_scope("merge"):
        smem = [pl.BlockSpec(memory_space=pltpu.SMEM)]
        q_piece, kv_piece = pl.pallas_call(
            merge_kernel,
            out_shape=(
                jax.ShapeDtypeStruct((PER * both + PAD, size), BF16),
                jax.ShapeDtypeStruct((2 * PER * both + PAD, size), BF16),
            ),
            in_specs=smem * 2 + vmem(4),
            out_specs=tuple(vmem(2)),
            compiler_params=params,
            name="merge",
        )(block_pos, other[3], own, *other[:3])
    half = PER * both + PAD
    block = PER * size + PAD

    def low(r):
        return r & -r

    def high(r):
        return 1 << (r.bit_length() - 1)

    def single(r):
        return r == low(r)

    def over(a, r):
        return lax.ppermute(a, "outer", [(o, o ^ r) for o in range(n_out)])

    with jax.named_scope("exchange"):
        whole = {r: over(kv_piece, r) if r else kv_piece for r in range(n_out) if single(r)}
        q_by = {0: q_piece}
        for r in reversed(range(1, chips)):
            q_by[r] = lax.ppermute(q_piece, "inner", along_inner(r, 0))
        k_by = {r: a[:half, :] for r, a in whole.items() if r}
        v_by = {r: a[half:, :] for r, a in whole.items() if r}
        for r in range(1, n_out):
            if not single(r):
                k_by[r] = over(k_by[r - high(r)], high(r))
        for r in sorted(range(1, n_out), key=lambda r: r.bit_count()):
            if not single(r):
                v_by[r] = over(v_by[r - low(r)], low(r))
        ks = [whole[r] if r in whole else k_by[r] for r in range(n_out)]
        vs = [whole[r] if r in whole else v_by[r] for r in range(n_out)]
        rows = tuple(half if r in whole else 0 for r in range(n_out))

    def shapes(wide):
        rows = CORES * block if wide else block
        return (jax.ShapeDtypeStruct((rows, tok), BF16),) * (1 if wide else CORES)

    work = 2 * PER * both * n_out * both * size

    def score(r, done):
        with jax.named_scope("score"):
            return pl.pallas_call(
                functools.partial(score_kernel, r == 0),
                out_shape=(
                    jax.ShapeDtypeStruct((PER, n_out * both, both), BF16),
                    jax.ShapeDtypeStruct((PER * 8, both), F32),
                ),
                in_specs=vmem(1 + n_out),
                out_specs=tuple(vmem(2)),
                compiler_params=params,
                cost_estimate=pl.CostEstimate(flops=work, bytes_accessed=2**20, transcendentals=work // (2 * size)),
                name="score",
            )(q_by[r] if done is None else after(q_by[r], done), *ks)

    def apply(r, wide):
        with jax.named_scope("apply"):
            return pl.pallas_call(
                functools.partial(apply_kernel, wide, rows),
                out_shape=shapes(wide),
                in_specs=vmem(2 + n_out),
                out_specs=tuple(vmem(len(shapes(wide)))),
                compiler_params=params,
                cost_estimate=pl.CostEstimate(flops=work, bytes_accessed=2**20, transcendentals=0),
                name="apply",
            )(*weights_by[r], *vs)

    def add(arrays, wide):
        with jax.named_scope("add"):
            return pl.pallas_call(
                functools.partial(add_kernel, len(arrays), wide),
                out_shape=shapes(wide),
                in_specs=vmem(len(arrays)),
                out_specs=tuple(vmem(len(shapes(wide)))),
                compiler_params=params,
                name="add",
            )(*arrays)

    arrived = {r: [] for r in range(chips)}
    ends = []

    def send(r, parts):
        with jax.named_scope("return"):
            if single(r):
                ends.extend(lax.ppermute(parts[x], "inner", along_inner(r, x)) for x in range(CORES))
            else:
                arrived[r - low(r)].append(lax.ppermute(parts[0], "inner", along_inner(low(r), 0)))

    def both_kernels(r, done):
        weights_by[r] = score(r, done)
        partial[r] = apply(r, r > 1)
        return partial[r][0]

    done = None
    weights_by, partial = {}, {}
    for r in reversed(range(1, chips)):
        done = both_kernels(r, done)
    for r in reversed(range(1, chips)):
        parts = partial[r]
        if arrived[r]:
            parts = add([parts[0], *arrived[r]], not single(r))
            done = parts[0]
        if r == 1:
            parts = [parts[0], after(parts[1], done)]
        send(r, parts)
    both_kernels(0, done)
    with jax.named_scope("return"):
        ends = [partial[0][0], lax.ppermute(partial[0][1], "inner", along_inner(0, 1))] + ends
    with jax.named_scope("combine"):
        return pl.pallas_call(
            functools.partial(combine_kernel, len(ends)),
            out_shape=jax.ShapeDtypeStruct((tok, width), BF16),
            in_specs=vmem(len(ends)),
            out_specs=vmem()[0],
            compiler_params=params,
            name="combine",
        )(*ends)


def solution(mesh):
    n_out, n_in = mesh.shape["outer"], mesh.shape["inner"]
    return jax.shard_map(
        functools.partial(shards, n_out, n_in),
        mesh=mesh,
        in_specs=(
            P(("outer", "inner"), None),
            P(("outer", "inner"), None),
            P(("outer", "inner"), None),
            P(("outer", "inner")),
        ),
        out_specs=P(("outer", "inner"), None),
        check_vma=False,
    )
```

```python
import functools
import math

import jax
import jax.numpy as jnp
from jax import lax
from jax.experimental import pallas as pl
from jax.experimental.pallas import tpu as pltpu
from jax.sharding import PartitionSpec as P

HEADS = 4
CORES = 2
PER = HEADS // CORES
PAD = 16
LOW = -1e30
FLOOR = -1e29
BF16 = jnp.bfloat16
F32 = jnp.float32


def nt_dot(a, b):
    return lax.dot_general(a, b, (((1,), (1,)), ((), ())), preferred_element_type=F32)


def place(own, other, out, at, turned=False):
    tok = own.shape[0]
    size = own.shape[1] // HEADS
    core = lax.rem(lax.axis_index("inner"), CORES)
    for b, ref in enumerate((own, other)):
        for j in range(PER):
            piece = ref[:, pl.ds(pl.multiple_of((core * PER + j) * size, size), size)]
            if turned:
                piece = piece.astype(F32).T.astype(BF16)
            row = at + j * CORES * tok + b * tok
            out[row : row + tok, :] = piece


def starts(p0, p1, size):
    half = PAD // CORES
    return jnp.concatenate([jnp.full((half, size), p[0].astype(F32), F32) for p in (p0, p1)], axis=0).astype(BF16)


def merge_kernel(p0, p1, own, q1, k1, v1, q_out, kv_out):
    tok = q1.shape[0]
    rows = PER * CORES * tok
    pos = starts(p0, p1, q_out.shape[1])
    place(own.at[0:tok, :], q1, q_out, 0)
    q_out[rows:, :] = pos
    place(own.at[tok : 2 * tok, :], k1, kv_out, 0)
    kv_out[rows : rows + PAD, :] = pos
    place(own.at[2 * tok : 3 * tok, :], v1, kv_out, rows + PAD, turned=True)


def score_kernel(same, q_ref, *refs):
    k_refs, (p_ref, top_ref) = refs[:-2], refs[-2:]
    size = q_ref.shape[1]
    tok = size
    both = CORES * tok
    half = PAD // CORES
    rate = size ** -0.5 * math.log2(math.e)
    at_or_before = lax.broadcasted_iota(jnp.int32, (tok, tok), 0) <= lax.broadcasted_iota(jnp.int32, (tok, tok), 1)

    def block_of(ref):
        first = ref[PER * both : PER * both + PAD, :].astype(F32)
        return [first[b * half : b * half + 1, :] for b in range(CORES)]

    q_block = jnp.concatenate(block_of(q_ref), axis=1)
    kept = [jnp.concatenate([p] * CORES, axis=1) <= q_block for ref in k_refs for p in block_of(ref)]
    for h in range(PER):
        q = q_ref[h * both : (h + 1) * both, :]
        scores = []
        for j, ref in enumerate(k_refs):
            s = nt_dot(ref[h * both : (h + 1) * both, :], q)
            for b in range(CORES):
                part = s[b * tok : (b + 1) * tok, :]
                if same and j == 0:
                    cols = [part[:, c * tok : (c + 1) * tok] for c in range(CORES)]
                    cols[b] = jnp.where(at_or_before, cols[b], LOW)
                    part = jnp.concatenate(cols, axis=1)
                scores.append(part)
        tops = [jnp.where(k, jnp.max(s, axis=0, keepdims=True), FLOOR) for k, s in zip(kept, scores)]
        top = jnp.maximum(functools.reduce(jnp.maximum, tops), FLOOR).astype(BF16).astype(F32)
        for i, (k, s) in enumerate(zip(kept, scores)):
            p_ref[h, i * tok : (i + 1) * tok, :] = jnp.exp2((s - jnp.where(k, top, -LOW)) * rate).astype(BF16)
        top_ref[h * 8 : (h + 1) * 8, :] = jnp.broadcast_to(top, (8, both))


def apply_kernel(wide, rows, p_ref, top_ref, *refs):
    nv = len(refs) - (1 if wide else CORES)
    v_refs, out_refs = refs[:nv], refs[nv:]
    size = v_refs[0].shape[1]
    tok = size
    both = CORES * tok
    block = PER * size + PAD

    def store(b, at, value):
        if wide:
            out_refs[0][b * block + at : b * block + at + value.shape[0], :] = value
        else:
            out_refs[b][at : at + value.shape[0], :] = value

    stats = [[] for _ in range(CORES)]
    for h in range(PER):
        vals = []
        for ref, row in zip(v_refs, rows):
            for b in range(CORES):
                at = row + h * both + b * tok
                vals.append(ref[at : at + tok, :])
        vt = jnp.concatenate(vals, axis=1)
        vt = jnp.concatenate([vt, jnp.ones((PAD, vt.shape[1]), BF16)], axis=0)
        o = jnp.dot(vt, p_ref[h], preferred_element_type=F32)
        total = o[size : size + 1, :]
        hi = total.astype(BF16).astype(F32)
        top = top_ref[h * 8 : h * 8 + 1, :]
        for b in range(CORES):
            cols = slice(b * tok, (b + 1) * tok)
            store(b, h * size, o[0:size, cols].astype(BF16))
            stats[b] += [top[:, cols], hi[:, cols], (total - hi)[:, cols]]
    for b in range(CORES):
        rest = jnp.zeros((PAD - 3 * PER, tok), F32)
        store(b, PER * size, jnp.concatenate(stats[b] + [rest], axis=0).astype(BF16))


def joined(parts, stats, h, rate):
    size = parts[0].shape[0]
    tops = [s[3 * h : 3 * h + 1, :] for s in stats]
    best = functools.reduce(jnp.maximum, tops)
    factors = [jnp.exp2((t - best) * rate) for t in tops]
    total = sum(f * (s[3 * h + 1 : 3 * h + 2, :] + s[3 * h + 2 : 3 * h + 3, :]) for f, s in zip(factors, stats))
    numer = sum(f * part.astype(F32) for f, part in zip(factors, parts))
    return best, total, numer


def add_kernel(n, wide, *refs):
    size = refs[0].shape[1]
    block = PER * size + PAD
    rate = size ** -0.5 * math.log2(math.e)
    for b in range(CORES):
        base = b * block
        stats = [ref[base + PER * size : base + block, :].astype(F32) for ref in refs[:n]]
        out, at = (refs[n], base) if wide else (refs[n + b], 0)
        rows = []
        for h in range(PER):
            parts = [ref[base + h * size : base + (h + 1) * size, :] for ref in refs[:n]]
            best, total, numer = joined(parts, stats, h, rate)
            hi = total.astype(BF16).astype(F32)
            rows += [best, hi, total - hi]
            out[at + h * size : at + (h + 1) * size, :] = numer.astype(BF16)
        rest = jnp.zeros((PAD - 3 * PER, size), F32)
        out[at + PER * size : at + block, :] = jnp.concatenate(rows + [rest], axis=0).astype(BF16)


def combine_kernel(n, *refs):
    parts, out_ref = refs[:n], refs[n]
    size = parts[0].shape[1]
    rate = size ** -0.5 * math.log2(math.e)
    core = lax.rem(lax.axis_index("inner"), CORES)
    for x in range(CORES):
        mine = parts[x::CORES]
        pair = jnp.bitwise_xor(core, x)
        stats = [part[PER * size :, :].astype(F32) for part in mine]
        for h in range(PER):
            _, total, numer = joined([part[h * size : (h + 1) * size, :] for part in mine], stats, h, rate)
            cols = pl.ds(pl.multiple_of((pair * PER + h) * size, size), size)
            out_ref[:, cols] = (numer * (1.0 / total)).T.astype(BF16)


def vmem(n=1):
    return [pl.BlockSpec(memory_space=pltpu.VMEM)] * n


def shards(n_out, n_in, queries, keys, values, block_pos):
    tok, width = queries.shape
    size = width // HEADS
    chips = n_in // CORES
    both = CORES * tok
    params = pltpu.CompilerParams(vmem_limit_bytes=40 * 1024 * 1024)

    def along_inner(r, x):
        return [(w * CORES + c, (w ^ r) * CORES + (c ^ x)) for w in range(chips) for c in range(CORES)]

    def after(a, b):
        return lax.optimization_barrier((a, b))[0]

    with jax.named_scope("swap"):
        other = [lax.ppermute(a, "inner", along_inner(0, 1)) for a in (queries, keys, values, block_pos)]
        own = jnp.concatenate([queries, keys, values], axis=0)
    with jax.named_scope("merge"):
        smem = [pl.BlockSpec(memory_space=pltpu.SMEM)]
        q_piece, kv_piece = pl.pallas_call(
            merge_kernel,
            out_shape=(
                jax.ShapeDtypeStruct((PER * both + PAD, size), BF16),
                jax.ShapeDtypeStruct((2 * PER * both + PAD, size), BF16),
            ),
            in_specs=smem * 2 + vmem(4),
            out_specs=tuple(vmem(2)),
            compiler_params=params,
            name="merge",
        )(block_pos, other[3], own, *other[:3])
    half = PER * both + PAD
    block = PER * size + PAD

    def low(r):
        return r & -r

    def high(r):
        return 1 << (r.bit_length() - 1)

    def single(r):
        return r == low(r)

    def over(a, r):
        return lax.ppermute(a, "outer", [(o, o ^ r) for o in range(n_out)])

    with jax.named_scope("exchange"):
        whole = {r: over(kv_piece, r) if r else kv_piece for r in range(n_out) if single(r)}
        q_by = {0: q_piece}
        for r in reversed(range(1, chips)):
            q_by[r] = lax.ppermute(q_piece, "inner", along_inner(r, 0))
        k_by = {r: a[:half, :] for r, a in whole.items() if r}
        v_by = {r: a[half:, :] for r, a in whole.items() if r}
        for r in range(1, n_out):
            if not single(r):
                k_by[r] = over(k_by[r - high(r)], high(r))
        for r in sorted(range(1, n_out), key=lambda r: r.bit_count()):
            if not single(r):
                v = v_by[r - low(r)]
                v_by[r] = over(after(v, q_by[1]) if chips > 1 else v, low(r))
        ks = [whole[r] if r in whole else k_by[r] for r in range(n_out)]
        vs = [whole[r] if r in whole else v_by[r] for r in range(n_out)]
        rows = tuple(half if r in whole else 0 for r in range(n_out))

    def shapes(wide):
        rows = CORES * block if wide else block
        return (jax.ShapeDtypeStruct((rows, tok), BF16),) * (1 if wide else CORES)

    work = 2 * PER * both * n_out * both * size

    def score(r, done):
        with jax.named_scope("score"):
            return pl.pallas_call(
                functools.partial(score_kernel, r == 0),
                out_shape=(
                    jax.ShapeDtypeStruct((PER, n_out * both, both), BF16),
                    jax.ShapeDtypeStruct((PER * 8, both), F32),
                ),
                in_specs=vmem(1 + n_out),
                out_specs=tuple(vmem(2)),
                compiler_params=params,
                cost_estimate=pl.CostEstimate(flops=work, bytes_accessed=2**20, transcendentals=work // (2 * size)),
                name="score",
            )(q_by[r] if done is None else after(q_by[r], done), *ks)

    def apply(r, wide):
        with jax.named_scope("apply"):
            return pl.pallas_call(
                functools.partial(apply_kernel, wide, rows),
                out_shape=shapes(wide),
                in_specs=vmem(2 + n_out),
                out_specs=tuple(vmem(len(shapes(wide)))),
                compiler_params=params,
                cost_estimate=pl.CostEstimate(flops=work, bytes_accessed=2**20, transcendentals=0),
                name="apply",
            )(*weights_by[r], *vs)

    def add(arrays, wide):
        with jax.named_scope("add"):
            return pl.pallas_call(
                functools.partial(add_kernel, len(arrays), wide),
                out_shape=shapes(wide),
                in_specs=vmem(len(arrays)),
                out_specs=tuple(vmem(len(shapes(wide)))),
                compiler_params=params,
                name="add",
            )(*arrays)

    arrived = {r: [] for r in range(chips)}
    ends = []

    def send(r, parts):
        with jax.named_scope("return"):
            if single(r):
                ends.extend(lax.ppermute(parts[x], "inner", along_inner(r, x)) for x in range(CORES))
            else:
                arrived[r - low(r)].append(lax.ppermute(parts[0], "inner", along_inner(low(r), 0)))

    def both_kernels(r, done):
        weights_by[r] = score(r, done)
        partial[r] = apply(r, r > 1)
        return partial[r][0]

    done = None
    weights_by, partial = {}, {}
    for r in reversed(range(1, chips)):
        done = both_kernels(r, done)
    for r in reversed(range(1, chips)):
        parts = partial[r]
        if arrived[r]:
            parts = add([parts[0], *arrived[r]], not single(r))
            done = parts[0]
        if r == 1:
            parts = [parts[0], after(parts[1], done)]
        send(r, parts)
    both_kernels(0, done)
    with jax.named_scope("return"):
        ends = [partial[0][0], lax.ppermute(partial[0][1], "inner", along_inner(0, 1))] + ends
    with jax.named_scope("combine"):
        return pl.pallas_call(
            functools.partial(combine_kernel, len(ends)),
            out_shape=jax.ShapeDtypeStruct((tok, width), BF16),
            in_specs=vmem(len(ends)),
            out_specs=vmem()[0],
            compiler_params=params,
            name="combine",
        )(*ends)


def solution(mesh):
    n_out, n_in = mesh.shape["outer"], mesh.shape["inner"]
    return jax.shard_map(
        functools.partial(shards, n_out, n_in),
        mesh=mesh,
        in_specs=(
            P(("outer", "inner"), None),
            P(("outer", "inner"), None),
            P(("outer", "inner"), None),
            P(("outer", "inner")),
        ),
        out_specs=P(("outer", "inner"), None),
        check_vma=False,
    )
```

```python
import functools
import math

import jax
import jax.numpy as jnp
from jax import lax
from jax.experimental import pallas as pl
from jax.experimental.pallas import tpu as pltpu
from jax.sharding import PartitionSpec as P

HEADS = 4
CORES = 2
PER = HEADS // CORES
PAD = 16
LOW = -1e30
FLOOR = -1e29
BF16 = jnp.bfloat16
F32 = jnp.float32


def nt_dot(a, b):
    return lax.dot_general(a, b, (((1,), (1,)), ((), ())), preferred_element_type=F32)


def place(own, other, out, at, turned=False):
    tok = own.shape[0]
    size = own.shape[1] // HEADS
    core = lax.rem(lax.axis_index("inner"), CORES)
    for b, ref in enumerate((own, other)):
        for j in range(PER):
            piece = ref[:, pl.ds(pl.multiple_of((core * PER + j) * size, size), size)]
            if turned:
                piece = piece.astype(F32).T.astype(BF16)
            row = at + j * CORES * tok + b * tok
            out[row : row + tok, :] = piece


def starts(p0, p1, size):
    half = PAD // CORES
    return jnp.concatenate([jnp.full((half, size), p[0].astype(F32), F32) for p in (p0, p1)], axis=0).astype(BF16)


def merge_kernel(p0, p1, own, q1, k1, v1, q_out, kv_out):
    tok = q1.shape[0]
    rows = PER * CORES * tok
    pos = starts(p0, p1, q_out.shape[1])
    place(own.at[0:tok, :], q1, q_out, 0)
    q_out[rows:, :] = pos
    place(own.at[tok : 2 * tok, :], k1, kv_out, 0)
    kv_out[rows : rows + PAD, :] = pos
    place(own.at[2 * tok : 3 * tok, :], v1, kv_out, rows + PAD, turned=True)


def score_kernel(same, q_ref, *refs):
    k_refs, (p_ref, top_ref) = refs[:-2], refs[-2:]
    size = q_ref.shape[1]
    tok = size
    both = CORES * tok
    half = PAD // CORES
    rate = size ** -0.5 * math.log2(math.e)
    at_or_before = lax.broadcasted_iota(jnp.int32, (tok, tok), 0) <= lax.broadcasted_iota(jnp.int32, (tok, tok), 1)

    def block_of(ref):
        first = ref[PER * both : PER * both + PAD, :].astype(F32)
        return [first[b * half : b * half + 1, :] for b in range(CORES)]

    q_block = jnp.concatenate(block_of(q_ref), axis=1)
    kept = [jnp.concatenate([p] * CORES, axis=1) <= q_block for ref in k_refs for p in block_of(ref)]
    for h in range(PER):
        q = q_ref[h * both : (h + 1) * both, :]
        scores = []
        for j, ref in enumerate(k_refs):
            s = nt_dot(ref[h * both : (h + 1) * both, :], q)
            for b in range(CORES):
                part = s[b * tok : (b + 1) * tok, :]
                if same and j == 0:
                    cols = [part[:, c * tok : (c + 1) * tok] for c in range(CORES)]
                    cols[b] = jnp.where(at_or_before, cols[b], LOW)
                    part = jnp.concatenate(cols, axis=1)
                scores.append(part)
        tops = [jnp.where(k, jnp.max(s, axis=0, keepdims=True), FLOOR) for k, s in zip(kept, scores)]
        top = jnp.maximum(functools.reduce(jnp.maximum, tops), FLOOR).astype(BF16).astype(F32)
        for i, (k, s) in enumerate(zip(kept, scores)):
            p_ref[h, i * tok : (i + 1) * tok, :] = jnp.exp2((s - jnp.where(k, top, -LOW)) * rate).astype(BF16)
        top_ref[h * 8 : (h + 1) * 8, :] = jnp.broadcast_to(top, (8, both))


def apply_kernel(wide, rows, p_ref, top_ref, *refs):
    nv = len(refs) - (1 if wide else CORES)
    v_refs, out_refs = refs[:nv], refs[nv:]
    size = v_refs[0].shape[1]
    tok = size
    both = CORES * tok
    block = PER * size + PAD

    def store(b, at, value):
        if wide:
            out_refs[0][b * block + at : b * block + at + value.shape[0], :] = value
        else:
            out_refs[b][at : at + value.shape[0], :] = value

    stats = [[] for _ in range(CORES)]
    for h in range(PER):
        vals = []
        for ref, row in zip(v_refs, rows):
            for b in range(CORES):
                at = row + h * both + b * tok
                vals.append(ref[at : at + tok, :])
        vt = jnp.concatenate(vals, axis=1)
        vt = jnp.concatenate([vt, jnp.ones((PAD, vt.shape[1]), BF16)], axis=0)
        o = jnp.dot(vt, p_ref[h], preferred_element_type=F32)
        total = o[size : size + 1, :]
        hi = total.astype(BF16).astype(F32)
        top = top_ref[h * 8 : h * 8 + 1, :]
        for b in range(CORES):
            cols = slice(b * tok, (b + 1) * tok)
            store(b, h * size, o[0:size, cols].astype(BF16))
            stats[b] += [top[:, cols], hi[:, cols], (total - hi)[:, cols]]
    for b in range(CORES):
        rest = jnp.zeros((PAD - 3 * PER, tok), F32)
        store(b, PER * size, jnp.concatenate(stats[b] + [rest], axis=0).astype(BF16))


def joined(parts, stats, h, rate):
    size = parts[0].shape[0]
    tops = [s[3 * h : 3 * h + 1, :] for s in stats]
    best = functools.reduce(jnp.maximum, tops)
    factors = [jnp.exp2((t - best) * rate) for t in tops]
    total = sum(f * (s[3 * h + 1 : 3 * h + 2, :] + s[3 * h + 2 : 3 * h + 3, :]) for f, s in zip(factors, stats))
    numer = sum(f * part.astype(F32) for f, part in zip(factors, parts))
    return best, total, numer


def add_kernel(n, wide, *refs):
    size = refs[0].shape[1]
    block = PER * size + PAD
    rate = size ** -0.5 * math.log2(math.e)
    for b in range(CORES):
        base = b * block
        stats = [ref[base + PER * size : base + block, :].astype(F32) for ref in refs[:n]]
        out, at = (refs[n], base) if wide else (refs[n + b], 0)
        rows = []
        for h in range(PER):
            parts = [ref[base + h * size : base + (h + 1) * size, :] for ref in refs[:n]]
            best, total, numer = joined(parts, stats, h, rate)
            hi = total.astype(BF16).astype(F32)
            rows += [best, hi, total - hi]
            out[at + h * size : at + (h + 1) * size, :] = numer.astype(BF16)
        rest = jnp.zeros((PAD - 3 * PER, size), F32)
        out[at + PER * size : at + block, :] = jnp.concatenate(rows + [rest], axis=0).astype(BF16)


def combine_kernel(n, *refs):
    parts, out_ref = refs[:n], refs[n]
    size = parts[0].shape[1]
    rate = size ** -0.5 * math.log2(math.e)
    core = lax.rem(lax.axis_index("inner"), CORES)
    for x in range(CORES):
        mine = parts[x::CORES]
        pair = jnp.bitwise_xor(core, x)
        stats = [part[PER * size :, :].astype(F32) for part in mine]
        for h in range(PER):
            _, total, numer = joined([part[h * size : (h + 1) * size, :] for part in mine], stats, h, rate)
            cols = pl.ds(pl.multiple_of((pair * PER + h) * size, size), size)
            out_ref[:, cols] = (numer * (1.0 / total)).T.astype(BF16)


def vmem(n=1):
    return [pl.BlockSpec(memory_space=pltpu.VMEM)] * n


def shards(n_out, n_in, queries, keys, values, block_pos):
    tok, width = queries.shape
    size = width // HEADS
    chips = n_in // CORES
    both = CORES * tok
    params = pltpu.CompilerParams(vmem_limit_bytes=40 * 1024 * 1024)

    def along_inner(r, x):
        return [(w * CORES + c, (w ^ r) * CORES + (c ^ x)) for w in range(chips) for c in range(CORES)]

    def after(a, b):
        return lax.optimization_barrier((a, b))[0]

    with jax.named_scope("swap"):
        other = [lax.ppermute(a, "inner", along_inner(0, 1)) for a in (queries, keys, values, block_pos)]
        own = jnp.concatenate([queries, keys, values], axis=0)
    with jax.named_scope("merge"):
        smem = [pl.BlockSpec(memory_space=pltpu.SMEM)]
        q_piece, kv_piece = pl.pallas_call(
            merge_kernel,
            out_shape=(
                jax.ShapeDtypeStruct((PER * both + PAD, size), BF16),
                jax.ShapeDtypeStruct((2 * PER * both + PAD, size), BF16),
            ),
            in_specs=smem * 2 + vmem(4),
            out_specs=tuple(vmem(2)),
            compiler_params=params,
            name="merge",
        )(block_pos, other[3], own, *other[:3])
    half = PER * both + PAD
    block = PER * size + PAD

    def low(r):
        return r & -r

    def high(r):
        return 1 << (r.bit_length() - 1)

    def single(r):
        return r == low(r)

    def over(a, r):
        return lax.ppermute(a, "outer", [(o, o ^ r) for o in range(n_out)])

    with jax.named_scope("exchange"):
        whole = {r: over(kv_piece, r) if r else kv_piece for r in range(n_out) if single(r)}
        q_by = {0: q_piece}
        for r in reversed(range(1, chips)):
            q_by[r] = lax.ppermute(q_piece, "inner", along_inner(r, 0))
        k_by = {r: a[:half, :] for r, a in whole.items() if r}
        v_by = {r: a[half:, :] for r, a in whole.items() if r}
        for r in range(1, n_out):
            if not single(r):
                k_by[r] = over(k_by[r - high(r)], high(r))
        for r in sorted(range(1, n_out), key=lambda r: r.bit_count()):
            if not single(r):
                v = v_by[r - low(r)]
                v_by[r] = over(after(v, q_by[1]) if chips > 1 else v, low(r))
        ks = [whole[r] if r in whole else k_by[r] for r in range(n_out)]
        vs = [whole[r] if r in whole else v_by[r] for r in range(n_out)]
        rows = tuple(half if r in whole else 0 for r in range(n_out))

    def shapes(wide):
        rows = CORES * block if wide else block
        return (jax.ShapeDtypeStruct((rows, tok), BF16),) * (1 if wide else CORES)

    work = 2 * PER * both * n_out * both * size

    def score(r, done):
        with jax.named_scope("score"):
            return pl.pallas_call(
                functools.partial(score_kernel, r == 0),
                out_shape=(
                    jax.ShapeDtypeStruct((PER, n_out * both, both), BF16),
                    jax.ShapeDtypeStruct((PER * 8, both), F32),
                ),
                in_specs=vmem(1 + n_out),
                out_specs=tuple(vmem(2)),
                compiler_params=params,
                cost_estimate=pl.CostEstimate(flops=work, bytes_accessed=2**20, transcendentals=work // (2 * size)),
                name="score",
            )(q_by[r] if done is None else after(q_by[r], done), *ks)

    def apply(r, wide):
        with jax.named_scope("apply"):
            return pl.pallas_call(
                functools.partial(apply_kernel, wide, rows),
                out_shape=shapes(wide),
                in_specs=vmem(2 + n_out),
                out_specs=tuple(vmem(len(shapes(wide)))),
                compiler_params=params,
                cost_estimate=pl.CostEstimate(flops=work, bytes_accessed=2**20, transcendentals=0),
                name="apply",
            )(*weights_by[r], *vs)

    def add(arrays, wide):
        with jax.named_scope("add"):
            return pl.pallas_call(
                functools.partial(add_kernel, len(arrays), wide),
                out_shape=shapes(wide),
                in_specs=vmem(len(arrays)),
                out_specs=tuple(vmem(len(shapes(wide)))),
                compiler_params=params,
                name="add",
            )(*arrays)

    arrived = {r: [] for r in range(chips)}
    ends = []

    def send(r, parts):
        with jax.named_scope("return"):
            if single(r):
                ends.extend(lax.ppermute(parts[x], "inner", along_inner(r, x)) for x in range(CORES))
            else:
                arrived[r - low(r)].append(lax.ppermute(parts[0], "inner", along_inner(low(r), 0)))

    def both_kernels(r, done):
        weights_by[r] = score(r, done)
        partial[r] = apply(r, r > 1)
        return partial[r][0]

    done = None
    weights_by, partial = {}, {}
    for r in sorted(range(1, chips), key=lambda r: (r != chips - 1, r != 1, -r)):
        done = both_kernels(r, done)
    for r in reversed(range(2, chips)):
        parts = partial[r]
        if arrived[r]:
            parts = add([parts[0], *arrived[r]], not single(r))
            done = parts[0]
        send(r, parts)
    done = both_kernels(0, done)
    if chips > 1:
        send(1, [partial[1][0], after(partial[1][1], done)])
    with jax.named_scope("return"):
        ends = [partial[0][0], lax.ppermute(partial[0][1], "inner", along_inner(0, 1))] + ends
    with jax.named_scope("combine"):
        return pl.pallas_call(
            functools.partial(combine_kernel, len(ends)),
            out_shape=jax.ShapeDtypeStruct((tok, width), BF16),
            in_specs=vmem(len(ends)),
            out_specs=vmem()[0],
            compiler_params=params,
            name="combine",
        )(*ends)


def solution(mesh):
    n_out, n_in = mesh.shape["outer"], mesh.shape["inner"]
    return jax.shard_map(
        functools.partial(shards, n_out, n_in),
        mesh=mesh,
        in_specs=(
            P(("outer", "inner"), None),
            P(("outer", "inner"), None),
            P(("outer", "inner"), None),
            P(("outer", "inner")),
        ),
        out_specs=P(("outer", "inner"), None),
        check_vma=False,
    )
```

```python
import functools
import math

import jax
import jax.numpy as jnp
from jax import lax
from jax.experimental import pallas as pl
from jax.experimental.pallas import tpu as pltpu
from jax.sharding import PartitionSpec as P

HEADS = 4
CORES = 2
PER = HEADS // CORES
PAD = 16
LOW = -1e30
FLOOR = -1e29
BF16 = jnp.bfloat16
F32 = jnp.float32


def nt_dot(a, b):
    return lax.dot_general(a, b, (((1,), (1,)), ((), ())), preferred_element_type=F32)


def place(own, other, out, at, turned=False):
    tok = own.shape[0]
    size = own.shape[1] // HEADS
    core = lax.rem(lax.axis_index("inner"), CORES)
    for b, ref in enumerate((own, other)):
        for j in range(PER):
            piece = ref[:, pl.ds(pl.multiple_of((core * PER + j) * size, size), size)]
            if turned:
                piece = piece.astype(F32).T.astype(BF16)
            row = at + j * CORES * tok + b * tok
            out[row : row + tok, :] = piece


def starts(p0, p1, size):
    half = PAD // CORES
    return jnp.concatenate([jnp.full((half, size), p[0].astype(F32), F32) for p in (p0, p1)], axis=0).astype(BF16)


def merge_kernel(p0, p1, own, q1, k1, v1, q_out, kv_out):
    tok = q1.shape[0]
    rows = PER * CORES * tok
    pos = starts(p0, p1, q_out.shape[1])
    place(own.at[0:tok, :], q1, q_out, 0)
    q_out[rows:, :] = pos
    place(own.at[tok : 2 * tok, :], k1, kv_out, 0)
    kv_out[rows : rows + PAD, :] = pos
    place(own.at[2 * tok : 3 * tok, :], v1, kv_out, rows + PAD, turned=True)


def score_kernel(same, q_ref, *refs):
    k_refs, (p_ref, top_ref) = refs[:-2], refs[-2:]
    size = q_ref.shape[1]
    tok = size
    both = CORES * tok
    half = PAD // CORES
    rate = size ** -0.5 * math.log2(math.e)
    at_or_before = lax.broadcasted_iota(jnp.int32, (tok, tok), 0) <= lax.broadcasted_iota(jnp.int32, (tok, tok), 1)

    def block_of(ref):
        first = ref[PER * both : PER * both + PAD, :].astype(F32)
        return [first[b * half : b * half + 1, :] for b in range(CORES)]

    q_block = jnp.concatenate(block_of(q_ref), axis=1)
    kept = [jnp.concatenate([p] * CORES, axis=1) <= q_block for ref in k_refs for p in block_of(ref)]
    for h in range(PER):
        q = q_ref[h * both : (h + 1) * both, :]
        scores = []
        for j, ref in enumerate(k_refs):
            s = nt_dot(ref[h * both : (h + 1) * both, :], q)
            for b in range(CORES):
                part = s[b * tok : (b + 1) * tok, :]
                if same and j == 0:
                    cols = [part[:, c * tok : (c + 1) * tok] for c in range(CORES)]
                    cols[b] = jnp.where(at_or_before, cols[b], LOW)
                    part = jnp.concatenate(cols, axis=1)
                scores.append(part)
        tops = [jnp.where(k, jnp.max(s, axis=0, keepdims=True), FLOOR) for k, s in zip(kept, scores)]
        top = jnp.maximum(functools.reduce(jnp.maximum, tops), FLOOR).astype(BF16).astype(F32)
        for i, (k, s) in enumerate(zip(kept, scores)):
            p_ref[h, i * tok : (i + 1) * tok, :] = jnp.exp2((s - jnp.where(k, top, -LOW)) * rate).astype(BF16)
        top_ref[h * 8 : (h + 1) * 8, :] = jnp.broadcast_to(top, (8, both))


def apply_kernel(wide, rows, p_ref, top_ref, *refs):
    nv = len(refs) - (1 if wide else CORES)
    v_refs, out_refs = refs[:nv], refs[nv:]
    size = v_refs[0].shape[1]
    tok = size
    both = CORES * tok
    block = PER * size + PAD

    def store(b, at, value):
        if wide:
            out_refs[0][b * block + at : b * block + at + value.shape[0], :] = value
        else:
            out_refs[b][at : at + value.shape[0], :] = value

    stats = [[] for _ in range(CORES)]
    for h in range(PER):
        vals = []
        for ref, row in zip(v_refs, rows):
            for b in range(CORES):
                at = row + h * both + b * tok
                vals.append(ref[at : at + tok, :])
        vt = jnp.concatenate(vals, axis=1)
        vt = jnp.concatenate([vt, jnp.ones((PAD, vt.shape[1]), BF16)], axis=0)
        o = jnp.dot(vt, p_ref[h], preferred_element_type=F32)
        total = o[size : size + 1, :]
        hi = total.astype(BF16).astype(F32)
        top = top_ref[h * 8 : h * 8 + 1, :]
        for b in range(CORES):
            cols = slice(b * tok, (b + 1) * tok)
            store(b, h * size, o[0:size, cols].astype(BF16))
            stats[b] += [top[:, cols], hi[:, cols], (total - hi)[:, cols]]
    for b in range(CORES):
        rest = jnp.zeros((PAD - 3 * PER, tok), F32)
        store(b, PER * size, jnp.concatenate(stats[b] + [rest], axis=0).astype(BF16))


def joined(parts, stats, h, rate):
    size = parts[0].shape[0]
    tops = [s[3 * h : 3 * h + 1, :] for s in stats]
    best = functools.reduce(jnp.maximum, tops)
    factors = [jnp.exp2((t - best) * rate) for t in tops]
    total = sum(f * (s[3 * h + 1 : 3 * h + 2, :] + s[3 * h + 2 : 3 * h + 3, :]) for f, s in zip(factors, stats))
    numer = sum(f * part.astype(F32) for f, part in zip(factors, parts))
    return best, total, numer


def add_kernel(n, wide, *refs):
    size = refs[0].shape[1]
    block = PER * size + PAD
    rate = size ** -0.5 * math.log2(math.e)
    for b in range(CORES):
        base = b * block
        stats = [ref[base + PER * size : base + block, :].astype(F32) for ref in refs[:n]]
        out, at = (refs[n], base) if wide else (refs[n + b], 0)
        rows = []
        for h in range(PER):
            parts = [ref[base + h * size : base + (h + 1) * size, :] for ref in refs[:n]]
            best, total, numer = joined(parts, stats, h, rate)
            hi = total.astype(BF16).astype(F32)
            rows += [best, hi, total - hi]
            out[at + h * size : at + (h + 1) * size, :] = numer.astype(BF16)
        rest = jnp.zeros((PAD - 3 * PER, size), F32)
        out[at + PER * size : at + block, :] = jnp.concatenate(rows + [rest], axis=0).astype(BF16)


def combine_kernel(n, *refs):
    parts, out_ref = refs[:n], refs[n]
    size = parts[0].shape[1]
    rate = size ** -0.5 * math.log2(math.e)
    core = lax.rem(lax.axis_index("inner"), CORES)
    for x in range(CORES):
        mine = parts[x::CORES]
        pair = jnp.bitwise_xor(core, x)
        stats = [part[PER * size :, :].astype(F32) for part in mine]
        for h in range(PER):
            _, total, numer = joined([part[h * size : (h + 1) * size, :] for part in mine], stats, h, rate)
            cols = pl.ds(pl.multiple_of((pair * PER + h) * size, size), size)
            out_ref[:, cols] = (numer * (1.0 / total)).T.astype(BF16)


def vmem(n=1):
    return [pl.BlockSpec(memory_space=pltpu.VMEM)] * n


def shards(n_out, n_in, queries, keys, values, block_pos):
    tok, width = queries.shape
    size = width // HEADS
    chips = n_in // CORES
    both = CORES * tok
    params = pltpu.CompilerParams(vmem_limit_bytes=40 * 1024 * 1024)

    def along_inner(r, x):
        return [(w * CORES + c, (w ^ r) * CORES + (c ^ x)) for w in range(chips) for c in range(CORES)]

    def after(a, b):
        return lax.optimization_barrier((a, b))[0]

    with jax.named_scope("swap"):
        other = [lax.ppermute(a, "inner", along_inner(0, 1)) for a in (queries, keys, values, block_pos)]
        own = jnp.concatenate([queries, keys, values], axis=0)
    with jax.named_scope("merge"):
        smem = [pl.BlockSpec(memory_space=pltpu.SMEM)]
        q_piece, kv_piece = pl.pallas_call(
            merge_kernel,
            out_shape=(
                jax.ShapeDtypeStruct((PER * both + PAD, size), BF16),
                jax.ShapeDtypeStruct((2 * PER * both + PAD, size), BF16),
            ),
            in_specs=smem * 2 + vmem(4),
            out_specs=tuple(vmem(2)),
            compiler_params=params,
            name="merge",
        )(block_pos, other[3], own, *other[:3])
    half = PER * both + PAD
    block = PER * size + PAD

    def low(r):
        return r & -r

    def high(r):
        return 1 << (r.bit_length() - 1)

    def single(r):
        return r == low(r)

    def over(a, r):
        return lax.ppermute(a, "outer", [(o, o ^ r) for o in range(n_out)])

    with jax.named_scope("exchange"):
        whole = {r: over(kv_piece, r) if r else kv_piece for r in range(n_out) if single(r)}
        q_by = {0: q_piece}
        for r in reversed(range(1, chips)):
            q_by[r] = lax.ppermute(q_piece, "inner", along_inner(r, 0))
        k_by = {r: a[:half, :] for r, a in whole.items() if r}
        v_by = {r: a[half:, :] for r, a in whole.items() if r}
        for r in range(1, n_out):
            if not single(r):
                k_by[r] = over(k_by[r - high(r)], high(r))
        for r in sorted(range(1, n_out), key=lambda r: r.bit_count()):
            if not single(r):
                v = v_by[r - low(r)]
                v_by[r] = over(after(v, q_by[1]) if chips > 1 else v, low(r))
        ks = [whole[r] if r in whole else k_by[r] for r in range(n_out)]
        vs = [whole[r] if r in whole else v_by[r] for r in range(n_out)]
        rows = tuple(half if r in whole else 0 for r in range(n_out))

    def shapes(wide):
        rows = CORES * block if wide else block
        return (jax.ShapeDtypeStruct((rows, tok), BF16),) * (1 if wide else CORES)

    work = 2 * PER * both * n_out * both * size

    def score(r, done):
        with jax.named_scope("score"):
            return pl.pallas_call(
                functools.partial(score_kernel, r == 0),
                out_shape=(
                    jax.ShapeDtypeStruct((PER, n_out * both, both), BF16),
                    jax.ShapeDtypeStruct((PER * 8, both), F32),
                ),
                in_specs=vmem(1 + n_out),
                out_specs=tuple(vmem(2)),
                compiler_params=params,
                cost_estimate=pl.CostEstimate(flops=work, bytes_accessed=2**20, transcendentals=work // (2 * size)),
                name="score",
            )(q_by[r] if done is None else after(q_by[r], done), *ks)

    def apply(r, wide):
        with jax.named_scope("apply"):
            return pl.pallas_call(
                functools.partial(apply_kernel, wide, rows),
                out_shape=shapes(wide),
                in_specs=vmem(2 + n_out),
                out_specs=tuple(vmem(len(shapes(wide)))),
                compiler_params=params,
                cost_estimate=pl.CostEstimate(flops=work, bytes_accessed=2**20, transcendentals=0),
                name="apply",
            )(*weights_by[r], *vs)

    def add(arrays, wide):
        with jax.named_scope("add"):
            return pl.pallas_call(
                functools.partial(add_kernel, len(arrays), wide),
                out_shape=shapes(wide),
                in_specs=vmem(len(arrays)),
                out_specs=tuple(vmem(len(shapes(wide)))),
                compiler_params=params,
                name="add",
            )(*arrays)

    arrived = {r: [] for r in range(chips)}
    ends = []

    def send(r, parts):
        with jax.named_scope("return"):
            if single(r):
                ends.extend(lax.ppermute(parts[x], "inner", along_inner(r, x)) for x in range(CORES))
            else:
                arrived[r - low(r)].append(lax.ppermute(parts[0], "inner", along_inner(low(r), 0)))

    def both_kernels(r, done):
        weights_by[r] = score(r, done)
        partial[r] = apply(r, r > 1)
        return partial[r][0]

    done = None
    weights_by, partial = {}, {}
    for r in sorted(range(1, chips), key=lambda r: (r != chips - 1, r != 1, -r)):
        done = both_kernels(r, done)
    for r in reversed(range(1, chips)):
        parts = partial[r]
        if arrived[r]:
            parts = add([parts[0], *arrived[r]], not single(r))
            done = parts[0]
        if r == 1:
            parts = [parts[0], after(parts[1], done)]
        send(r, parts)
    both_kernels(0, done)
    with jax.named_scope("return"):
        ends = [partial[0][0], lax.ppermute(partial[0][1], "inner", along_inner(0, 1))] + ends
    with jax.named_scope("combine"):
        return pl.pallas_call(
            functools.partial(combine_kernel, len(ends)),
            out_shape=jax.ShapeDtypeStruct((tok, width), BF16),
            in_specs=vmem(len(ends)),
            out_specs=vmem()[0],
            compiler_params=params,
            name="combine",
        )(*ends)


def solution(mesh):
    n_out, n_in = mesh.shape["outer"], mesh.shape["inner"]
    return jax.shard_map(
        functools.partial(shards, n_out, n_in),
        mesh=mesh,
        in_specs=(
            P(("outer", "inner"), None),
            P(("outer", "inner"), None),
            P(("outer", "inner"), None),
            P(("outer", "inner")),
        ),
        out_specs=P(("outer", "inner"), None),
        check_vma=False,
    )
```

```python
import functools
import math

import jax
import jax.numpy as jnp
from jax import lax
from jax.experimental import pallas as pl
from jax.experimental.pallas import tpu as pltpu
from jax.sharding import PartitionSpec as P

HEADS = 4
CORES = 2
PER = HEADS // CORES
PAD = 16
LOW = -1e30
FLOOR = -1e29
BF16 = jnp.bfloat16
F32 = jnp.float32


def nt_dot(a, b):
    return lax.dot_general(a, b, (((1,), (1,)), ((), ())), preferred_element_type=F32)


def place(own, other, out, at, turned=False):
    tok = own.shape[0]
    size = own.shape[1] // HEADS
    core = lax.rem(lax.axis_index("inner"), CORES)
    for b, ref in enumerate((own, other)):
        for j in range(PER):
            piece = ref[:, pl.ds(pl.multiple_of((core * PER + j) * size, size), size)]
            if turned:
                piece = piece.astype(F32).T.astype(BF16)
            row = at + j * CORES * tok + b * tok
            out[row : row + tok, :] = piece


def starts(p0, p1, size):
    half = PAD // CORES
    return jnp.concatenate([jnp.full((half, size), p[0].astype(F32), F32) for p in (p0, p1)], axis=0).astype(BF16)


def merge_kernel(p0, p1, own, q1, k1, v1, q_out, kv_out):
    tok = q1.shape[0]
    rows = PER * CORES * tok
    pos = starts(p0, p1, q_out.shape[1])
    place(own.at[0:tok, :], q1, q_out, 0)
    q_out[rows:, :] = pos
    place(own.at[tok : 2 * tok, :], k1, kv_out, 0)
    kv_out[rows : rows + PAD, :] = pos
    place(own.at[2 * tok : 3 * tok, :], v1, kv_out, rows + PAD, turned=True)


def score_kernel(same, q_ref, *refs):
    k_refs, (p_ref, top_ref) = refs[:-2], refs[-2:]
    size = q_ref.shape[1]
    tok = size
    both = CORES * tok
    half = PAD // CORES
    rate = size ** -0.5 * math.log2(math.e)
    at_or_before = lax.broadcasted_iota(jnp.int32, (tok, tok), 0) <= lax.broadcasted_iota(jnp.int32, (tok, tok), 1)

    def block_of(ref):
        first = ref[PER * both : PER * both + PAD, :].astype(F32)
        return [first[b * half : b * half + 1, :] for b in range(CORES)]

    q_block = jnp.concatenate(block_of(q_ref), axis=1)
    kept = [jnp.concatenate([p] * CORES, axis=1) <= q_block for ref in k_refs for p in block_of(ref)]
    for h in range(PER):
        q = q_ref[h * both : (h + 1) * both, :]
        scores = []
        for j, ref in enumerate(k_refs):
            s = nt_dot(ref[h * both : (h + 1) * both, :], q)
            for b in range(CORES):
                part = s[b * tok : (b + 1) * tok, :]
                if same and j == 0:
                    cols = [part[:, c * tok : (c + 1) * tok] for c in range(CORES)]
                    cols[b] = jnp.where(at_or_before, cols[b], LOW)
                    part = jnp.concatenate(cols, axis=1)
                scores.append(part)
        tops = [jnp.where(k, jnp.max(s, axis=0, keepdims=True), FLOOR) for k, s in zip(kept, scores)]
        top = jnp.maximum(functools.reduce(jnp.maximum, tops), FLOOR).astype(BF16).astype(F32)
        for i, (k, s) in enumerate(zip(kept, scores)):
            p_ref[h, i * tok : (i + 1) * tok, :] = jnp.exp2((s - jnp.where(k, top, -LOW)) * rate).astype(BF16)
        top_ref[h * 8 : (h + 1) * 8, :] = jnp.broadcast_to(top, (8, both))


def apply_kernel(wide, rows, p_ref, top_ref, *refs):
    nv = len(refs) - (1 if wide else CORES)
    v_refs, out_refs = refs[:nv], refs[nv:]
    size = v_refs[0].shape[1]
    tok = size
    both = CORES * tok
    block = PER * size + PAD

    def store(b, at, value):
        if wide:
            out_refs[0][b * block + at : b * block + at + value.shape[0], :] = value
        else:
            out_refs[b][at : at + value.shape[0], :] = value

    stats = [[] for _ in range(CORES)]
    for h in range(PER):
        vals = []
        for ref, row in zip(v_refs, rows):
            for b in range(CORES):
                at = row + h * both + b * tok
                vals.append(ref[at : at + tok, :])
        vt = jnp.concatenate(vals, axis=1)
        vt = jnp.concatenate([vt, jnp.ones((PAD, vt.shape[1]), BF16)], axis=0)
        o = jnp.dot(vt, p_ref[h], preferred_element_type=F32)
        total = o[size : size + 1, :]
        hi = total.astype(BF16).astype(F32)
        top = top_ref[h * 8 : h * 8 + 1, :]
        for b in range(CORES):
            cols = slice(b * tok, (b + 1) * tok)
            store(b, h * size, o[0:size, cols].astype(BF16))
            stats[b] += [top[:, cols], hi[:, cols], (total - hi)[:, cols]]
    for b in range(CORES):
        rest = jnp.zeros((PAD - 3 * PER, tok), F32)
        store(b, PER * size, jnp.concatenate(stats[b] + [rest], axis=0).astype(BF16))


def joined(parts, stats, h, rate):
    size = parts[0].shape[0]
    tops = [s[3 * h : 3 * h + 1, :] for s in stats]
    best = functools.reduce(jnp.maximum, tops)
    factors = [jnp.exp2((t - best) * rate) for t in tops]
    total = sum(f * (s[3 * h + 1 : 3 * h + 2, :] + s[3 * h + 2 : 3 * h + 3, :]) for f, s in zip(factors, stats))
    numer = sum(f * part.astype(F32) for f, part in zip(factors, parts))
    return best, total, numer


def add_kernel(n, wide, *refs):
    size = refs[0].shape[1]
    block = PER * size + PAD
    rate = size ** -0.5 * math.log2(math.e)
    for b in range(CORES):
        base = b * block
        stats = [ref[base + PER * size : base + block, :].astype(F32) for ref in refs[:n]]
        out, at = (refs[n], base) if wide else (refs[n + b], 0)
        rows = []
        for h in range(PER):
            parts = [ref[base + h * size : base + (h + 1) * size, :] for ref in refs[:n]]
            best, total, numer = joined(parts, stats, h, rate)
            hi = total.astype(BF16).astype(F32)
            rows += [best, hi, total - hi]
            out[at + h * size : at + (h + 1) * size, :] = numer.astype(BF16)
        rest = jnp.zeros((PAD - 3 * PER, size), F32)
        out[at + PER * size : at + block, :] = jnp.concatenate(rows + [rest], axis=0).astype(BF16)


def combine_kernel(n, *refs):
    parts, out_ref = refs[:n], refs[n]
    size = parts[0].shape[1]
    rate = size ** -0.5 * math.log2(math.e)
    core = lax.rem(lax.axis_index("inner"), CORES)
    for x in range(CORES):
        mine = parts[x::CORES]
        pair = jnp.bitwise_xor(core, x)
        stats = [part[PER * size :, :].astype(F32) for part in mine]
        for h in range(PER):
            _, total, numer = joined([part[h * size : (h + 1) * size, :] for part in mine], stats, h, rate)
            cols = pl.ds(pl.multiple_of((pair * PER + h) * size, size), size)
            out_ref[:, cols] = (numer * (1.0 / total)).T.astype(BF16)


def vmem(n=1):
    return [pl.BlockSpec(memory_space=pltpu.VMEM)] * n


def shards(n_out, n_in, queries, keys, values, block_pos):
    tok, width = queries.shape
    size = width // HEADS
    chips = n_in // CORES
    both = CORES * tok
    params = pltpu.CompilerParams(vmem_limit_bytes=40 * 1024 * 1024)

    def along_inner(r, x):
        return [(w * CORES + c, (w ^ r) * CORES + (c ^ x)) for w in range(chips) for c in range(CORES)]

    def after(a, b):
        return lax.optimization_barrier((a, b))[0]

    with jax.named_scope("swap"):
        other = [lax.ppermute(a, "inner", along_inner(0, 1)) for a in (queries, keys, values, block_pos)]
        own = jnp.concatenate([queries, keys, values], axis=0)
    with jax.named_scope("merge"):
        smem = [pl.BlockSpec(memory_space=pltpu.SMEM)]
        q_piece, kv_piece = pl.pallas_call(
            merge_kernel,
            out_shape=(
                jax.ShapeDtypeStruct((PER * both + PAD, size), BF16),
                jax.ShapeDtypeStruct((2 * PER * both + PAD, size), BF16),
            ),
            in_specs=smem * 2 + vmem(4),
            out_specs=tuple(vmem(2)),
            compiler_params=params,
            name="merge",
        )(block_pos, other[3], own, *other[:3])
    half = PER * both + PAD
    block = PER * size + PAD

    def low(r):
        return r & -r

    def high(r):
        return 1 << (r.bit_length() - 1)

    def single(r):
        return r == low(r)

    def over(a, r):
        return lax.ppermute(a, "outer", [(o, o ^ r) for o in range(n_out)])

    with jax.named_scope("exchange"):
        whole = {r: over(kv_piece, r) if r else kv_piece for r in range(n_out) if single(r)}
        q_by = {0: q_piece}
        for r in reversed(range(1, chips)):
            q_by[r] = lax.ppermute(q_piece, "inner", along_inner(r, 0))
        k_by = {r: a[:half, :] for r, a in whole.items() if r}
        v_by = {r: a[half:, :] for r, a in whole.items() if r}
        for r in range(1, n_out):
            if not single(r):
                k_by[r] = over(k_by[r - high(r)], high(r))
        for r in sorted(range(1, n_out), key=lambda r: r.bit_count()):
            if not single(r):
                v = v_by[r - low(r)]
                v_by[r] = over(after(v, q_by[1]) if chips > 1 else v, low(r))
        ks = [whole[r] if r in whole else k_by[r] for r in range(n_out)]
        vs = [whole[r] if r in whole else v_by[r] for r in range(n_out)]
        rows = tuple(half if r in whole else 0 for r in range(n_out))

    def shapes(wide):
        rows = CORES * block if wide else block
        return (jax.ShapeDtypeStruct((rows, tok), BF16),) * (1 if wide else CORES)

    work = 2 * PER * both * n_out * both * size

    def score(r, done):
        with jax.named_scope("score"):
            return pl.pallas_call(
                functools.partial(score_kernel, r == 0),
                out_shape=(
                    jax.ShapeDtypeStruct((PER, n_out * both, both), BF16),
                    jax.ShapeDtypeStruct((PER * 8, both), F32),
                ),
                in_specs=vmem(1 + n_out),
                out_specs=tuple(vmem(2)),
                compiler_params=params,
                cost_estimate=pl.CostEstimate(flops=work, bytes_accessed=2**20, transcendentals=work // (2 * size)),
                name="score",
            )(q_by[r] if done is None else after(q_by[r], done), *ks)

    def apply(r, wide):
        with jax.named_scope("apply"):
            return pl.pallas_call(
                functools.partial(apply_kernel, wide, rows),
                out_shape=shapes(wide),
                in_specs=vmem(2 + n_out),
                out_specs=tuple(vmem(len(shapes(wide)))),
                compiler_params=params,
                cost_estimate=pl.CostEstimate(flops=work, bytes_accessed=2**20, transcendentals=0),
                name="apply",
            )(*weights_by[r], *vs)

    def add(arrays, wide):
        with jax.named_scope("add"):
            return pl.pallas_call(
                functools.partial(add_kernel, len(arrays), wide),
                out_shape=shapes(wide),
                in_specs=vmem(len(arrays)),
                out_specs=tuple(vmem(len(shapes(wide)))),
                compiler_params=params,
                name="add",
            )(*arrays)

    arrived = {r: [] for r in range(chips)}
    ends = []

    def send(r, parts):
        with jax.named_scope("return"):
            if single(r):
                ends.extend(lax.ppermute(parts[x], "inner", along_inner(r, x)) for x in range(CORES))
            else:
                arrived[r - low(r)].append(lax.ppermute(parts[0], "inner", along_inner(low(r), 0)))

    def both_kernels(r, done):
        weights_by[r] = score(r, done)
        partial[r] = apply(r, r > 1)
        return partial[r][0]

    done = None
    weights_by, partial = {}, {}
    for r in sorted(range(1, chips), key=lambda r: (r != chips - 1, r != 1, -r)):
        done = both_kernels(r, done)
    last = done
    for r in reversed(range(1, chips)):
        parts = partial[r]
        if arrived[r]:
            parts = add([parts[0], *arrived[r]], not single(r))
            done = parts[0]
        if r == 1:
            parts = [parts[0], after(parts[1], last)]
        send(r, parts)
    both_kernels(0, done)
    with jax.named_scope("return"):
        ends = [partial[0][0], lax.ppermute(partial[0][1], "inner", along_inner(0, 1))] + ends
    with jax.named_scope("combine"):
        return pl.pallas_call(
            functools.partial(combine_kernel, len(ends)),
            out_shape=jax.ShapeDtypeStruct((tok, width), BF16),
            in_specs=vmem(len(ends)),
            out_specs=vmem()[0],
            compiler_params=params,
            name="combine",
        )(*ends)


def solution(mesh):
    n_out, n_in = mesh.shape["outer"], mesh.shape["inner"]
    return jax.shard_map(
        functools.partial(shards, n_out, n_in),
        mesh=mesh,
        in_specs=(
            P(("outer", "inner"), None),
            P(("outer", "inner"), None),
            P(("outer", "inner"), None),
            P(("outer", "inner")),
        ),
        out_specs=P(("outer", "inner"), None),
        check_vma=False,
    )
```

```python
import functools
import math

import jax
import jax.numpy as jnp
from jax import lax
from jax.experimental import pallas as pl
from jax.experimental.pallas import tpu as pltpu
from jax.sharding import PartitionSpec as P

HEADS = 4
CORES = 2
PER = HEADS // CORES
PAD = 16
LOW = -1e30
FLOOR = -1e29
BF16 = jnp.bfloat16
F32 = jnp.float32


def nt_dot(a, b):
    return lax.dot_general(a, b, (((1,), (1,)), ((), ())), preferred_element_type=F32)


def place(own, other, out, at, turned=False):
    tok = own.shape[0]
    size = own.shape[1] // HEADS
    core = lax.rem(lax.axis_index("inner"), CORES)
    for b, ref in enumerate((own, other)):
        for j in range(PER):
            piece = ref[:, pl.ds(pl.multiple_of((core * PER + j) * size, size), size)]
            if turned:
                piece = piece.astype(F32).T.astype(BF16)
            row = at + j * CORES * tok + b * tok
            out[row : row + tok, :] = piece


def merge_kernel(p0, p1, own, q1, k1, v1, q_out, kv_out, pos, sem):
    tok = q1.shape[0]
    size = q_out.shape[1]
    rows = PER * CORES * tok
    copy = pltpu.make_async_copy(p1, pos, sem)
    copy.start()
    place(own.at[tok : 2 * tok, :], k1, kv_out, 0)
    place(own.at[2 * tok : 3 * tok, :], v1, kv_out, rows + PAD, turned=True)
    place(own.at[0:tok, :], q1, q_out, 0)
    copy.wait()
    half = PAD // CORES
    starts = [jnp.full((half, size), p[0].astype(F32), F32) for p in (p0, pos)]
    starts = jnp.concatenate(starts, axis=0).astype(BF16)
    q_out[rows:, :] = starts
    kv_out[rows : rows + PAD, :] = starts


def score_kernel(same, q_ref, *refs):
    k_refs, (p_ref, top_ref) = refs[:-2], refs[-2:]
    size = q_ref.shape[1]
    tok = size
    both = CORES * tok
    half = PAD // CORES
    rate = size ** -0.5 * math.log2(math.e)
    at_or_before = lax.broadcasted_iota(jnp.int32, (tok, tok), 0) <= lax.broadcasted_iota(jnp.int32, (tok, tok), 1)

    def block_of(ref):
        first = ref[PER * both : PER * both + PAD, :].astype(F32)
        return [first[b * half : b * half + 1, :] for b in range(CORES)]

    q_block = jnp.concatenate(block_of(q_ref), axis=1)
    kept = [jnp.concatenate([p] * CORES, axis=1) <= q_block for ref in k_refs for p in block_of(ref)]
    for h in range(PER):
        q = q_ref[h * both : (h + 1) * both, :]
        scores = []
        for j, ref in enumerate(k_refs):
            s = nt_dot(ref[h * both : (h + 1) * both, :], q)
            for b in range(CORES):
                part = s[b * tok : (b + 1) * tok, :]
                if same and j == 0:
                    cols = [part[:, c * tok : (c + 1) * tok] for c in range(CORES)]
                    cols[b] = jnp.where(at_or_before, cols[b], LOW)
                    part = jnp.concatenate(cols, axis=1)
                scores.append(part)
        tops = [jnp.where(k, jnp.max(s, axis=0, keepdims=True), FLOOR) for k, s in zip(kept, scores)]
        top = jnp.maximum(functools.reduce(jnp.maximum, tops), FLOOR).astype(BF16).astype(F32)
        for i, (k, s) in enumerate(zip(kept, scores)):
            p_ref[h, i * tok : (i + 1) * tok, :] = jnp.exp2((s - jnp.where(k, top, -LOW)) * rate).astype(BF16)
        top_ref[h * 8 : (h + 1) * 8, :] = jnp.broadcast_to(top, (8, both))


def apply_kernel(wide, rows, p_ref, top_ref, *refs):
    nv = len(refs) - (1 if wide else CORES)
    v_refs, out_refs = refs[:nv], refs[nv:]
    size = v_refs[0].shape[1]
    tok = size
    both = CORES * tok
    block = PER * size + PAD

    def store(b, at, value):
        if wide:
            out_refs[0][b * block + at : b * block + at + value.shape[0], :] = value
        else:
            out_refs[b][at : at + value.shape[0], :] = value

    stats = [[] for _ in range(CORES)]
    for h in range(PER):
        vals = []
        for ref, row in zip(v_refs, rows):
            for b in range(CORES):
                at = row + h * both + b * tok
                vals.append(ref[at : at + tok, :])
        vt = jnp.concatenate(vals, axis=1)
        vt = jnp.concatenate([vt, jnp.ones((PAD, vt.shape[1]), BF16)], axis=0)
        o = jnp.dot(vt, p_ref[h], preferred_element_type=F32)
        total = o[size : size + 1, :]
        hi = total.astype(BF16).astype(F32)
        top = top_ref[h * 8 : h * 8 + 1, :]
        for b in range(CORES):
            cols = slice(b * tok, (b + 1) * tok)
            store(b, h * size, o[0:size, cols].astype(BF16))
            stats[b] += [top[:, cols], hi[:, cols], (total - hi)[:, cols]]
    for b in range(CORES):
        rest = jnp.zeros((PAD - 3 * PER, tok), F32)
        store(b, PER * size, jnp.concatenate(stats[b] + [rest], axis=0).astype(BF16))


def joined(parts, stats, h, rate):
    size = parts[0].shape[0]
    tops = [s[3 * h : 3 * h + 1, :] for s in stats]
    best = functools.reduce(jnp.maximum, tops)
    factors = [jnp.exp2((t - best) * rate) for t in tops]
    total = sum(f * (s[3 * h + 1 : 3 * h + 2, :] + s[3 * h + 2 : 3 * h + 3, :]) for f, s in zip(factors, stats))
    numer = sum(f * part.astype(F32) for f, part in zip(factors, parts))
    return best, total, numer


def add_kernel(n, wide, *refs):
    size = refs[0].shape[1]
    block = PER * size + PAD
    rate = size ** -0.5 * math.log2(math.e)
    for b in range(CORES):
        base = b * block
        stats = [ref[base + PER * size : base + block, :].astype(F32) for ref in refs[:n]]
        out, at = (refs[n], base) if wide else (refs[n + b], 0)
        rows = []
        for h in range(PER):
            parts = [ref[base + h * size : base + (h + 1) * size, :] for ref in refs[:n]]
            best, total, numer = joined(parts, stats, h, rate)
            hi = total.astype(BF16).astype(F32)
            rows += [best, hi, total - hi]
            out[at + h * size : at + (h + 1) * size, :] = numer.astype(BF16)
        rest = jnp.zeros((PAD - 3 * PER, size), F32)
        out[at + PER * size : at + block, :] = jnp.concatenate(rows + [rest], axis=0).astype(BF16)


def combine_kernel(n, *refs):
    parts, out_ref, heads, sems = refs[:n], *refs[n:]
    size = parts[0].shape[1]
    rate = size ** -0.5 * math.log2(math.e)
    core = lax.rem(lax.axis_index("inner"), CORES)
    copies = []
    for x in range(CORES):
        mine = parts[x::CORES]
        pair = jnp.bitwise_xor(core, x)
        stats = [part[PER * size :, :].astype(F32) for part in mine]
        for h in range(PER):
            at = x * PER + h
            _, total, numer = joined([part[h * size : (h + 1) * size, :] for part in mine], stats, h, rate)
            heads[at] = (numer * (1.0 / total)).T.astype(BF16)
            cols = pl.ds(pl.multiple_of((pair * PER + h) * size, size), size)
            copies.append(pltpu.make_async_copy(heads.at[at], out_ref.at[:, cols], sems.at[at]))
            copies[-1].start()
    for copy in copies:
        copy.wait()


def vmem(n=1):
    return [pl.BlockSpec(memory_space=pltpu.VMEM)] * n


def shards(n_out, n_in, queries, keys, values, block_pos):
    tok, width = queries.shape
    size = width // HEADS
    chips = n_in // CORES
    both = CORES * tok
    params = pltpu.CompilerParams(vmem_limit_bytes=40 * 1024 * 1024)

    def along_inner(r, x):
        return [(w * CORES + c, (w ^ r) * CORES + (c ^ x)) for w in range(chips) for c in range(CORES)]

    def after(a, b):
        return lax.optimization_barrier((a, b))[0]

    with jax.named_scope("swap"):
        other = [lax.ppermute(a, "inner", along_inner(0, 1)) for a in (queries, keys, values, block_pos)]
        own = jnp.concatenate([queries, keys, values], axis=0)
    with jax.named_scope("merge"):
        smem = [pl.BlockSpec(memory_space=pltpu.SMEM)]
        q_piece, kv_piece = pl.pallas_call(
            merge_kernel,
            out_shape=(
                jax.ShapeDtypeStruct((PER * both + PAD, size), BF16),
                jax.ShapeDtypeStruct((2 * PER * both + PAD, size), BF16),
            ),
            in_specs=smem + [pl.BlockSpec(memory_space=pl.ANY)] + vmem(4),
            out_specs=tuple(vmem(2)),
            scratch_shapes=[pltpu.SMEM((1,), jnp.int32), pltpu.SemaphoreType.DMA],
            compiler_params=params,
            name="merge",
        )(block_pos, other[3], own, *other[:3])
    half = PER * both + PAD
    block = PER * size + PAD

    def low(r):
        return r & -r

    def high(r):
        return 1 << (r.bit_length() - 1)

    def single(r):
        return r == low(r)

    def over(a, r):
        return lax.ppermute(a, "outer", [(o, o ^ r) for o in range(n_out)])

    with jax.named_scope("exchange"):
        whole = {r: over(kv_piece, r) if r else kv_piece for r in range(n_out) if single(r)}
        q_by = {0: q_piece}
        for r in reversed(range(1, chips)):
            q_by[r] = lax.ppermute(q_piece, "inner", along_inner(r, 0))
        k_by = {r: a[:half, :] for r, a in whole.items() if r}
        v_by = {r: a[half:, :] for r, a in whole.items() if r}
        for r in range(1, n_out):
            if not single(r):
                k_by[r] = over(k_by[r - high(r)], high(r))
        for r in sorted(range(1, n_out), key=lambda r: r.bit_count()):
            if not single(r):
                v = v_by[r - low(r)]
                v_by[r] = over(after(v, q_by[1]) if chips > 1 else v, low(r))
        ks = [whole[r] if r in whole else k_by[r] for r in range(n_out)]
        vs = [whole[r] if r in whole else v_by[r] for r in range(n_out)]
        rows = tuple(half if r in whole else 0 for r in range(n_out))

    def shapes(wide):
        rows = CORES * block if wide else block
        return (jax.ShapeDtypeStruct((rows, tok), BF16),) * (1 if wide else CORES)

    work = 2 * PER * both * n_out * both * size

    def score(r, done):
        with jax.named_scope("score"):
            return pl.pallas_call(
                functools.partial(score_kernel, r == 0),
                out_shape=(
                    jax.ShapeDtypeStruct((PER, n_out * both, both), BF16),
                    jax.ShapeDtypeStruct((PER * 8, both), F32),
                ),
                in_specs=vmem(1 + n_out),
                out_specs=tuple(vmem(2)),
                compiler_params=params,
                cost_estimate=pl.CostEstimate(flops=work, bytes_accessed=2**20, transcendentals=work // (2 * size)),
                name="score",
            )(q_by[r] if done is None else after(q_by[r], done), *ks)

    def apply(r, wide):
        with jax.named_scope("apply"):
            return pl.pallas_call(
                functools.partial(apply_kernel, wide, rows),
                out_shape=shapes(wide),
                in_specs=vmem(2 + n_out),
                out_specs=tuple(vmem(len(shapes(wide)))),
                compiler_params=params,
                cost_estimate=pl.CostEstimate(flops=work, bytes_accessed=2**20, transcendentals=0),
                name="apply",
            )(*weights_by[r], *vs)

    def add(arrays, wide):
        with jax.named_scope("add"):
            return pl.pallas_call(
                functools.partial(add_kernel, len(arrays), wide),
                out_shape=shapes(wide),
                in_specs=vmem(len(arrays)),
                out_specs=tuple(vmem(len(shapes(wide)))),
                compiler_params=params,
                name="add",
            )(*arrays)

    arrived = {r: [] for r in range(chips)}
    ends = []

    def send(r, parts):
        with jax.named_scope("return"):
            if single(r):
                ends.extend(lax.ppermute(parts[x], "inner", along_inner(r, x)) for x in range(CORES))
            else:
                arrived[r - low(r)].append(lax.ppermute(parts[0], "inner", along_inner(low(r), 0)))

    def both_kernels(r, done):
        weights_by[r] = score(r, done)
        partial[r] = apply(r, r > 1)
        return partial[r][0]

    done = None
    weights_by, partial = {}, {}
    for r in sorted(range(1, chips), key=lambda r: (r != chips - 1, r != 1, -r)):
        done = both_kernels(r, done)
    for r in reversed(range(2, chips)):
        parts = partial[r]
        if arrived[r]:
            parts = add([parts[0], *arrived[r]], not single(r))
            done = parts[0]
        send(r, parts)
    done = both_kernels(0, done)
    if chips > 1:
        send(1, [partial[1][0], after(partial[1][1], done)])
    with jax.named_scope("return"):
        ends = [partial[0][0], lax.ppermute(partial[0][1], "inner", along_inner(0, 1))] + ends
    with jax.named_scope("combine"):
        return pl.pallas_call(
            functools.partial(combine_kernel, len(ends)),
            out_shape=jax.ShapeDtypeStruct((tok, width), BF16),
            in_specs=vmem(len(ends)),
            out_specs=pl.BlockSpec(memory_space=pl.ANY),
            scratch_shapes=[pltpu.VMEM((HEADS, tok, size), BF16), pltpu.SemaphoreType.DMA((HEADS,))],
            compiler_params=params,
            name="combine",
        )(*ends)


def solution(mesh):
    n_out, n_in = mesh.shape["outer"], mesh.shape["inner"]
    return jax.shard_map(
        functools.partial(shards, n_out, n_in),
        mesh=mesh,
        in_specs=(
            P(("outer", "inner"), None),
            P(("outer", "inner"), None),
            P(("outer", "inner"), None),
            P(("outer", "inner")),
        ),
        out_specs=P(("outer", "inner"), None),
        check_vma=False,
    )
```

```python
import functools
import math

import jax
import jax.numpy as jnp
from jax import lax
from jax.experimental import pallas as pl
from jax.experimental.pallas import tpu as pltpu
from jax.sharding import PartitionSpec as P

HEADS = 4
CORES = 2
PER = HEADS // CORES
PAD = 16
LOW = -1e30
FLOOR = -1e29
BF16 = jnp.bfloat16
F32 = jnp.float32


def nt_dot(a, b):
    return lax.dot_general(a, b, (((1,), (1,)), ((), ())), preferred_element_type=F32)


def place(own, other, out, at, turned=False):
    tok = own.shape[0]
    size = own.shape[1] // HEADS
    core = lax.rem(lax.axis_index("inner"), CORES)
    for b, ref in enumerate((own, other)):
        for j in range(PER):
            piece = ref[:, pl.ds(pl.multiple_of((core * PER + j) * size, size), size)]
            if turned:
                piece = piece.astype(F32).T.astype(BF16)
            row = at + j * CORES * tok + b * tok
            out[row : row + tok, :] = piece


def starts(p0, p1, size):
    half = PAD // CORES
    return jnp.concatenate([jnp.broadcast_to(p[...].astype(F32), (half, size)) for p in (p0, p1)], axis=0).astype(BF16)


def merge_kernel(p0, p1, own, q1, k1, v1, q_out, kv_out):
    tok = q1.shape[0]
    rows = PER * CORES * tok
    pos = starts(p0, p1, q_out.shape[1])
    place(own.at[0:tok, :], q1, q_out, 0)
    q_out[rows:, :] = pos
    place(own.at[tok : 2 * tok, :], k1, kv_out, 0)
    kv_out[rows : rows + PAD, :] = pos
    place(own.at[2 * tok : 3 * tok, :], v1, kv_out, rows + PAD, turned=True)


def score_kernel(same, q_ref, *refs):
    k_refs, (p_ref, top_ref) = refs[:-2], refs[-2:]
    size = q_ref.shape[1]
    tok = size
    both = CORES * tok
    half = PAD // CORES
    rate = size ** -0.5 * math.log2(math.e)
    at_or_before = lax.broadcasted_iota(jnp.int32, (tok, tok), 0) <= lax.broadcasted_iota(jnp.int32, (tok, tok), 1)

    def block_of(ref):
        first = ref[PER * both : PER * both + PAD, :].astype(F32)
        return [first[b * half : b * half + 1, :] for b in range(CORES)]

    q_block = jnp.concatenate(block_of(q_ref), axis=1)
    kept = [jnp.concatenate([p] * CORES, axis=1) <= q_block for ref in k_refs for p in block_of(ref)]
    for h in range(PER):
        q = q_ref[h * both : (h + 1) * both, :]
        scores = []
        for j, ref in enumerate(k_refs):
            s = nt_dot(ref[h * both : (h + 1) * both, :], q)
            for b in range(CORES):
                part = s[b * tok : (b + 1) * tok, :]
                if same and j == 0:
                    cols = [part[:, c * tok : (c + 1) * tok] for c in range(CORES)]
                    cols[b] = jnp.where(at_or_before, cols[b], LOW)
                    part = jnp.concatenate(cols, axis=1)
                scores.append(part)
        tops = [jnp.where(k, jnp.max(s, axis=0, keepdims=True), FLOOR) for k, s in zip(kept, scores)]
        top = jnp.maximum(functools.reduce(jnp.maximum, tops), FLOOR).astype(BF16).astype(F32)
        for i, (k, s) in enumerate(zip(kept, scores)):
            p_ref[h, i * tok : (i + 1) * tok, :] = jnp.exp2((s - jnp.where(k, top, -LOW)) * rate).astype(BF16)
        top_ref[h * 8 : (h + 1) * 8, :] = jnp.broadcast_to(top, (8, both))


def apply_kernel(wide, rows, p_ref, top_ref, *refs):
    nv = len(refs) - (1 if wide else CORES)
    v_refs, out_refs = refs[:nv], refs[nv:]
    size = v_refs[0].shape[1]
    tok = size
    both = CORES * tok
    block = PER * size + PAD

    def store(b, at, value):
        if wide:
            out_refs[0][b * block + at : b * block + at + value.shape[0], :] = value
        else:
            out_refs[b][at : at + value.shape[0], :] = value

    stats = [[] for _ in range(CORES)]
    for h in range(PER):
        vals = []
        for ref, row in zip(v_refs, rows):
            for b in range(CORES):
                at = row + h * both + b * tok
                vals.append(ref[at : at + tok, :])
        vt = jnp.concatenate(vals, axis=1)
        vt = jnp.concatenate([vt, jnp.ones((PAD, vt.shape[1]), BF16)], axis=0)
        o = jnp.dot(vt, p_ref[h], preferred_element_type=F32)
        total = o[size : size + 1, :]
        hi = total.astype(BF16).astype(F32)
        top = top_ref[h * 8 : h * 8 + 1, :]
        for b in range(CORES):
            cols = slice(b * tok, (b + 1) * tok)
            store(b, h * size, o[0:size, cols].astype(BF16))
            stats[b] += [top[:, cols], hi[:, cols], (total - hi)[:, cols]]
    for b in range(CORES):
        rest = jnp.zeros((PAD - 3 * PER, tok), F32)
        store(b, PER * size, jnp.concatenate(stats[b] + [rest], axis=0).astype(BF16))


def joined(parts, stats, h, rate):
    size = parts[0].shape[0]
    tops = [s[3 * h : 3 * h + 1, :] for s in stats]
    best = functools.reduce(jnp.maximum, tops)
    factors = [jnp.exp2((t - best) * rate) for t in tops]
    total = sum(f * (s[3 * h + 1 : 3 * h + 2, :] + s[3 * h + 2 : 3 * h + 3, :]) for f, s in zip(factors, stats))
    numer = sum(f * part.astype(F32) for f, part in zip(factors, parts))
    return best, total, numer


def add_kernel(n, wide, *refs):
    size = refs[0].shape[1]
    block = PER * size + PAD
    rate = size ** -0.5 * math.log2(math.e)
    for b in range(CORES):
        base = b * block
        stats = [ref[base + PER * size : base + block, :].astype(F32) for ref in refs[:n]]
        out, at = (refs[n], base) if wide else (refs[n + b], 0)
        rows = []
        for h in range(PER):
            parts = [ref[base + h * size : base + (h + 1) * size, :] for ref in refs[:n]]
            best, total, numer = joined(parts, stats, h, rate)
            hi = total.astype(BF16).astype(F32)
            rows += [best, hi, total - hi]
            out[at + h * size : at + (h + 1) * size, :] = numer.astype(BF16)
        rest = jnp.zeros((PAD - 3 * PER, size), F32)
        out[at + PER * size : at + block, :] = jnp.concatenate(rows + [rest], axis=0).astype(BF16)


def combine_kernel(n, *refs):
    parts, out_ref = refs[:n], refs[n]
    size = parts[0].shape[1]
    rate = size ** -0.5 * math.log2(math.e)
    core = lax.rem(lax.axis_index("inner"), CORES)
    for x in range(CORES):
        mine = parts[x::CORES]
        pair = jnp.bitwise_xor(core, x)
        stats = [part[PER * size :, :].astype(F32) for part in mine]
        for h in range(PER):
            _, total, numer = joined([part[h * size : (h + 1) * size, :] for part in mine], stats, h, rate)
            cols = pl.ds(pl.multiple_of((pair * PER + h) * size, size), size)
            out_ref[:, cols] = (numer * (1.0 / total)).T.astype(BF16)


def vmem(n=1):
    return [pl.BlockSpec(memory_space=pltpu.VMEM)] * n


def shards(n_out, n_in, queries, keys, values, block_pos):
    tok, width = queries.shape
    size = width // HEADS
    chips = n_in // CORES
    both = CORES * tok
    params = pltpu.CompilerParams(vmem_limit_bytes=40 * 1024 * 1024)

    def along_inner(r, x):
        return [(w * CORES + c, (w ^ r) * CORES + (c ^ x)) for w in range(chips) for c in range(CORES)]

    def after(a, b):
        return lax.optimization_barrier((a, b))[0]

    with jax.named_scope("swap"):
        here = block_pos.reshape(1, 1)
        other = [lax.ppermute(a, "inner", along_inner(0, 1)) for a in (queries, keys, values, here)]
        own = jnp.concatenate([queries, keys, values], axis=0)
    with jax.named_scope("merge"):
        q_piece, kv_piece = pl.pallas_call(
            merge_kernel,
            out_shape=(
                jax.ShapeDtypeStruct((PER * both + PAD, size), BF16),
                jax.ShapeDtypeStruct((2 * PER * both + PAD, size), BF16),
            ),
            in_specs=vmem(6),
            out_specs=tuple(vmem(2)),
            compiler_params=params,
            name="merge",
        )(here, other[3], own, *other[:3])
    half = PER * both + PAD
    block = PER * size + PAD

    def low(r):
        return r & -r

    def high(r):
        return 1 << (r.bit_length() - 1)

    def single(r):
        return r == low(r)

    def over(a, r):
        return lax.ppermute(a, "outer", [(o, o ^ r) for o in range(n_out)])

    with jax.named_scope("exchange"):
        whole = {r: over(kv_piece, r) if r else kv_piece for r in range(n_out) if single(r)}
        q_by = {0: q_piece}
        for r in reversed(range(1, chips)):
            q_by[r] = lax.ppermute(q_piece, "inner", along_inner(r, 0))
        k_by = {r: a[:half, :] for r, a in whole.items() if r}
        v_by = {r: a[half:, :] for r, a in whole.items() if r}
        for r in range(1, n_out):
            if not single(r):
                k_by[r] = over(k_by[r - high(r)], high(r))
        for r in sorted(range(1, n_out), key=lambda r: r.bit_count()):
            if not single(r):
                v = v_by[r - low(r)]
                v_by[r] = over(after(v, q_by[1]) if chips > 1 else v, low(r))
        ks = [whole[r] if r in whole else k_by[r] for r in range(n_out)]
        vs = [whole[r] if r in whole else v_by[r] for r in range(n_out)]
        rows = tuple(half if r in whole else 0 for r in range(n_out))

    def shapes(wide):
        rows = CORES * block if wide else block
        return (jax.ShapeDtypeStruct((rows, tok), BF16),) * (1 if wide else CORES)

    work = 2 * PER * both * n_out * both * size

    def score(r, done):
        with jax.named_scope("score"):
            return pl.pallas_call(
                functools.partial(score_kernel, r == 0),
                out_shape=(
                    jax.ShapeDtypeStruct((PER, n_out * both, both), BF16),
                    jax.ShapeDtypeStruct((PER * 8, both), F32),
                ),
                in_specs=vmem(1 + n_out),
                out_specs=tuple(vmem(2)),
                compiler_params=params,
                cost_estimate=pl.CostEstimate(flops=work, bytes_accessed=2**20, transcendentals=work // (2 * size)),
                name="score",
            )(q_by[r] if done is None else after(q_by[r], done), *ks)

    def apply(r, wide):
        with jax.named_scope("apply"):
            return pl.pallas_call(
                functools.partial(apply_kernel, wide, rows),
                out_shape=shapes(wide),
                in_specs=vmem(2 + n_out),
                out_specs=tuple(vmem(len(shapes(wide)))),
                compiler_params=params,
                cost_estimate=pl.CostEstimate(flops=work, bytes_accessed=2**20, transcendentals=0),
                name="apply",
            )(*weights_by[r], *vs)

    def add(arrays, wide):
        with jax.named_scope("add"):
            return pl.pallas_call(
                functools.partial(add_kernel, len(arrays), wide),
                out_shape=shapes(wide),
                in_specs=vmem(len(arrays)),
                out_specs=tuple(vmem(len(shapes(wide)))),
                compiler_params=params,
                name="add",
            )(*arrays)

    arrived = {r: [] for r in range(chips)}
    ends = []

    def send(r, parts):
        with jax.named_scope("return"):
            if single(r):
                ends.extend(lax.ppermute(parts[x], "inner", along_inner(r, x)) for x in range(CORES))
            else:
                arrived[r - low(r)].append(lax.ppermute(parts[0], "inner", along_inner(low(r), 0)))

    def both_kernels(r, done):
        weights_by[r] = score(r, done)
        partial[r] = apply(r, r > 1)
        return partial[r][0]

    done = None
    weights_by, partial = {}, {}
    for r in sorted(range(1, chips), key=lambda r: (r != chips - 1, r != 1, -r)):
        done = both_kernels(r, done)
    for r in reversed(range(2, chips)):
        parts = partial[r]
        if arrived[r]:
            parts = add([parts[0], *arrived[r]], not single(r))
            done = parts[0]
        send(r, parts)
    done = both_kernels(0, done)
    if chips > 1:
        send(1, [partial[1][0], after(partial[1][1], done)])
    with jax.named_scope("return"):
        ends = [partial[0][0], lax.ppermute(partial[0][1], "inner", along_inner(0, 1))] + ends
    with jax.named_scope("combine"):
        return pl.pallas_call(
            functools.partial(combine_kernel, len(ends)),
            out_shape=jax.ShapeDtypeStruct((tok, width), BF16),
            in_specs=vmem(len(ends)),
            out_specs=vmem()[0],
            compiler_params=params,
            name="combine",
        )(*ends)


def solution(mesh):
    n_out, n_in = mesh.shape["outer"], mesh.shape["inner"]
    return jax.shard_map(
        functools.partial(shards, n_out, n_in),
        mesh=mesh,
        in_specs=(
            P(("outer", "inner"), None),
            P(("outer", "inner"), None),
            P(("outer", "inner"), None),
            P(("outer", "inner")),
        ),
        out_specs=P(("outer", "inner"), None),
        check_vma=False,
    )
```

```python
import functools
import math

import jax
import jax.numpy as jnp
from jax import lax
from jax.experimental import pallas as pl
from jax.experimental.pallas import tpu as pltpu
from jax.sharding import PartitionSpec as P

HEADS = 4
CORES = 2
PER = HEADS // CORES
PAD = 16
LOW = -1e30
FLOOR = -1e29
BF16 = jnp.bfloat16
F32 = jnp.float32


def nt_dot(a, b):
    return lax.dot_general(a, b, (((1,), (1,)), ((), ())), preferred_element_type=F32)


def place(own, other, out, at, turned=False):
    tok = own.shape[0]
    size = own.shape[1] // HEADS
    core = lax.rem(lax.axis_index("inner"), CORES)
    for b, ref in enumerate((own, other)):
        for j in range(PER):
            piece = ref[:, pl.ds(pl.multiple_of((core * PER + j) * size, size), size)]
            if turned:
                piece = piece.astype(F32).T.astype(BF16)
            row = at + j * CORES * tok + b * tok
            out[row : row + tok, :] = piece


def starts(p0, p1, size):
    half = PAD // CORES
    return jnp.concatenate([jnp.full((half, size), p[0].astype(F32), F32) for p in (p0, p1)], axis=0).astype(BF16)


def merge_kernel(p0, p1, own, q1, k1, v1, q_out, kv_out):
    tok = q1.shape[0]
    rows = PER * CORES * tok
    pos = starts(p0, p1, q_out.shape[1])
    place(own.at[0:tok, :], q1, q_out, 0)
    q_out[rows:, :] = pos
    place(own.at[tok : 2 * tok, :], k1, kv_out, 0)
    kv_out[rows : rows + PAD, :] = pos
    place(own.at[2 * tok : 3 * tok, :], v1, kv_out, rows + PAD, turned=True)


def score_kernel(same, q_ref, *refs):
    k_refs, (p_ref, top_ref) = refs[:-2], refs[-2:]
    size = q_ref.shape[1]
    tok = size
    both = CORES * tok
    half = PAD // CORES
    rate = size ** -0.5 * math.log2(math.e)
    at_or_before = lax.broadcasted_iota(jnp.int32, (tok, tok), 0) <= lax.broadcasted_iota(jnp.int32, (tok, tok), 1)

    def block_of(ref):
        first = ref[PER * both : PER * both + PAD, :].astype(F32)
        return [first[b * half : b * half + 1, :] for b in range(CORES)]

    q_block = jnp.concatenate(block_of(q_ref), axis=1)
    kept = [jnp.concatenate([p] * CORES, axis=1) <= q_block for ref in k_refs for p in block_of(ref)]
    for h in range(PER):
        q = q_ref[h * both : (h + 1) * both, :]
        scores = []
        for j, ref in enumerate(k_refs):
            s = nt_dot(ref[h * both : (h + 1) * both, :], q)
            for b in range(CORES):
                part = s[b * tok : (b + 1) * tok, :]
                if same and j == 0:
                    cols = [part[:, c * tok : (c + 1) * tok] for c in range(CORES)]
                    cols[b] = jnp.where(at_or_before, cols[b], LOW)
                    part = jnp.concatenate(cols, axis=1)
                scores.append(part)
        tops = [jnp.where(k, jnp.max(s, axis=0, keepdims=True), FLOOR) for k, s in zip(kept, scores)]
        top = jnp.maximum(functools.reduce(jnp.maximum, tops), FLOOR).astype(BF16).astype(F32)
        for i, (k, s) in enumerate(zip(kept, scores)):
            p_ref[h, i * tok : (i + 1) * tok, :] = jnp.exp2((s - jnp.where(k, top, -LOW)) * rate).astype(BF16)
        top_ref[h * 8 : (h + 1) * 8, :] = jnp.broadcast_to(top, (8, both))


def apply_kernel(wide, rows, p_ref, top_ref, *refs):
    nv = len(refs) - (1 if wide else CORES)
    v_refs, out_refs = refs[:nv], refs[nv:]
    size = v_refs[0].shape[1]
    tok = size
    both = CORES * tok
    block = PER * size + PAD

    def store(b, at, value):
        if wide:
            out_refs[0][b * block + at : b * block + at + value.shape[0], :] = value
        else:
            out_refs[b][at : at + value.shape[0], :] = value

    stats = [[] for _ in range(CORES)]
    for h in range(PER):
        vals = []
        for ref, row in zip(v_refs, rows):
            for b in range(CORES):
                at = row + h * both + b * tok
                vals.append(ref[at : at + tok, :])
        vt = jnp.concatenate(vals, axis=1)
        vt = jnp.concatenate([vt, jnp.ones((PAD, vt.shape[1]), BF16)], axis=0)
        o = jnp.dot(vt, p_ref[h], preferred_element_type=F32)
        total = o[size : size + 1, :]
        hi = total.astype(BF16).astype(F32)
        top = top_ref[h * 8 : h * 8 + 1, :]
        for b in range(CORES):
            cols = slice(b * tok, (b + 1) * tok)
            store(b, h * size, o[0:size, cols].astype(BF16))
            stats[b] += [top[:, cols], hi[:, cols], (total - hi)[:, cols]]
    for b in range(CORES):
        rest = jnp.zeros((PAD - 3 * PER, tok), F32)
        store(b, PER * size, jnp.concatenate(stats[b] + [rest], axis=0).astype(BF16))


def joined(parts, stats, h, rate):
    size = parts[0].shape[0]
    tops = [s[3 * h : 3 * h + 1, :] for s in stats]
    best = functools.reduce(jnp.maximum, tops)
    factors = [jnp.exp2((t - best) * rate) for t in tops]
    total = sum(f * (s[3 * h + 1 : 3 * h + 2, :] + s[3 * h + 2 : 3 * h + 3, :]) for f, s in zip(factors, stats))
    numer = sum(f * part.astype(F32) for f, part in zip(factors, parts))
    return best, total, numer


def add_kernel(n, wide, *refs):
    size = refs[0].shape[1]
    block = PER * size + PAD
    rate = size ** -0.5 * math.log2(math.e)
    for b in range(CORES):
        base = b * block
        stats = [ref[base + PER * size : base + block, :].astype(F32) for ref in refs[:n]]
        out, at = (refs[n], base) if wide else (refs[n + b], 0)
        rows = []
        for h in range(PER):
            parts = [ref[base + h * size : base + (h + 1) * size, :] for ref in refs[:n]]
            best, total, numer = joined(parts, stats, h, rate)
            hi = total.astype(BF16).astype(F32)
            rows += [best, hi, total - hi]
            out[at + h * size : at + (h + 1) * size, :] = numer.astype(BF16)
        rest = jnp.zeros((PAD - 3 * PER, size), F32)
        out[at + PER * size : at + block, :] = jnp.concatenate(rows + [rest], axis=0).astype(BF16)


def combine_kernel(n, *refs):
    parts, out_ref = refs[:n], refs[n]
    size = parts[0].shape[1]
    rate = size ** -0.5 * math.log2(math.e)
    core = lax.rem(lax.axis_index("inner"), CORES)
    for x in range(CORES):
        mine = parts[x::CORES]
        pair = jnp.bitwise_xor(core, x)
        stats = [part[PER * size :, :].astype(F32) for part in mine]
        for h in range(PER):
            _, total, numer = joined([part[h * size : (h + 1) * size, :] for part in mine], stats, h, rate)
            cols = pl.ds(pl.multiple_of((pair * PER + h) * size, size), size)
            out_ref[:, cols] = (numer * (1.0 / total)).T.astype(BF16)


def vmem(n=1):
    return [pl.BlockSpec(memory_space=pltpu.VMEM)] * n


def shards(n_out, n_in, queries, keys, values, block_pos):
    tok, width = queries.shape
    size = width // HEADS
    chips = n_in // CORES
    both = CORES * tok
    params = pltpu.CompilerParams(vmem_limit_bytes=40 * 1024 * 1024)

    def along_inner(r, x):
        return [(w * CORES + c, (w ^ r) * CORES + (c ^ x)) for w in range(chips) for c in range(CORES)]

    def after(a, b):
        return lax.optimization_barrier((a, b))[0]

    with jax.named_scope("swap"):
        other = [lax.ppermute(a, "inner", along_inner(0, 1)) for a in (queries, keys, values, block_pos)]
        own = jnp.concatenate([queries, keys, values], axis=0)
    with jax.named_scope("merge"):
        smem = [pl.BlockSpec(memory_space=pltpu.SMEM)]
        q_piece, kv_piece = pl.pallas_call(
            merge_kernel,
            out_shape=(
                jax.ShapeDtypeStruct((PER * both + PAD, size), BF16),
                jax.ShapeDtypeStruct((2 * PER * both + PAD, size), BF16),
            ),
            in_specs=smem * 2 + vmem(4),
            out_specs=tuple(vmem(2)),
            compiler_params=params,
            name="merge",
        )(block_pos, other[3], own, *other[:3])
    half = PER * both + PAD
    block = PER * size + PAD

    def low(r):
        return r & -r

    def high(r):
        return 1 << (r.bit_length() - 1)

    def single(r):
        return r == low(r)

    def over(a, r):
        return lax.ppermute(a, "outer", [(o, o ^ r) for o in range(n_out)])

    with jax.named_scope("exchange"):
        whole = {r: over(kv_piece, r) if r else kv_piece for r in range(n_out) if single(r)}
        q_by = {0: q_piece}
        for r in sorted(range(1, chips), key=lambda r: (r != chips - 1, r)):
            piece = q_piece if r in (1, chips - 1) else after(q_piece, q_by[1])
            q_by[r] = lax.ppermute(piece, "inner", along_inner(r, 0))
        k_by = {r: a[:half, :] for r, a in whole.items() if r}
        v_by = {r: a[half:, :] for r, a in whole.items() if r}
        for r in range(1, n_out):
            if not single(r):
                k_by[r] = over(k_by[r - high(r)], high(r))
        for r in sorted(range(1, n_out), key=lambda r: r.bit_count()):
            if not single(r):
                v_by[r] = over(v_by[r - low(r)], low(r))
        ks = [whole[r] if r in whole else k_by[r] for r in range(n_out)]
        vs = [whole[r] if r in whole else v_by[r] for r in range(n_out)]
        rows = tuple(half if r in whole else 0 for r in range(n_out))

    def shapes(wide):
        rows = CORES * block if wide else block
        return (jax.ShapeDtypeStruct((rows, tok), BF16),) * (1 if wide else CORES)

    work = 2 * PER * both * n_out * both * size

    def score(r, done):
        with jax.named_scope("score"):
            return pl.pallas_call(
                functools.partial(score_kernel, r == 0),
                out_shape=(
                    jax.ShapeDtypeStruct((PER, n_out * both, both), BF16),
                    jax.ShapeDtypeStruct((PER * 8, both), F32),
                ),
                in_specs=vmem(1 + n_out),
                out_specs=tuple(vmem(2)),
                compiler_params=params,
                cost_estimate=pl.CostEstimate(flops=work, bytes_accessed=2**20, transcendentals=work // (2 * size)),
                name="score",
            )(q_by[r] if done is None else after(q_by[r], done), *ks)

    def apply(r, wide):
        with jax.named_scope("apply"):
            return pl.pallas_call(
                functools.partial(apply_kernel, wide, rows),
                out_shape=shapes(wide),
                in_specs=vmem(2 + n_out),
                out_specs=tuple(vmem(len(shapes(wide)))),
                compiler_params=params,
                cost_estimate=pl.CostEstimate(flops=work, bytes_accessed=2**20, transcendentals=0),
                name="apply",
            )(*weights_by[r], *vs)

    def add(arrays, wide):
        with jax.named_scope("add"):
            return pl.pallas_call(
                functools.partial(add_kernel, len(arrays), wide),
                out_shape=shapes(wide),
                in_specs=vmem(len(arrays)),
                out_specs=tuple(vmem(len(shapes(wide)))),
                compiler_params=params,
                name="add",
            )(*arrays)

    arrived = {r: [] for r in range(chips)}
    ends = []

    def send(r, parts):
        with jax.named_scope("return"):
            if single(r):
                ends.extend(lax.ppermute(parts[x], "inner", along_inner(r, x)) for x in range(CORES))
            else:
                arrived[r - low(r)].append(lax.ppermute(parts[0], "inner", along_inner(low(r), 0)))

    def both_kernels(r, done):
        weights_by[r] = score(r, done)
        partial[r] = apply(r, r > 1)
        return partial[r][0]

    done = None
    weights_by, partial = {}, {}
    for r in sorted(range(1, chips), key=lambda r: (r != chips - 1, r != 1, -r)):
        done = both_kernels(r, done)
    for r in reversed(range(2, chips)):
        parts = partial[r]
        if arrived[r]:
            parts = add([parts[0], *arrived[r]], not single(r))
            done = parts[0]
        send(r, parts)
    done = both_kernels(0, done)
    if chips > 1:
        send(1, [partial[1][0], after(partial[1][1], done)])
    with jax.named_scope("return"):
        ends = [partial[0][0], lax.ppermute(partial[0][1], "inner", along_inner(0, 1))] + ends
    with jax.named_scope("combine"):
        return pl.pallas_call(
            functools.partial(combine_kernel, len(ends)),
            out_shape=jax.ShapeDtypeStruct((tok, width), BF16),
            in_specs=vmem(len(ends)),
            out_specs=vmem()[0],
            compiler_params=params,
            name="combine",
        )(*ends)


def solution(mesh):
    n_out, n_in = mesh.shape["outer"], mesh.shape["inner"]
    return jax.shard_map(
        functools.partial(shards, n_out, n_in),
        mesh=mesh,
        in_specs=(
            P(("outer", "inner"), None),
            P(("outer", "inner"), None),
            P(("outer", "inner"), None),
            P(("outer", "inner")),
        ),
        out_specs=P(("outer", "inner"), None),
        check_vma=False,
    )
```

```python
import functools
import math

import jax
import jax.numpy as jnp
from jax import lax
from jax.experimental import pallas as pl
from jax.experimental.pallas import tpu as pltpu
from jax.sharding import PartitionSpec as P

HEADS = 4
CORES = 2
PER = HEADS // CORES
PAD = 16
LOW = -1e30
FLOOR = -1e29
BF16 = jnp.bfloat16
F32 = jnp.float32


def nt_dot(a, b):
    return lax.dot_general(a, b, (((1,), (1,)), ((), ())), preferred_element_type=F32)


def place(own, other, out, at, turned=False):
    tok = own.shape[0]
    size = own.shape[1] // HEADS
    core = lax.rem(lax.axis_index("inner"), CORES)
    for b, ref in enumerate((own, other)):
        for j in range(PER):
            piece = ref[:, pl.ds(pl.multiple_of((core * PER + j) * size, size), size)]
            if turned:
                piece = piece.T
            row = at + j * CORES * tok + b * tok
            out[row : row + tok, :] = piece


def starts(p0, p1, size):
    half = PAD // CORES
    return jnp.concatenate([jnp.full((half, size), p[0].astype(F32), F32) for p in (p0, p1)], axis=0).astype(BF16)


def merge_kernel(p0, p1, own, q1, k1, v1, q_out, kv_out):
    tok = q1.shape[0]
    rows = PER * CORES * tok
    pos = starts(p0, p1, q_out.shape[1])
    place(own.at[0:tok, :], q1, q_out, 0)
    q_out[rows:, :] = pos
    place(own.at[tok : 2 * tok, :], k1, kv_out, 0)
    kv_out[rows : rows + PAD, :] = pos
    place(own.at[2 * tok : 3 * tok, :], v1, kv_out, rows + PAD, turned=True)


def score_kernel(same, q_ref, *refs):
    k_refs, (p_ref, top_ref) = refs[:-2], refs[-2:]
    size = q_ref.shape[1]
    tok = size
    both = CORES * tok
    half = PAD // CORES
    rate = size ** -0.5 * math.log2(math.e)
    at_or_before = lax.broadcasted_iota(jnp.int32, (tok, tok), 0) <= lax.broadcasted_iota(jnp.int32, (tok, tok), 1)

    def block_of(ref):
        first = ref[PER * both : PER * both + PAD, :].astype(F32)
        return [first[b * half : b * half + 1, :] for b in range(CORES)]

    q_block = jnp.concatenate(block_of(q_ref), axis=1)
    kept = [jnp.concatenate([p] * CORES, axis=1) <= q_block for ref in k_refs for p in block_of(ref)]
    for h in range(PER):
        q = q_ref[h * both : (h + 1) * both, :]
        scores = []
        for j, ref in enumerate(k_refs):
            s = nt_dot(ref[h * both : (h + 1) * both, :], q)
            for b in range(CORES):
                part = s[b * tok : (b + 1) * tok, :]
                if same and j == 0:
                    cols = [part[:, c * tok : (c + 1) * tok] for c in range(CORES)]
                    cols[b] = jnp.where(at_or_before, cols[b], LOW)
                    part = jnp.concatenate(cols, axis=1)
                scores.append(part)
        tops = [jnp.where(k, jnp.max(s, axis=0, keepdims=True), FLOOR) for k, s in zip(kept, scores)]
        top = jnp.maximum(functools.reduce(jnp.maximum, tops), FLOOR).astype(BF16).astype(F32)
        for i, (k, s) in enumerate(zip(kept, scores)):
            p_ref[h, i * tok : (i + 1) * tok, :] = jnp.exp2((s - jnp.where(k, top, -LOW)) * rate).astype(BF16)
        top_ref[h * 8 : (h + 1) * 8, :] = jnp.broadcast_to(top, (8, both))


def apply_kernel(wide, rows, p_ref, top_ref, *refs):
    nv = len(refs) - (1 if wide else CORES)
    v_refs, out_refs = refs[:nv], refs[nv:]
    size = v_refs[0].shape[1]
    tok = size
    both = CORES * tok
    block = PER * size + PAD

    def store(b, at, value):
        if wide:
            out_refs[0][b * block + at : b * block + at + value.shape[0], :] = value
        else:
            out_refs[b][at : at + value.shape[0], :] = value

    stats = [[] for _ in range(CORES)]
    for h in range(PER):
        vals = []
        for ref, row in zip(v_refs, rows):
            for b in range(CORES):
                at = row + h * both + b * tok
                vals.append(ref[at : at + tok, :])
        vt = jnp.concatenate(vals, axis=1)
        vt = jnp.concatenate([vt, jnp.ones((PAD, vt.shape[1]), BF16)], axis=0)
        o = jnp.dot(vt, p_ref[h], preferred_element_type=F32)
        total = o[size : size + 1, :]
        hi = total.astype(BF16).astype(F32)
        top = top_ref[h * 8 : h * 8 + 1, :]
        for b in range(CORES):
            cols = slice(b * tok, (b + 1) * tok)
            store(b, h * size, o[0:size, cols].astype(BF16))
            stats[b] += [top[:, cols], hi[:, cols], (total - hi)[:, cols]]
    for b in range(CORES):
        rest = jnp.zeros((PAD - 3 * PER, tok), F32)
        store(b, PER * size, jnp.concatenate(stats[b] + [rest], axis=0).astype(BF16))


def joined(parts, stats, h, rate):
    size = parts[0].shape[0]
    tops = [s[3 * h : 3 * h + 1, :] for s in stats]
    best = functools.reduce(jnp.maximum, tops)
    factors = [jnp.exp2((t - best) * rate) for t in tops]
    total = sum(f * (s[3 * h + 1 : 3 * h + 2, :] + s[3 * h + 2 : 3 * h + 3, :]) for f, s in zip(factors, stats))
    numer = sum(f * part.astype(F32) for f, part in zip(factors, parts))
    return best, total, numer


def add_kernel(n, wide, *refs):
    size = refs[0].shape[1]
    block = PER * size + PAD
    rate = size ** -0.5 * math.log2(math.e)
    for b in range(CORES):
        base = b * block
        stats = [ref[base + PER * size : base + block, :].astype(F32) for ref in refs[:n]]
        out, at = (refs[n], base) if wide else (refs[n + b], 0)
        rows = []
        for h in range(PER):
            parts = [ref[base + h * size : base + (h + 1) * size, :] for ref in refs[:n]]
            best, total, numer = joined(parts, stats, h, rate)
            hi = total.astype(BF16).astype(F32)
            rows += [best, hi, total - hi]
            out[at + h * size : at + (h + 1) * size, :] = numer.astype(BF16)
        rest = jnp.zeros((PAD - 3 * PER, size), F32)
        out[at + PER * size : at + block, :] = jnp.concatenate(rows + [rest], axis=0).astype(BF16)


def combine_kernel(n, *refs):
    parts, out_ref = refs[:n], refs[n]
    size = parts[0].shape[1]
    rate = size ** -0.5 * math.log2(math.e)
    core = lax.rem(lax.axis_index("inner"), CORES)
    for x in range(CORES):
        mine = parts[x::CORES]
        pair = jnp.bitwise_xor(core, x)
        stats = [part[PER * size :, :].astype(F32) for part in mine]
        for h in range(PER):
            _, total, numer = joined([part[h * size : (h + 1) * size, :] for part in mine], stats, h, rate)
            cols = pl.ds(pl.multiple_of((pair * PER + h) * size, size), size)
            out_ref[:, cols] = (numer * (1.0 / total)).astype(BF16).T


def vmem(n=1):
    return [pl.BlockSpec(memory_space=pltpu.VMEM)] * n


def shards(n_out, n_in, queries, keys, values, block_pos):
    tok, width = queries.shape
    size = width // HEADS
    chips = n_in // CORES
    both = CORES * tok
    params = pltpu.CompilerParams(vmem_limit_bytes=40 * 1024 * 1024)

    def along_inner(r, x):
        return [(w * CORES + c, (w ^ r) * CORES + (c ^ x)) for w in range(chips) for c in range(CORES)]

    def after(a, b):
        return lax.optimization_barrier((a, b))[0]

    with jax.named_scope("swap"):
        other = [lax.ppermute(a, "inner", along_inner(0, 1)) for a in (queries, keys, values, block_pos)]
        own = jnp.concatenate([queries, keys, values], axis=0)
    with jax.named_scope("merge"):
        smem = [pl.BlockSpec(memory_space=pltpu.SMEM)]
        q_piece, kv_piece = pl.pallas_call(
            merge_kernel,
            out_shape=(
                jax.ShapeDtypeStruct((PER * both + PAD, size), BF16),
                jax.ShapeDtypeStruct((2 * PER * both + PAD, size), BF16),
            ),
            in_specs=smem * 2 + vmem(4),
            out_specs=tuple(vmem(2)),
            compiler_params=params,
            name="merge",
        )(block_pos, other[3], own, *other[:3])
    half = PER * both + PAD
    block = PER * size + PAD

    def low(r):
        return r & -r

    def high(r):
        return 1 << (r.bit_length() - 1)

    def single(r):
        return r == low(r)

    def over(a, r):
        return lax.ppermute(a, "outer", [(o, o ^ r) for o in range(n_out)])

    with jax.named_scope("exchange"):
        whole = {r: over(kv_piece, r) if r else kv_piece for r in range(n_out) if single(r)}
        q_by = {0: q_piece}
        for r in sorted(range(1, chips), key=lambda r: (r != chips - 1, r)):
            piece = q_piece if r in (1, chips - 1) else after(q_piece, q_by[1])
            q_by[r] = lax.ppermute(piece, "inner", along_inner(r, 0))
        k_by = {r: a[:half, :] for r, a in whole.items() if r}
        v_by = {r: a[half:, :] for r, a in whole.items() if r}
        for r in range(1, n_out):
            if not single(r):
                k_by[r] = over(k_by[r - high(r)], high(r))
        for r in sorted(range(1, n_out), key=lambda r: r.bit_count()):
            if not single(r):
                v_by[r] = over(v_by[r - low(r)], low(r))
        ks = [whole[r] if r in whole else k_by[r] for r in range(n_out)]
        vs = [whole[r] if r in whole else v_by[r] for r in range(n_out)]
        rows = tuple(half if r in whole else 0 for r in range(n_out))

    def shapes(wide):
        rows = CORES * block if wide else block
        return (jax.ShapeDtypeStruct((rows, tok), BF16),) * (1 if wide else CORES)

    work = 2 * PER * both * n_out * both * size

    def score(r, done):
        with jax.named_scope("score"):
            return pl.pallas_call(
                functools.partial(score_kernel, r == 0),
                out_shape=(
                    jax.ShapeDtypeStruct((PER, n_out * both, both), BF16),
                    jax.ShapeDtypeStruct((PER * 8, both), F32),
                ),
                in_specs=vmem(1 + n_out),
                out_specs=tuple(vmem(2)),
                compiler_params=params,
                cost_estimate=pl.CostEstimate(flops=work, bytes_accessed=2**20, transcendentals=work // (2 * size)),
                name="score",
            )(q_by[r] if done is None else after(q_by[r], done), *ks)

    def apply(r, wide):
        with jax.named_scope("apply"):
            return pl.pallas_call(
                functools.partial(apply_kernel, wide, rows),
                out_shape=shapes(wide),
                in_specs=vmem(2 + n_out),
                out_specs=tuple(vmem(len(shapes(wide)))),
                compiler_params=params,
                cost_estimate=pl.CostEstimate(flops=work, bytes_accessed=2**20, transcendentals=0),
                name="apply",
            )(*weights_by[r], *vs)

    def add(arrays, wide):
        with jax.named_scope("add"):
            return pl.pallas_call(
                functools.partial(add_kernel, len(arrays), wide),
                out_shape=shapes(wide),
                in_specs=vmem(len(arrays)),
                out_specs=tuple(vmem(len(shapes(wide)))),
                compiler_params=params,
                name="add",
            )(*arrays)

    arrived = {r: [] for r in range(chips)}
    ends = []

    def send(r, parts):
        with jax.named_scope("return"):
            if single(r):
                ends.extend(lax.ppermute(parts[x], "inner", along_inner(r, x)) for x in range(CORES))
            else:
                arrived[r - low(r)].append(lax.ppermute(parts[0], "inner", along_inner(low(r), 0)))

    def both_kernels(r, done):
        weights_by[r] = score(r, done)
        partial[r] = apply(r, r > 1)
        return partial[r][0]

    done = None
    weights_by, partial = {}, {}
    for r in sorted(range(1, chips), key=lambda r: (r != chips - 1, r != 1, -r)):
        done = both_kernels(r, done)
    for r in reversed(range(2, chips)):
        parts = partial[r]
        if arrived[r]:
            parts = add([parts[0], *arrived[r]], not single(r))
            done = parts[0]
        send(r, parts)
    done = both_kernels(0, done)
    if chips > 1:
        send(1, [partial[1][0], after(partial[1][1], done)])
    with jax.named_scope("return"):
        ends = [partial[0][0], lax.ppermute(partial[0][1], "inner", along_inner(0, 1))] + ends
    with jax.named_scope("combine"):
        return pl.pallas_call(
            functools.partial(combine_kernel, len(ends)),
            out_shape=jax.ShapeDtypeStruct((tok, width), BF16),
            in_specs=vmem(len(ends)),
            out_specs=vmem()[0],
            compiler_params=params,
            name="combine",
        )(*ends)


def solution(mesh):
    n_out, n_in = mesh.shape["outer"], mesh.shape["inner"]
    return jax.shard_map(
        functools.partial(shards, n_out, n_in),
        mesh=mesh,
        in_specs=(
            P(("outer", "inner"), None),
            P(("outer", "inner"), None),
            P(("outer", "inner"), None),
            P(("outer", "inner")),
        ),
        out_specs=P(("outer", "inner"), None),
        check_vma=False,
    )
```

```python
import functools
import math

import jax
import jax.numpy as jnp
from jax import lax
from jax.experimental import pallas as pl
from jax.experimental.pallas import tpu as pltpu
from jax.sharding import PartitionSpec as P

HEADS = 4
CORES = 2
PER = HEADS // CORES
PAD = 16
LOW = -1e30
FLOOR = -1e29
BF16 = jnp.bfloat16
F32 = jnp.float32


def nt_dot(a, b):
    return lax.dot_general(a, b, (((1,), (1,)), ((), ())), preferred_element_type=F32)


def place(own, other, out, at, turned=False):
    tok = own.shape[0]
    size = own.shape[1] // HEADS
    core = lax.rem(lax.axis_index("inner"), CORES)
    for b, ref in enumerate((own, other)):
        for j in range(PER):
            piece = ref[:, pl.ds(pl.multiple_of((core * PER + j) * size, size), size)]
            if turned:
                piece = piece.T
            row = at + j * CORES * tok + b * tok
            out[row : row + tok, :] = piece


def starts(p0, p1, size):
    half = PAD // CORES
    return jnp.concatenate([jnp.full((half, size), p[0].astype(F32), F32) for p in (p0, p1)], axis=0).astype(BF16)


def merge_kernel(p0, p1, own, q1, k1, v1, q_out, kv_out):
    tok = q1.shape[0]
    rows = PER * CORES * tok
    pos = starts(p0, p1, q_out.shape[1])
    place(own.at[0:tok, :], q1, q_out, 0)
    q_out[rows:, :] = pos
    place(own.at[tok : 2 * tok, :], k1, kv_out, 0)
    kv_out[rows : rows + PAD, :] = pos
    place(own.at[2 * tok : 3 * tok, :], v1, kv_out, rows + PAD, turned=True)


def pick_kernel(k0, v0, k1, v1, k_out, v_out):
    core = lax.rem(lax.axis_index("inner"), CORES)

    @pl.when(core == 0)
    def _():
        k_out[...] = k0[...]
        v_out[...] = v0[...]

    @pl.when(core != 0)
    def _():
        k_out[...] = k1[...]
        v_out[...] = v1[...]


def score_kernel(same, q_ref, *refs):
    k_refs, (p_ref, top_ref) = refs[:-2], refs[-2:]
    size = q_ref.shape[1]
    tok = size
    both = CORES * tok
    half = PAD // CORES
    rate = size ** -0.5 * math.log2(math.e)
    at_or_before = lax.broadcasted_iota(jnp.int32, (tok, tok), 0) <= lax.broadcasted_iota(jnp.int32, (tok, tok), 1)

    def block_of(ref):
        first = ref[PER * both : PER * both + PAD, :].astype(F32)
        return [first[b * half : b * half + 1, :] for b in range(CORES)]

    q_block = jnp.concatenate(block_of(q_ref), axis=1)
    kept = [jnp.concatenate([p] * CORES, axis=1) <= q_block for ref in k_refs for p in block_of(ref)]
    for h in range(PER):
        q = q_ref[h * both : (h + 1) * both, :]
        scores = []
        for j, ref in enumerate(k_refs):
            s = nt_dot(ref[h * both : (h + 1) * both, :], q)
            for b in range(CORES):
                part = s[b * tok : (b + 1) * tok, :]
                if same and j == 0:
                    cols = [part[:, c * tok : (c + 1) * tok] for c in range(CORES)]
                    cols[b] = jnp.where(at_or_before, cols[b], LOW)
                    part = jnp.concatenate(cols, axis=1)
                scores.append(part)
        tops = [jnp.where(k, jnp.max(s, axis=0, keepdims=True), FLOOR) for k, s in zip(kept, scores)]
        top = jnp.maximum(functools.reduce(jnp.maximum, tops), FLOOR).astype(BF16).astype(F32)
        for i, (k, s) in enumerate(zip(kept, scores)):
            p_ref[h, i * tok : (i + 1) * tok, :] = jnp.exp2((s - jnp.where(k, top, -LOW)) * rate).astype(BF16)
        top_ref[h * 8 : (h + 1) * 8, :] = jnp.broadcast_to(top, (8, both))


def apply_kernel(wide, rows, p_ref, top_ref, *refs):
    nv = len(refs) - (1 if wide else CORES)
    v_refs, out_refs = refs[:nv], refs[nv:]
    size = v_refs[0].shape[1]
    tok = size
    both = CORES * tok
    block = PER * size + PAD

    def store(b, at, value):
        if wide:
            out_refs[0][b * block + at : b * block + at + value.shape[0], :] = value
        else:
            out_refs[b][at : at + value.shape[0], :] = value

    stats = [[] for _ in range(CORES)]
    for h in range(PER):
        vals = []
        for ref, row in zip(v_refs, rows):
            for b in range(CORES):
                at = row + h * both + b * tok
                vals.append(ref[at : at + tok, :])
        vt = jnp.concatenate(vals, axis=1)
        vt = jnp.concatenate([vt, jnp.ones((PAD, vt.shape[1]), BF16)], axis=0)
        o = jnp.dot(vt, p_ref[h], preferred_element_type=F32)
        total = o[size : size + 1, :]
        hi = total.astype(BF16).astype(F32)
        top = top_ref[h * 8 : h * 8 + 1, :]
        for b in range(CORES):
            cols = slice(b * tok, (b + 1) * tok)
            store(b, h * size, o[0:size, cols].astype(BF16))
            stats[b] += [top[:, cols], hi[:, cols], (total - hi)[:, cols]]
    for b in range(CORES):
        rest = jnp.zeros((PAD - 3 * PER, tok), F32)
        store(b, PER * size, jnp.concatenate(stats[b] + [rest], axis=0).astype(BF16))


def joined(parts, stats, h, rate):
    size = parts[0].shape[0]
    tops = [s[3 * h : 3 * h + 1, :] for s in stats]
    best = functools.reduce(jnp.maximum, tops)
    factors = [jnp.exp2((t - best) * rate) for t in tops]
    total = sum(f * (s[3 * h + 1 : 3 * h + 2, :] + s[3 * h + 2 : 3 * h + 3, :]) for f, s in zip(factors, stats))
    numer = sum(f * part.astype(F32) for f, part in zip(factors, parts))
    return best, total, numer


def add_kernel(n, wide, *refs):
    size = refs[0].shape[1]
    block = PER * size + PAD
    rate = size ** -0.5 * math.log2(math.e)
    for b in range(CORES):
        base = b * block
        stats = [ref[base + PER * size : base + block, :].astype(F32) for ref in refs[:n]]
        out, at = (refs[n], base) if wide else (refs[n + b], 0)
        rows = []
        for h in range(PER):
            parts = [ref[base + h * size : base + (h + 1) * size, :] for ref in refs[:n]]
            best, total, numer = joined(parts, stats, h, rate)
            hi = total.astype(BF16).astype(F32)
            rows += [best, hi, total - hi]
            out[at + h * size : at + (h + 1) * size, :] = numer.astype(BF16)
        rest = jnp.zeros((PAD - 3 * PER, size), F32)
        out[at + PER * size : at + block, :] = jnp.concatenate(rows + [rest], axis=0).astype(BF16)


def combine_kernel(n, *refs):
    parts, out_ref = refs[:n], refs[n]
    size = parts[0].shape[1]
    rate = size ** -0.5 * math.log2(math.e)
    core = lax.rem(lax.axis_index("inner"), CORES)
    for x in range(CORES):
        mine = parts[x::CORES]
        pair = jnp.bitwise_xor(core, x)
        stats = [part[PER * size :, :].astype(F32) for part in mine]
        for h in range(PER):
            _, total, numer = joined([part[h * size : (h + 1) * size, :] for part in mine], stats, h, rate)
            cols = pl.ds(pl.multiple_of((pair * PER + h) * size, size), size)
            out_ref[:, cols] = (numer * (1.0 / total)).astype(BF16).T


def vmem(n=1):
    return [pl.BlockSpec(memory_space=pltpu.VMEM)] * n


def shards(n_out, n_in, queries, keys, values, block_pos):
    tok, width = queries.shape
    size = width // HEADS
    chips = n_in // CORES
    both = CORES * tok
    params = pltpu.CompilerParams(vmem_limit_bytes=40 * 1024 * 1024)

    def along_inner(r, x):
        return [(w * CORES + c, (w ^ r) * CORES + (c ^ x)) for w in range(chips) for c in range(CORES)]

    def after(a, b):
        return lax.optimization_barrier((a, b))[0]

    with jax.named_scope("swap"):
        other = [lax.ppermute(a, "inner", along_inner(0, 1)) for a in (queries, keys, values, block_pos)]
        own = jnp.concatenate([queries, keys, values], axis=0)
    with jax.named_scope("merge"):
        smem = [pl.BlockSpec(memory_space=pltpu.SMEM)]
        q_piece, kv_piece = pl.pallas_call(
            merge_kernel,
            out_shape=(
                jax.ShapeDtypeStruct((PER * both + PAD, size), BF16),
                jax.ShapeDtypeStruct((2 * PER * both + PAD, size), BF16),
            ),
            in_specs=smem * 2 + vmem(4),
            out_specs=tuple(vmem(2)),
            compiler_params=params,
            name="merge",
        )(block_pos, other[3], own, *other[:3])
    half = PER * both + PAD
    block = PER * size + PAD

    def low(r):
        return r & -r

    def high(r):
        return 1 << (r.bit_length() - 1)

    def single(r):
        return r == low(r)

    def over(a, flips):
        pairs = [
            (o * n_in + w * CORES + c, (o ^ flips[c]) * n_in + w * CORES + c)
            for o in range(n_out)
            for w in range(chips)
            for c in range(CORES)
        ]
        return lax.ppermute(a, ("outer", "inner"), pairs)

    def pick(first, second):
        return pl.pallas_call(
            pick_kernel,
            out_shape=tuple(jax.ShapeDtypeStruct(a.shape, BF16) for a in first),
            in_specs=vmem(4),
            out_specs=tuple(vmem(2)),
            compiler_params=params,
            name="pick",
        )(*first, *second)

    with jax.named_scope("exchange"):
        whole = {r: over(kv_piece, (r, r)) if r else kv_piece for r in range(n_out) if single(r)}
        q_by = {0: q_piece}
        for r in sorted(range(1, chips), key=lambda r: (r != chips - 1, r)):
            piece = q_piece if r in (1, chips - 1) else after(q_piece, q_by[1])
            q_by[r] = lax.ppermute(piece, "inner", along_inner(r, 0))
        k_by = {r: a[:half, :] for r, a in whole.items() if r}
        v_by = {r: a[half:, :] for r, a in whole.items() if r}
        for r in sorted(range(1, n_out), key=lambda r: r.bit_count()):
            if not single(r):
                one, two = r - high(r), r - low(r)
                k, v = pick((k_by[one], v_by[one]), (k_by[two], v_by[two]))
                k_by[r] = over(k, (high(r), low(r)))
                v_by[r] = over(after(v, q_by[1]) if chips > 1 else v, (high(r), low(r)))
        ks = [whole[r] if r in whole else k_by[r] for r in range(n_out)]
        vs = [whole[r] if r in whole else v_by[r] for r in range(n_out)]
        rows = tuple(half if r in whole else 0 for r in range(n_out))

    def shapes(wide):
        rows = CORES * block if wide else block
        return (jax.ShapeDtypeStruct((rows, tok), BF16),) * (1 if wide else CORES)

    work = 2 * PER * both * n_out * both * size

    def score(r, done):
        with jax.named_scope("score"):
            return pl.pallas_call(
                functools.partial(score_kernel, r == 0),
                out_shape=(
                    jax.ShapeDtypeStruct((PER, n_out * both, both), BF16),
                    jax.ShapeDtypeStruct((PER * 8, both), F32),
                ),
                in_specs=vmem(1 + n_out),
                out_specs=tuple(vmem(2)),
                compiler_params=params,
                cost_estimate=pl.CostEstimate(flops=work, bytes_accessed=2**20, transcendentals=work // (2 * size)),
                name="score",
            )(q_by[r] if done is None else after(q_by[r], done), *ks)

    def apply(r, wide):
        with jax.named_scope("apply"):
            return pl.pallas_call(
                functools.partial(apply_kernel, wide, rows),
                out_shape=shapes(wide),
                in_specs=vmem(2 + n_out),
                out_specs=tuple(vmem(len(shapes(wide)))),
                compiler_params=params,
                cost_estimate=pl.CostEstimate(flops=work, bytes_accessed=2**20, transcendentals=0),
                name="apply",
            )(*weights_by[r], *vs)

    def add(arrays, wide):
        with jax.named_scope("add"):
            return pl.pallas_call(
                functools.partial(add_kernel, len(arrays), wide),
                out_shape=shapes(wide),
                in_specs=vmem(len(arrays)),
                out_specs=tuple(vmem(len(shapes(wide)))),
                compiler_params=params,
                name="add",
            )(*arrays)

    arrived = {r: [] for r in range(chips)}
    ends = []

    def send(r, parts):
        with jax.named_scope("return"):
            if single(r):
                ends.extend(lax.ppermute(parts[x], "inner", along_inner(r, x)) for x in range(CORES))
            else:
                arrived[r - low(r)].append(lax.ppermute(parts[0], "inner", along_inner(low(r), 0)))

    def both_kernels(r, done):
        weights_by[r] = score(r, done)
        partial[r] = apply(r, r > 1)
        return partial[r][0]

    done = None
    weights_by, partial = {}, {}
    for r in sorted(range(1, chips), key=lambda r: (r != chips - 1, r != 1, -r)):
        done = both_kernels(r, done)
    for r in reversed(range(2, chips)):
        parts = partial[r]
        if arrived[r]:
            parts = add([parts[0], *arrived[r]], not single(r))
            done = parts[0]
        send(r, parts)
    done = both_kernels(0, done)
    if chips > 1:
        send(1, [partial[1][0], after(partial[1][1], done)])
    with jax.named_scope("return"):
        ends = [partial[0][0], lax.ppermute(partial[0][1], "inner", along_inner(0, 1))] + ends
    with jax.named_scope("combine"):
        return pl.pallas_call(
            functools.partial(combine_kernel, len(ends)),
            out_shape=jax.ShapeDtypeStruct((tok, width), BF16),
            in_specs=vmem(len(ends)),
            out_specs=vmem()[0],
            compiler_params=params,
            name="combine",
        )(*ends)


def solution(mesh):
    n_out, n_in = mesh.shape["outer"], mesh.shape["inner"]
    return jax.shard_map(
        functools.partial(shards, n_out, n_in),
        mesh=mesh,
        in_specs=(
            P(("outer", "inner"), None),
            P(("outer", "inner"), None),
            P(("outer", "inner"), None),
            P(("outer", "inner")),
        ),
        out_specs=P(("outer", "inner"), None),
        check_vma=False,
    )
```

```python
import functools
import math

import jax
import jax.numpy as jnp
from jax import lax
from jax.experimental import pallas as pl
from jax.experimental.pallas import tpu as pltpu
from jax.sharding import PartitionSpec as P

HEADS = 4
CORES = 2
PER = HEADS // CORES
PAD = 16
LOW = -1e30
FLOOR = -1e29
BF16 = jnp.bfloat16
F32 = jnp.float32


def nt_dot(a, b):
    return lax.dot_general(a, b, (((1,), (1,)), ((), ())), preferred_element_type=F32)


def place(own, other, out, at, turned=False):
    tok = own.shape[0]
    size = own.shape[1] // HEADS
    core = lax.rem(lax.axis_index("inner"), CORES)
    for b, ref in enumerate((own, other)):
        for j in range(PER):
            piece = ref[:, pl.ds(pl.multiple_of((core * PER + j) * size, size), size)]
            if turned:
                piece = piece.T
            row = at + j * CORES * tok + b * tok
            out[row : row + tok, :] = piece


def starts(p0, p1):
    half = PAD // CORES
    return jnp.concatenate([p[...].astype(F32)[0:half, :] for p in (p0, p1)], axis=0).astype(BF16)


def merge_kernel(p0, p1, own, q1, k1, v1, q_out, kv_out):
    tok = q1.shape[0]
    rows = PER * CORES * tok
    pos = starts(p0, p1)
    place(own.at[0:tok, :], q1, q_out, 0)
    q_out[rows:, :] = pos
    place(own.at[tok : 2 * tok, :], k1, kv_out, 0)
    kv_out[rows : rows + PAD, :] = pos
    place(own.at[2 * tok : 3 * tok, :], v1, kv_out, rows + PAD, turned=True)


def score_kernel(same, q_ref, *refs):
    k_refs, (p_ref, top_ref) = refs[:-2], refs[-2:]
    size = q_ref.shape[1]
    tok = size
    both = CORES * tok
    half = PAD // CORES
    rate = size ** -0.5 * math.log2(math.e)
    at_or_before = lax.broadcasted_iota(jnp.int32, (tok, tok), 0) <= lax.broadcasted_iota(jnp.int32, (tok, tok), 1)

    def block_of(ref):
        first = ref[PER * both : PER * both + PAD, :].astype(F32)
        return [first[b * half : b * half + 1, :] for b in range(CORES)]

    q_block = jnp.concatenate(block_of(q_ref), axis=1)
    kept = [jnp.concatenate([p] * CORES, axis=1) <= q_block for ref in k_refs for p in block_of(ref)]
    for h in range(PER):
        q = q_ref[h * both : (h + 1) * both, :]
        scores = []
        for j, ref in enumerate(k_refs):
            s = nt_dot(ref[h * both : (h + 1) * both, :], q)
            for b in range(CORES):
                part = s[b * tok : (b + 1) * tok, :]
                if same and j == 0:
                    cols = [part[:, c * tok : (c + 1) * tok] for c in range(CORES)]
                    cols[b] = jnp.where(at_or_before, cols[b], LOW)
                    part = jnp.concatenate(cols, axis=1)
                scores.append(part)
        tops = [jnp.where(k, jnp.max(s, axis=0, keepdims=True), FLOOR) for k, s in zip(kept, scores)]
        top = jnp.maximum(functools.reduce(jnp.maximum, tops), FLOOR).astype(BF16).astype(F32)
        for i, (k, s) in enumerate(zip(kept, scores)):
            p_ref[h, i * tok : (i + 1) * tok, :] = jnp.exp2((s - jnp.where(k, top, -LOW)) * rate).astype(BF16)
        top_ref[h * 8 : (h + 1) * 8, :] = jnp.broadcast_to(top, (8, both))


def apply_kernel(wide, rows, p_ref, top_ref, *refs):
    nv = len(refs) - (1 if wide else CORES)
    v_refs, out_refs = refs[:nv], refs[nv:]
    size = v_refs[0].shape[1]
    tok = size
    both = CORES * tok
    block = PER * size + PAD

    def store(b, at, value):
        if wide:
            out_refs[0][b * block + at : b * block + at + value.shape[0], :] = value
        else:
            out_refs[b][at : at + value.shape[0], :] = value

    stats = [[] for _ in range(CORES)]
    for h in range(PER):
        vals = []
        for ref, row in zip(v_refs, rows):
            for b in range(CORES):
                at = row + h * both + b * tok
                vals.append(ref[at : at + tok, :])
        vt = jnp.concatenate(vals, axis=1)
        vt = jnp.concatenate([vt, jnp.ones((PAD, vt.shape[1]), BF16)], axis=0)
        o = jnp.dot(vt, p_ref[h], preferred_element_type=F32)
        total = o[size : size + 1, :]
        hi = total.astype(BF16).astype(F32)
        top = top_ref[h * 8 : h * 8 + 1, :]
        for b in range(CORES):
            cols = slice(b * tok, (b + 1) * tok)
            store(b, h * size, o[0:size, cols].astype(BF16))
            stats[b] += [top[:, cols], hi[:, cols], (total - hi)[:, cols]]
    for b in range(CORES):
        rest = jnp.zeros((PAD - 3 * PER, tok), F32)
        store(b, PER * size, jnp.concatenate(stats[b] + [rest], axis=0).astype(BF16))


def joined(parts, stats, h, rate):
    size = parts[0].shape[0]
    tops = [s[3 * h : 3 * h + 1, :] for s in stats]
    best = functools.reduce(jnp.maximum, tops)
    factors = [jnp.exp2((t - best) * rate) for t in tops]
    total = sum(f * (s[3 * h + 1 : 3 * h + 2, :] + s[3 * h + 2 : 3 * h + 3, :]) for f, s in zip(factors, stats))
    numer = sum(f * part.astype(F32) for f, part in zip(factors, parts))
    return best, total, numer


def add_kernel(n, wide, *refs):
    size = refs[0].shape[1]
    block = PER * size + PAD
    rate = size ** -0.5 * math.log2(math.e)
    for b in range(CORES):
        base = b * block
        stats = [ref[base + PER * size : base + block, :].astype(F32) for ref in refs[:n]]
        out, at = (refs[n], base) if wide else (refs[n + b], 0)
        rows = []
        for h in range(PER):
            parts = [ref[base + h * size : base + (h + 1) * size, :] for ref in refs[:n]]
            best, total, numer = joined(parts, stats, h, rate)
            hi = total.astype(BF16).astype(F32)
            rows += [best, hi, total - hi]
            out[at + h * size : at + (h + 1) * size, :] = numer.astype(BF16)
        rest = jnp.zeros((PAD - 3 * PER, size), F32)
        out[at + PER * size : at + block, :] = jnp.concatenate(rows + [rest], axis=0).astype(BF16)


def combine_kernel(n, *refs):
    parts, out_ref = refs[:n], refs[n]
    size = parts[0].shape[1]
    rate = size ** -0.5 * math.log2(math.e)
    core = lax.rem(lax.axis_index("inner"), CORES)
    for x in range(CORES):
        mine = parts[x::CORES]
        pair = jnp.bitwise_xor(core, x)
        stats = [part[PER * size :, :].astype(F32) for part in mine]
        for h in range(PER):
            _, total, numer = joined([part[h * size : (h + 1) * size, :] for part in mine], stats, h, rate)
            cols = pl.ds(pl.multiple_of((pair * PER + h) * size, size), size)
            out_ref[:, cols] = (numer * (1.0 / total)).astype(BF16).T


def vmem(n=1):
    return [pl.BlockSpec(memory_space=pltpu.VMEM)] * n


def shards(n_out, n_in, queries, keys, values, block_pos):
    tok, width = queries.shape
    size = width // HEADS
    chips = n_in // CORES
    both = CORES * tok
    params = pltpu.CompilerParams(vmem_limit_bytes=40 * 1024 * 1024)

    def along_inner(r, x):
        return [(w * CORES + c, (w ^ r) * CORES + (c ^ x)) for w in range(chips) for c in range(CORES)]

    def after(a, b):
        return lax.optimization_barrier((a, b))[0]

    with jax.named_scope("swap"):
        here = jnp.broadcast_to(block_pos.astype(BF16)[:, None], (PAD, size))
        other = [lax.ppermute(a, "inner", along_inner(0, 1)) for a in (queries, keys, values, here)]
        own = jnp.concatenate([queries, keys, values], axis=0)
    with jax.named_scope("merge"):
        q_piece, kv_piece = pl.pallas_call(
            merge_kernel,
            out_shape=(
                jax.ShapeDtypeStruct((PER * both + PAD, size), BF16),
                jax.ShapeDtypeStruct((2 * PER * both + PAD, size), BF16),
            ),
            in_specs=vmem(6),
            out_specs=tuple(vmem(2)),
            compiler_params=params,
            name="merge",
        )(here, other[3], own, *other[:3])
    half = PER * both + PAD
    block = PER * size + PAD

    def low(r):
        return r & -r

    def high(r):
        return 1 << (r.bit_length() - 1)

    def single(r):
        return r == low(r)

    def over(a, r):
        return lax.ppermute(a, "outer", [(o, o ^ r) for o in range(n_out)])

    with jax.named_scope("exchange"):
        whole = {r: over(kv_piece, r) if r else kv_piece for r in range(n_out) if single(r)}
        q_by = {0: q_piece}
        for r in sorted(range(1, chips), key=lambda r: (r != chips - 1, r)):
            piece = q_piece if r in (1, chips - 1) else after(q_piece, q_by[1])
            q_by[r] = lax.ppermute(piece, "inner", along_inner(r, 0))
        k_by = {r: a[:half, :] for r, a in whole.items() if r}
        v_by = {r: a[half:, :] for r, a in whole.items() if r}
        for r in range(1, n_out):
            if not single(r):
                k_by[r] = over(k_by[r - high(r)], high(r))
        for r in sorted(range(1, n_out), key=lambda r: r.bit_count()):
            if not single(r):
                v_by[r] = over(v_by[r - low(r)], low(r))
        ks = [whole[r] if r in whole else k_by[r] for r in range(n_out)]
        vs = [whole[r] if r in whole else v_by[r] for r in range(n_out)]
        rows = tuple(half if r in whole else 0 for r in range(n_out))

    def shapes(wide):
        rows = CORES * block if wide else block
        return (jax.ShapeDtypeStruct((rows, tok), BF16),) * (1 if wide else CORES)

    work = 2 * PER * both * n_out * both * size

    def score(r, done):
        with jax.named_scope("score"):
            return pl.pallas_call(
                functools.partial(score_kernel, r == 0),
                out_shape=(
                    jax.ShapeDtypeStruct((PER, n_out * both, both), BF16),
                    jax.ShapeDtypeStruct((PER * 8, both), F32),
                ),
                in_specs=vmem(1 + n_out),
                out_specs=tuple(vmem(2)),
                compiler_params=params,
                cost_estimate=pl.CostEstimate(flops=work, bytes_accessed=2**20, transcendentals=work // (2 * size)),
                name="score",
            )(q_by[r] if done is None else after(q_by[r], done), *ks)

    def apply(r, wide):
        with jax.named_scope("apply"):
            return pl.pallas_call(
                functools.partial(apply_kernel, wide, rows),
                out_shape=shapes(wide),
                in_specs=vmem(2 + n_out),
                out_specs=tuple(vmem(len(shapes(wide)))),
                compiler_params=params,
                cost_estimate=pl.CostEstimate(flops=work, bytes_accessed=2**20, transcendentals=0),
                name="apply",
            )(*weights_by[r], *vs)

    def add(arrays, wide):
        with jax.named_scope("add"):
            return pl.pallas_call(
                functools.partial(add_kernel, len(arrays), wide),
                out_shape=shapes(wide),
                in_specs=vmem(len(arrays)),
                out_specs=tuple(vmem(len(shapes(wide)))),
                compiler_params=params,
                name="add",
            )(*arrays)

    arrived = {r: [] for r in range(chips)}
    ends = []

    def send(r, parts):
        with jax.named_scope("return"):
            if single(r):
                ends.extend(lax.ppermute(parts[x], "inner", along_inner(r, x)) for x in range(CORES))
            else:
                arrived[r - low(r)].append(lax.ppermute(parts[0], "inner", along_inner(low(r), 0)))

    def both_kernels(r, done):
        weights_by[r] = score(r, done)
        partial[r] = apply(r, r > 1)
        return partial[r][0]

    done = None
    weights_by, partial = {}, {}
    for r in sorted(range(1, chips), key=lambda r: (r != chips - 1, r != 1, -r)):
        done = both_kernels(r, done)
    for r in reversed(range(2, chips)):
        parts = partial[r]
        if arrived[r]:
            parts = add([parts[0], *arrived[r]], not single(r))
            done = parts[0]
        send(r, parts)
    done = both_kernels(0, done)
    if chips > 1:
        send(1, [partial[1][0], after(partial[1][1], done)])
    with jax.named_scope("return"):
        ends = [partial[0][0], lax.ppermute(partial[0][1], "inner", along_inner(0, 1))] + ends
    with jax.named_scope("combine"):
        return pl.pallas_call(
            functools.partial(combine_kernel, len(ends)),
            out_shape=jax.ShapeDtypeStruct((tok, width), BF16),
            in_specs=vmem(len(ends)),
            out_specs=vmem()[0],
            compiler_params=params,
            name="combine",
        )(*ends)


def solution(mesh):
    n_out, n_in = mesh.shape["outer"], mesh.shape["inner"]
    return jax.shard_map(
        functools.partial(shards, n_out, n_in),
        mesh=mesh,
        in_specs=(
            P(("outer", "inner"), None),
            P(("outer", "inner"), None),
            P(("outer", "inner"), None),
            P(("outer", "inner")),
        ),
        out_specs=P(("outer", "inner"), None),
        check_vma=False,
    )
```

```python
import functools
import math

import jax
import jax.numpy as jnp
from jax import lax
from jax.experimental import pallas as pl
from jax.experimental.pallas import tpu as pltpu
from jax.sharding import PartitionSpec as P

HEADS = 4
CORES = 2
PER = HEADS // CORES
PAD = 16
LOW = -1e30
FLOOR = -1e29
BF16 = jnp.bfloat16
F32 = jnp.float32


def nt_dot(a, b):
    return lax.dot_general(a, b, (((1,), (1,)), ((), ())), preferred_element_type=F32)


def place(own, other, out, at, turned=False):
    tok = own.shape[0]
    size = own.shape[1] // HEADS
    core = lax.rem(lax.axis_index("inner"), CORES)
    for b, ref in enumerate((own, other)):
        for j in range(PER):
            piece = ref[:, pl.ds(pl.multiple_of((core * PER + j) * size, size), size)]
            if turned:
                piece = piece.T
            row = at + j * CORES * tok + b * tok
            out[row : row + tok, :] = piece


def starts(p0, p1):
    half = PAD // CORES
    return jnp.concatenate([p[...].astype(F32)[0:half, :] for p in (p0, p1)], axis=0).astype(BF16)


def merge_kernel(p0, p1, own, q1, k1, v1, q_out, kv_out):
    tok, width = q1.shape
    rows = PER * CORES * tok
    pos = starts(p0, p1)
    place(own.at[:, 0:width], q1, q_out, 0)
    q_out[rows:, :] = pos
    place(own.at[:, width : 2 * width], k1, kv_out, 0)
    kv_out[rows : rows + PAD, :] = pos
    place(own.at[:, 2 * width : 3 * width], v1, kv_out, rows + PAD, turned=True)


def score_kernel(same, q_ref, *refs):
    k_refs, (p_ref, top_ref) = refs[:-2], refs[-2:]
    size = q_ref.shape[1]
    tok = size
    both = CORES * tok
    half = PAD // CORES
    rate = size ** -0.5 * math.log2(math.e)
    at_or_before = lax.broadcasted_iota(jnp.int32, (tok, tok), 0) <= lax.broadcasted_iota(jnp.int32, (tok, tok), 1)

    def block_of(ref):
        first = ref[PER * both : PER * both + PAD, :].astype(F32)
        return [first[b * half : b * half + 1, :] for b in range(CORES)]

    q_block = jnp.concatenate(block_of(q_ref), axis=1)
    kept = [jnp.concatenate([p] * CORES, axis=1) <= q_block for ref in k_refs for p in block_of(ref)]
    for h in range(PER):
        q = q_ref[h * both : (h + 1) * both, :]
        scores = []
        for j, ref in enumerate(k_refs):
            s = nt_dot(ref[h * both : (h + 1) * both, :], q)
            for b in range(CORES):
                part = s[b * tok : (b + 1) * tok, :]
                if same and j == 0:
                    cols = [part[:, c * tok : (c + 1) * tok] for c in range(CORES)]
                    cols[b] = jnp.where(at_or_before, cols[b], LOW)
                    part = jnp.concatenate(cols, axis=1)
                scores.append(part)
        tops = [jnp.where(k, jnp.max(s, axis=0, keepdims=True), FLOOR) for k, s in zip(kept, scores)]
        top = jnp.maximum(functools.reduce(jnp.maximum, tops), FLOOR).astype(BF16).astype(F32)
        for i, (k, s) in enumerate(zip(kept, scores)):
            p_ref[h, i * tok : (i + 1) * tok, :] = jnp.exp2((s - jnp.where(k, top, -LOW)) * rate).astype(BF16)
        top_ref[h * 8 : (h + 1) * 8, :] = jnp.broadcast_to(top, (8, both))


def apply_kernel(wide, rows, p_ref, top_ref, *refs):
    nv = len(refs) - (1 if wide else CORES)
    v_refs, out_refs = refs[:nv], refs[nv:]
    size = v_refs[0].shape[1]
    tok = size
    both = CORES * tok
    block = PER * size + PAD

    def store(b, at, value):
        if wide:
            out_refs[0][b * block + at : b * block + at + value.shape[0], :] = value
        else:
            out_refs[b][at : at + value.shape[0], :] = value

    stats = [[] for _ in range(CORES)]
    for h in range(PER):
        vals = []
        for ref, row in zip(v_refs, rows):
            for b in range(CORES):
                at = row + h * both + b * tok
                vals.append(ref[at : at + tok, :])
        vt = jnp.concatenate(vals, axis=1)
        vt = jnp.concatenate([vt, jnp.ones((PAD, vt.shape[1]), BF16)], axis=0)
        o = jnp.dot(vt, p_ref[h], preferred_element_type=F32)
        total = o[size : size + 1, :]
        hi = total.astype(BF16).astype(F32)
        top = top_ref[h * 8 : h * 8 + 1, :]
        for b in range(CORES):
            cols = slice(b * tok, (b + 1) * tok)
            store(b, h * size, o[0:size, cols].astype(BF16))
            stats[b] += [top[:, cols], hi[:, cols], (total - hi)[:, cols]]
    for b in range(CORES):
        rest = jnp.zeros((PAD - 3 * PER, tok), F32)
        store(b, PER * size, jnp.concatenate(stats[b] + [rest], axis=0).astype(BF16))


def joined(parts, stats, h, rate):
    size = parts[0].shape[0]
    tops = [s[3 * h : 3 * h + 1, :] for s in stats]
    best = functools.reduce(jnp.maximum, tops)
    factors = [jnp.exp2((t - best) * rate) for t in tops]
    total = sum(f * (s[3 * h + 1 : 3 * h + 2, :] + s[3 * h + 2 : 3 * h + 3, :]) for f, s in zip(factors, stats))
    numer = sum(f * part.astype(F32) for f, part in zip(factors, parts))
    return best, total, numer


def add_kernel(n, wide, *refs):
    size = refs[0].shape[1]
    block = PER * size + PAD
    rate = size ** -0.5 * math.log2(math.e)
    for b in range(CORES):
        base = b * block
        stats = [ref[base + PER * size : base + block, :].astype(F32) for ref in refs[:n]]
        out, at = (refs[n], base) if wide else (refs[n + b], 0)
        rows = []
        for h in range(PER):
            parts = [ref[base + h * size : base + (h + 1) * size, :] for ref in refs[:n]]
            best, total, numer = joined(parts, stats, h, rate)
            hi = total.astype(BF16).astype(F32)
            rows += [best, hi, total - hi]
            out[at + h * size : at + (h + 1) * size, :] = numer.astype(BF16)
        rest = jnp.zeros((PAD - 3 * PER, size), F32)
        out[at + PER * size : at + block, :] = jnp.concatenate(rows + [rest], axis=0).astype(BF16)


def combine_kernel(n, *refs):
    parts, out_ref = refs[:n], refs[n]
    size = parts[0].shape[1]
    rate = size ** -0.5 * math.log2(math.e)
    core = lax.rem(lax.axis_index("inner"), CORES)
    for x in range(CORES):
        mine = parts[x::CORES]
        pair = jnp.bitwise_xor(core, x)
        stats = [part[PER * size :, :].astype(F32) for part in mine]
        for h in range(PER):
            _, total, numer = joined([part[h * size : (h + 1) * size, :] for part in mine], stats, h, rate)
            cols = pl.ds(pl.multiple_of((pair * PER + h) * size, size), size)
            out_ref[:, cols] = (numer * (1.0 / total)).astype(BF16).T


def vmem(n=1):
    return [pl.BlockSpec(memory_space=pltpu.VMEM)] * n


def shards(n_out, n_in, queries, keys, values, block_pos):
    tok, width = queries.shape
    size = width // HEADS
    chips = n_in // CORES
    both = CORES * tok
    params = pltpu.CompilerParams(vmem_limit_bytes=40 * 1024 * 1024)

    def along_inner(r, x):
        return [(w * CORES + c, (w ^ r) * CORES + (c ^ x)) for w in range(chips) for c in range(CORES)]

    def after(a, b):
        return lax.optimization_barrier((a, b))[0]

    with jax.named_scope("swap"):
        here = jnp.broadcast_to(block_pos.astype(BF16)[:, None], (PAD, size))
        other = [lax.ppermute(a, "inner", along_inner(0, 1)) for a in (queries, keys, values, here)]
        own = jnp.concatenate([queries, keys, values], axis=1)
    with jax.named_scope("merge"):
        q_piece, kv_piece = pl.pallas_call(
            merge_kernel,
            out_shape=(
                jax.ShapeDtypeStruct((PER * both + PAD, size), BF16),
                jax.ShapeDtypeStruct((2 * PER * both + PAD, size), BF16),
            ),
            in_specs=vmem(6),
            out_specs=tuple(vmem(2)),
            compiler_params=params,
            name="merge",
        )(here, other[3], own, *other[:3])
    half = PER * both + PAD
    block = PER * size + PAD

    def low(r):
        return r & -r

    def high(r):
        return 1 << (r.bit_length() - 1)

    def single(r):
        return r == low(r)

    def over(a, r):
        return lax.ppermute(a, "outer", [(o, o ^ r) for o in range(n_out)])

    with jax.named_scope("exchange"):
        whole = {r: over(kv_piece, r) if r else kv_piece for r in range(n_out) if single(r)}
        q_by = {0: q_piece}
        for r in sorted(range(1, chips), key=lambda r: (r != chips - 1, r)):
            piece = q_piece if r in (1, chips - 1) else after(q_piece, q_by[1])
            q_by[r] = lax.ppermute(piece, "inner", along_inner(r, 0))
        k_by = {r: a[:half, :] for r, a in whole.items() if r}
        v_by = {r: a[half:, :] for r, a in whole.items() if r}
        for r in range(1, n_out):
            if not single(r):
                k_by[r] = over(k_by[r - high(r)], high(r))
        for r in sorted(range(1, n_out), key=lambda r: r.bit_count()):
            if not single(r):
                v_by[r] = over(v_by[r - low(r)], low(r))
        ks = [whole[r] if r in whole else k_by[r] for r in range(n_out)]
        vs = [whole[r] if r in whole else v_by[r] for r in range(n_out)]
        rows = tuple(half if r in whole else 0 for r in range(n_out))

    def shapes(wide):
        rows = CORES * block if wide else block
        return (jax.ShapeDtypeStruct((rows, tok), BF16),) * (1 if wide else CORES)

    work = 2 * PER * both * n_out * both * size

    def score(r, done):
        with jax.named_scope("score"):
            return pl.pallas_call(
                functools.partial(score_kernel, r == 0),
                out_shape=(
                    jax.ShapeDtypeStruct((PER, n_out * both, both), BF16),
                    jax.ShapeDtypeStruct((PER * 8, both), F32),
                ),
                in_specs=vmem(1 + n_out),
                out_specs=tuple(vmem(2)),
                compiler_params=params,
                cost_estimate=pl.CostEstimate(flops=work, bytes_accessed=2**20, transcendentals=work // (2 * size)),
                name="score",
            )(q_by[r] if done is None else after(q_by[r], done), *ks)

    def apply(r, wide):
        with jax.named_scope("apply"):
            return pl.pallas_call(
                functools.partial(apply_kernel, wide, rows),
                out_shape=shapes(wide),
                in_specs=vmem(2 + n_out),
                out_specs=tuple(vmem(len(shapes(wide)))),
                compiler_params=params,
                cost_estimate=pl.CostEstimate(flops=work, bytes_accessed=2**20, transcendentals=0),
                name="apply",
            )(*weights_by[r], *vs)

    def add(arrays, wide):
        with jax.named_scope("add"):
            return pl.pallas_call(
                functools.partial(add_kernel, len(arrays), wide),
                out_shape=shapes(wide),
                in_specs=vmem(len(arrays)),
                out_specs=tuple(vmem(len(shapes(wide)))),
                compiler_params=params,
                name="add",
            )(*arrays)

    arrived = {r: [] for r in range(chips)}
    ends = []

    def send(r, parts):
        with jax.named_scope("return"):
            if single(r):
                ends.extend(lax.ppermute(parts[x], "inner", along_inner(r, x)) for x in range(CORES))
            else:
                arrived[r - low(r)].append(lax.ppermute(parts[0], "inner", along_inner(low(r), 0)))

    def both_kernels(r, done):
        weights_by[r] = score(r, done)
        partial[r] = apply(r, r > 1)
        return partial[r][0]

    done = None
    weights_by, partial = {}, {}
    for r in sorted(range(1, chips), key=lambda r: (r != chips - 1, r != 1, -r)):
        done = both_kernels(r, done)
    for r in reversed(range(2, chips)):
        parts = partial[r]
        if arrived[r]:
            parts = add([parts[0], *arrived[r]], not single(r))
            done = parts[0]
        send(r, parts)
    done = both_kernels(0, done)
    if chips > 1:
        send(1, [partial[1][0], after(partial[1][1], done)])
    with jax.named_scope("return"):
        ends = [partial[0][0], lax.ppermute(partial[0][1], "inner", along_inner(0, 1))] + ends
    with jax.named_scope("combine"):
        return pl.pallas_call(
            functools.partial(combine_kernel, len(ends)),
            out_shape=jax.ShapeDtypeStruct((tok, width), BF16),
            in_specs=vmem(len(ends)),
            out_specs=vmem()[0],
            compiler_params=params,
            name="combine",
        )(*ends)


def solution(mesh):
    n_out, n_in = mesh.shape["outer"], mesh.shape["inner"]
    return jax.shard_map(
        functools.partial(shards, n_out, n_in),
        mesh=mesh,
        in_specs=(
            P(("outer", "inner"), None),
            P(("outer", "inner"), None),
            P(("outer", "inner"), None),
            P(("outer", "inner")),
        ),
        out_specs=P(("outer", "inner"), None),
        check_vma=False,
    )
```

```python
import functools
import math

import jax
import jax.numpy as jnp
from jax import lax
from jax.experimental import pallas as pl
from jax.experimental.pallas import tpu as pltpu
from jax.sharding import PartitionSpec as P

HEADS = 4
CORES = 2
PER = HEADS // CORES
PAD = 16
LOW = -1e30
FLOOR = -1e29
BF16 = jnp.bfloat16
F32 = jnp.float32


def nt_dot(a, b):
    return lax.dot_general(a, b, (((1,), (1,)), ((), ())), preferred_element_type=F32)


def place(own, other, out, at, turned=False):
    tok = own.shape[0]
    size = own.shape[1] // HEADS
    core = lax.rem(lax.axis_index("inner"), CORES)
    for b, ref in enumerate((own, other)):
        for j in range(PER):
            piece = ref[:, pl.ds(pl.multiple_of((core * PER + j) * size, size), size)]
            if turned:
                piece = piece.T
            row = at + j * CORES * tok + b * tok
            out[row : row + tok, :] = piece


def starts(p0, p1):
    half = PAD // CORES
    return jnp.concatenate([p[...].astype(F32)[0:half, :] for p in (p0, p1)], axis=0).astype(BF16)


def merge_kernel(p0, p1, own, q1, k1, v1, q_out, kv_out):
    tok = q1.shape[0]
    rows = PER * CORES * tok
    pos = starts(p0, p1)
    place(own.at[0:tok, :], q1, q_out, 0)
    q_out[rows:, :] = pos
    place(own.at[tok : 2 * tok, :], k1, kv_out, 0)
    kv_out[rows : rows + PAD, :] = pos
    place(own.at[2 * tok : 3 * tok, :], v1, kv_out, rows + PAD, turned=True)


def score_kernel(same, q_ref, *refs):
    k_refs, (p_ref, top_ref) = refs[:-2], refs[-2:]
    size = q_ref.shape[1]
    tok = size
    both = CORES * tok
    half = PAD // CORES
    rate = size ** -0.5 * math.log2(math.e)
    at_or_before = lax.broadcasted_iota(jnp.int32, (tok, tok), 0) <= lax.broadcasted_iota(jnp.int32, (tok, tok), 1)

    def block_of(ref):
        first = ref[PER * both : PER * both + PAD, :].astype(F32)
        return [first[b * half : b * half + 1, :] for b in range(CORES)]

    q_block = jnp.concatenate(block_of(q_ref), axis=1)
    kept = [jnp.concatenate([p] * CORES, axis=1) <= q_block for ref in k_refs for p in block_of(ref)]
    for h in range(PER):
        q = q_ref[h * both : (h + 1) * both, :]
        scores = []
        for j, ref in enumerate(k_refs):
            s = nt_dot(ref[h * both : (h + 1) * both, :], q)
            for b in range(CORES):
                part = s[b * tok : (b + 1) * tok, :]
                if same and j == 0:
                    cols = [part[:, c * tok : (c + 1) * tok] for c in range(CORES)]
                    cols[b] = jnp.where(at_or_before, cols[b], LOW)
                    part = jnp.concatenate(cols, axis=1)
                scores.append(part)
        tops = [jnp.where(k, jnp.max(s, axis=0, keepdims=True), FLOOR) for k, s in zip(kept, scores)]
        top = jnp.maximum(functools.reduce(jnp.maximum, tops), FLOOR).astype(BF16).astype(F32)
        for i, (k, s) in enumerate(zip(kept, scores)):
            p_ref[h, i * tok : (i + 1) * tok, :] = jnp.exp2((s - jnp.where(k, top, -LOW)) * rate).astype(BF16)
        top_ref[h * 8 : (h + 1) * 8, :] = jnp.broadcast_to(top, (8, both))


def apply_kernel(wide, rows, p_ref, top_ref, *refs):
    nv = len(refs) - (1 if wide else CORES)
    v_refs, out_refs = refs[:nv], refs[nv:]
    size = v_refs[0].shape[1]
    tok = size
    both = CORES * tok
    block = PER * size + PAD

    def store(b, at, value):
        if wide:
            out_refs[0][b * block + at : b * block + at + value.shape[0], :] = value
        else:
            out_refs[b][at : at + value.shape[0], :] = value

    stats = [[] for _ in range(CORES)]
    for h in range(PER):
        vals = []
        for ref, row in zip(v_refs, rows):
            for b in range(CORES):
                at = row + h * both + b * tok
                vals.append(ref[at : at + tok, :])
        vt = jnp.concatenate(vals, axis=1)
        vt = jnp.concatenate([vt, jnp.ones((PAD, vt.shape[1]), BF16)], axis=0)
        o = jnp.dot(vt, p_ref[h], preferred_element_type=F32)
        total = o[size : size + 1, :]
        hi = total.astype(BF16).astype(F32)
        top = top_ref[h * 8 : h * 8 + 1, :]
        for b in range(CORES):
            cols = slice(b * tok, (b + 1) * tok)
            store(b, h * size, o[0:size, cols].astype(BF16))
            stats[b] += [top[:, cols], hi[:, cols], (total - hi)[:, cols]]
    for b in range(CORES):
        rest = jnp.zeros((PAD - 3 * PER, tok), F32)
        store(b, PER * size, jnp.concatenate(stats[b] + [rest], axis=0).astype(BF16))


def joined(parts, stats, h, rate):
    size = parts[0].shape[0]
    tops = [s[3 * h : 3 * h + 1, :] for s in stats]
    best = functools.reduce(jnp.maximum, tops)
    factors = [jnp.exp2((t - best) * rate) for t in tops]
    total = sum(f * (s[3 * h + 1 : 3 * h + 2, :] + s[3 * h + 2 : 3 * h + 3, :]) for f, s in zip(factors, stats))
    numer = sum(f * part.astype(F32) for f, part in zip(factors, parts))
    return best, total, numer


def add_kernel(n, wide, *refs):
    size = refs[0].shape[1]
    block = PER * size + PAD
    rate = size ** -0.5 * math.log2(math.e)
    for b in range(CORES):
        base = b * block
        stats = [ref[base + PER * size : base + block, :].astype(F32) for ref in refs[:n]]
        out, at = (refs[n], base) if wide else (refs[n + b], 0)
        rows = []
        for h in range(PER):
            parts = [ref[base + h * size : base + (h + 1) * size, :] for ref in refs[:n]]
            best, total, numer = joined(parts, stats, h, rate)
            hi = total.astype(BF16).astype(F32)
            rows += [best, hi, total - hi]
            out[at + h * size : at + (h + 1) * size, :] = numer.astype(BF16)
        rest = jnp.zeros((PAD - 3 * PER, size), F32)
        out[at + PER * size : at + block, :] = jnp.concatenate(rows + [rest], axis=0).astype(BF16)


def combine_kernel(n, *refs):
    parts, out_ref = refs[:n], refs[n]
    size = parts[0].shape[1]
    rate = size ** -0.5 * math.log2(math.e)
    core = lax.rem(lax.axis_index("inner"), CORES)
    for x in range(CORES):
        mine = parts[x::CORES]
        pair = jnp.bitwise_xor(core, x)
        stats = [part[PER * size :, :].astype(F32) for part in mine]
        for h in range(PER):
            _, total, numer = joined([part[h * size : (h + 1) * size, :] for part in mine], stats, h, rate)
            cols = pl.ds(pl.multiple_of((pair * PER + h) * size, size), size)
            out_ref[:, cols] = (numer * (1.0 / total)).astype(BF16).T


def vmem(n=1):
    return [pl.BlockSpec(memory_space=pltpu.VMEM)] * n


def shards(n_out, n_in, queries, keys, values, block_pos):
    tok, width = queries.shape
    size = width // HEADS
    chips = n_in // CORES
    both = CORES * tok
    params = pltpu.CompilerParams(vmem_limit_bytes=40 * 1024 * 1024)

    def along_inner(r, x):
        return [(w * CORES + c, (w ^ r) * CORES + (c ^ x)) for w in range(chips) for c in range(CORES)]

    def after(a, b):
        return lax.optimization_barrier((a, b))[0]

    with jax.named_scope("swap"):
        here = jnp.broadcast_to(block_pos.astype(BF16)[:, None], (PAD, size))
        other = [lax.ppermute(a, "inner", along_inner(0, 1)) for a in (queries, keys, values, here)]
        own = jnp.concatenate([queries, keys, values], axis=0)
    with jax.named_scope("merge"):
        q_piece, kv_piece = pl.pallas_call(
            merge_kernel,
            out_shape=(
                jax.ShapeDtypeStruct((PER * both + PAD, size), BF16),
                jax.ShapeDtypeStruct((2 * PER * both + PAD, size), BF16),
            ),
            in_specs=vmem(6),
            out_specs=tuple(vmem(2)),
            compiler_params=params,
            name="merge",
        )(here, other[3], own, *other[:3])
    half = PER * both + PAD
    block = PER * size + PAD

    def low(r):
        return r & -r

    def high(r):
        return 1 << (r.bit_length() - 1)

    def single(r):
        return r == low(r)

    def over(a, r):
        return lax.ppermute(a, "outer", [(o, o ^ r) for o in range(n_out)])

    with jax.named_scope("exchange"):
        whole = {r: over(kv_piece, r) if r else kv_piece for r in range(n_out) if single(r)}
        q_by = {0: q_piece}
        for r in sorted(range(1, chips), key=lambda r: (r != chips - 1, r)):
            piece = q_piece if r in (1, chips - 1) else after(q_piece, q_by[1])
            q_by[r] = lax.ppermute(piece, "inner", along_inner(r, 0))
        k_by = {r: a[:half, :] for r, a in whole.items() if r}
        v_by = {r: a[half:, :] for r, a in whole.items() if r}
        for r in range(1, n_out):
            if not single(r):
                k_by[r] = over(k_by[r - high(r)], high(r))
        for r in sorted(range(1, n_out), key=lambda r: r.bit_count()):
            if not single(r):
                v_by[r] = over(v_by[r - low(r)], low(r))
        ks = [whole[r] if r in whole else k_by[r] for r in range(n_out)]
        vs = [whole[r] if r in whole else v_by[r] for r in range(n_out)]
        rows = tuple(half if r in whole else 0 for r in range(n_out))

    def shapes(wide):
        rows = CORES * block if wide else block
        return (jax.ShapeDtypeStruct((rows, tok), BF16),) * (1 if wide else CORES)

    work = 2 * PER * both * n_out * both * size

    def score(r, done):
        with jax.named_scope("score"):
            return pl.pallas_call(
                functools.partial(score_kernel, r == 0),
                out_shape=(
                    jax.ShapeDtypeStruct((PER, n_out * both, both), BF16),
                    jax.ShapeDtypeStruct((PER * 8, both), F32),
                ),
                in_specs=vmem(1 + n_out),
                out_specs=tuple(vmem(2)),
                compiler_params=params,
                cost_estimate=pl.CostEstimate(flops=work, bytes_accessed=2**20, transcendentals=work // (2 * size)),
                name="score",
            )(q_by[r] if done is None else after(q_by[r], done), *ks)

    def apply(r, wide):
        with jax.named_scope("apply"):
            return pl.pallas_call(
                functools.partial(apply_kernel, wide, rows),
                out_shape=shapes(wide),
                in_specs=vmem(2 + n_out),
                out_specs=tuple(vmem(len(shapes(wide)))),
                compiler_params=params,
                cost_estimate=pl.CostEstimate(flops=work, bytes_accessed=2**20, transcendentals=0),
                name="apply",
            )(*weights_by[r], *vs)

    def add(arrays, wide):
        with jax.named_scope("add"):
            return pl.pallas_call(
                functools.partial(add_kernel, len(arrays), wide),
                out_shape=shapes(wide),
                in_specs=vmem(len(arrays)),
                out_specs=tuple(vmem(len(shapes(wide)))),
                compiler_params=params,
                name="add",
            )(*arrays)

    arrived = {r: [] for r in range(chips)}
    ends = []

    def send(r, parts):
        with jax.named_scope("return"):
            if single(r) and r > 1:
                both_blocks = lax.ppermute(parts[0], "inner", along_inner(r, 0))
                ends.append(both_blocks[:block, :])
                ends.append(lax.ppermute(both_blocks[block:, :], "inner", along_inner(0, 1)))
            elif single(r):
                ends.extend(lax.ppermute(parts[x], "inner", along_inner(r, x)) for x in range(CORES))
            else:
                arrived[r - low(r)].append(lax.ppermute(parts[0], "inner", along_inner(low(r), 0)))

    def both_kernels(r, done):
        weights_by[r] = score(r, done)
        partial[r] = apply(r, r > 1)
        return partial[r][0]

    done = None
    weights_by, partial = {}, {}
    for r in sorted(range(1, chips), key=lambda r: (r != chips - 1, r != 1, -r)):
        done = both_kernels(r, done)
    for r in reversed(range(2, chips)):
        parts = partial[r]
        if arrived[r]:
            parts = add([parts[0], *arrived[r]], True)
            done = parts[0]
        send(r, parts)
    done = both_kernels(0, done)
    if chips > 1:
        send(1, [partial[1][0], after(partial[1][1], done)])
    with jax.named_scope("return"):
        ends = [partial[0][0], lax.ppermute(partial[0][1], "inner", along_inner(0, 1))] + ends
    with jax.named_scope("combine"):
        return pl.pallas_call(
            functools.partial(combine_kernel, len(ends)),
            out_shape=jax.ShapeDtypeStruct((tok, width), BF16),
            in_specs=vmem(len(ends)),
            out_specs=vmem()[0],
            compiler_params=params,
            name="combine",
        )(*ends)


def solution(mesh):
    n_out, n_in = mesh.shape["outer"], mesh.shape["inner"]
    return jax.shard_map(
        functools.partial(shards, n_out, n_in),
        mesh=mesh,
        in_specs=(
            P(("outer", "inner"), None),
            P(("outer", "inner"), None),
            P(("outer", "inner"), None),
            P(("outer", "inner")),
        ),
        out_specs=P(("outer", "inner"), None),
        check_vma=False,
    )
```

```python
import functools
import math

import jax
import jax.numpy as jnp
from jax import lax
from jax.experimental import pallas as pl
from jax.experimental.pallas import tpu as pltpu
from jax.sharding import PartitionSpec as P

HEADS = 4
CORES = 2
PER = HEADS // CORES
PAD = 16
LOW = -1e30
FLOOR = -1e29
BF16 = jnp.bfloat16
F32 = jnp.float32


def nt_dot(a, b):
    return lax.dot_general(a, b, (((1,), (1,)), ((), ())), preferred_element_type=F32)


def place(own, other, out, at, turned=False):
    tok = own.shape[0]
    size = own.shape[1] // HEADS
    core = lax.rem(lax.axis_index("inner"), CORES)
    for b, ref in enumerate((own, other)):
        for j in range(PER):
            piece = ref[:, pl.ds(pl.multiple_of((core * PER + j) * size, size), size)]
            if turned:
                piece = piece.T
            row = at + j * CORES * tok + b * tok
            out[row : row + tok, :] = piece


def starts(p0, p1):
    half = PAD // CORES
    return jnp.concatenate([p[...].astype(F32)[0:half, :] for p in (p0, p1)], axis=0).astype(BF16)


def merge_kernel(p0, p1, own, q1, k1, v1, q_out, kv_out):
    tok = q1.shape[0]
    rows = PER * CORES * tok
    pos = starts(p0, p1)
    place(own.at[0:tok, :], q1, q_out, 0)
    q_out[rows:, :] = pos
    place(own.at[tok : 2 * tok, :], k1, kv_out, 0)
    kv_out[rows : rows + PAD, :] = pos
    place(own.at[2 * tok : 3 * tok, :], v1, kv_out, rows + PAD, turned=True)


def score_kernel(same, q_ref, *refs):
    k_refs, (p_ref, top_ref) = refs[:-2], refs[-2:]
    size = q_ref.shape[1]
    tok = size
    both = CORES * tok
    half = PAD // CORES
    rate = size ** -0.5 * math.log2(math.e)
    at_or_before = lax.broadcasted_iota(jnp.int32, (tok, tok), 0) <= lax.broadcasted_iota(jnp.int32, (tok, tok), 1)

    def block_of(ref):
        first = ref[PER * both : PER * both + PAD, :].astype(F32)
        return [first[b * half : b * half + 1, :] for b in range(CORES)]

    q_block = jnp.concatenate(block_of(q_ref), axis=1)
    kept = [jnp.concatenate([p] * CORES, axis=1) <= q_block for ref in k_refs for p in block_of(ref)]
    for h in range(PER):
        q = q_ref[h * both : (h + 1) * both, :]
        scores = []
        for j, ref in enumerate(k_refs):
            s = nt_dot(ref[h * both : (h + 1) * both, :], q)
            for b in range(CORES):
                part = s[b * tok : (b + 1) * tok, :]
                if same and j == 0:
                    cols = [part[:, c * tok : (c + 1) * tok] for c in range(CORES)]
                    cols[b] = jnp.where(at_or_before, cols[b], LOW)
                    part = jnp.concatenate(cols, axis=1)
                scores.append(part)
        tops = [jnp.where(k, jnp.max(s, axis=0, keepdims=True), FLOOR) for k, s in zip(kept, scores)]
        top = jnp.maximum(functools.reduce(jnp.maximum, tops), FLOOR).astype(BF16).astype(F32)
        for i, (k, s) in enumerate(zip(kept, scores)):
            p_ref[h, i * tok : (i + 1) * tok, :] = jnp.exp2((s - jnp.where(k, top, -LOW)) * rate).astype(BF16)
        top_ref[h * 8 : (h + 1) * 8, :] = jnp.broadcast_to(top, (8, both))


def apply_kernel(wide, rows, p_ref, top_ref, *refs):
    nv = len(refs) - (1 if wide else CORES)
    v_refs, out_refs = refs[:nv], refs[nv:]
    size = v_refs[0].shape[1]
    tok = size
    both = CORES * tok
    block = PER * size + PAD

    def store(b, at, value):
        if wide:
            out_refs[0][b * block + at : b * block + at + value.shape[0], :] = value
        else:
            out_refs[b][at : at + value.shape[0], :] = value

    stats = [[] for _ in range(CORES)]
    for h in range(PER):
        vals = []
        for ref, row in zip(v_refs, rows):
            for b in range(CORES):
                at = row + h * both + b * tok
                vals.append(ref[at : at + tok, :])
        vt = jnp.concatenate(vals, axis=1)
        vt = jnp.concatenate([vt, jnp.ones((PAD, vt.shape[1]), BF16)], axis=0)
        o = jnp.dot(vt, p_ref[h], preferred_element_type=F32)
        total = o[size : size + 1, :]
        hi = total.astype(BF16).astype(F32)
        top = top_ref[h * 8 : h * 8 + 1, :]
        for b in range(CORES):
            cols = slice(b * tok, (b + 1) * tok)
            store(b, h * size, o[0:size, cols].astype(BF16))
            stats[b] += [top[:, cols], hi[:, cols], (total - hi)[:, cols]]
    for b in range(CORES):
        rest = jnp.zeros((PAD - 3 * PER, tok), F32)
        store(b, PER * size, jnp.concatenate(stats[b] + [rest], axis=0).astype(BF16))


def joined(parts, stats, h, rate):
    size = parts[0].shape[0]
    tops = [s[3 * h : 3 * h + 1, :] for s in stats]
    best = functools.reduce(jnp.maximum, tops)
    factors = [jnp.exp2((t - best) * rate) for t in tops]
    total = sum(f * (s[3 * h + 1 : 3 * h + 2, :] + s[3 * h + 2 : 3 * h + 3, :]) for f, s in zip(factors, stats))
    numer = sum(f * part.astype(F32) for f, part in zip(factors, parts))
    return best, total, numer


def add_kernel(n, wide, *refs):
    size = refs[0].shape[1]
    block = PER * size + PAD
    rate = size ** -0.5 * math.log2(math.e)
    for b in range(CORES):
        base = b * block
        stats = [ref[base + PER * size : base + block, :].astype(F32) for ref in refs[:n]]
        out, at = (refs[n], base) if wide else (refs[n + b], 0)
        rows = []
        for h in range(PER):
            parts = [ref[base + h * size : base + (h + 1) * size, :] for ref in refs[:n]]
            best, total, numer = joined(parts, stats, h, rate)
            hi = total.astype(BF16).astype(F32)
            rows += [best, hi, total - hi]
            out[at + h * size : at + (h + 1) * size, :] = numer.astype(BF16)
        rest = jnp.zeros((PAD - 3 * PER, size), F32)
        out[at + PER * size : at + block, :] = jnp.concatenate(rows + [rest], axis=0).astype(BF16)


def combine_kernel(n, *refs):
    parts, out_ref = refs[:n], refs[n]
    size = parts[0].shape[1]
    rate = size ** -0.5 * math.log2(math.e)
    core = lax.rem(lax.axis_index("inner"), CORES)
    for x in range(CORES):
        mine = parts[x::CORES]
        pair = jnp.bitwise_xor(core, x)
        stats = [part[PER * size :, :].astype(F32) for part in mine]
        for h in range(PER):
            _, total, numer = joined([part[h * size : (h + 1) * size, :] for part in mine], stats, h, rate)
            cols = pl.ds(pl.multiple_of((pair * PER + h) * size, size), size)
            out_ref[:, cols] = (numer * (1.0 / total)).astype(BF16).T


def vmem(n=1):
    return [pl.BlockSpec(memory_space=pltpu.VMEM)] * n


def shards(n_out, n_in, queries, keys, values, block_pos):
    tok, width = queries.shape
    size = width // HEADS
    chips = n_in // CORES
    both = CORES * tok
    params = pltpu.CompilerParams(vmem_limit_bytes=40 * 1024 * 1024)

    def along_inner(r, x):
        return [(w * CORES + c, (w ^ r) * CORES + (c ^ x)) for w in range(chips) for c in range(CORES)]

    def after(a, b):
        return lax.optimization_barrier((a, b))[0]

    with jax.named_scope("swap"):
        here = jnp.broadcast_to(block_pos.astype(BF16)[:, None], (PAD, size))
        other = [lax.ppermute(a, "inner", along_inner(0, 1)) for a in (queries, keys, values, here)]
        own = jnp.concatenate([queries, keys, values], axis=0)
    with jax.named_scope("merge"):
        q_piece, kv_piece = pl.pallas_call(
            merge_kernel,
            out_shape=(
                jax.ShapeDtypeStruct((PER * both + PAD, size), BF16),
                jax.ShapeDtypeStruct((2 * PER * both + PAD, size), BF16),
            ),
            in_specs=vmem(6),
            out_specs=tuple(vmem(2)),
            compiler_params=params,
            name="merge",
        )(here, other[3], own, *other[:3])
    half = PER * both + PAD
    block = PER * size + PAD

    def low(r):
        return r & -r

    def high(r):
        return 1 << (r.bit_length() - 1)

    def single(r):
        return r == low(r)

    def over(a, r):
        return lax.ppermute(a, "outer", [(o, o ^ r) for o in range(n_out)])

    with jax.named_scope("exchange"):
        whole = {r: over(kv_piece, r) if r else kv_piece for r in range(n_out) if single(r)}
        q_by = {0: q_piece}
        for r in sorted(range(1, chips), key=lambda r: (r != chips - 1, r)):
            piece = q_piece if r in (1, chips - 1) else after(q_piece, q_by[1])
            q_by[r] = lax.ppermute(piece, "inner", along_inner(r, 0))
        k_by = {r: a[:half, :] for r, a in whole.items() if r}
        v_by = {r: a[half:, :] for r, a in whole.items() if r}
        for r in range(1, n_out):
            if not single(r):
                k_by[r] = over(k_by[r - high(r)], high(r))
        for r in sorted(range(1, n_out), key=lambda r: r.bit_count()):
            if not single(r):
                v_by[r] = over(v_by[r - low(r)], low(r))
        ks = [whole[r] if r in whole else k_by[r] for r in range(n_out)]
        vs = [whole[r] if r in whole else v_by[r] for r in range(n_out)]
        rows = tuple(half if r in whole else 0 for r in range(n_out))

    def shapes(wide):
        rows = CORES * block if wide else block
        return (jax.ShapeDtypeStruct((rows, tok), BF16),) * (1 if wide else CORES)

    work = 2 * PER * both * n_out * both * size

    def score(r, done):
        with jax.named_scope("score"):
            return pl.pallas_call(
                functools.partial(score_kernel, r == 0),
                out_shape=(
                    jax.ShapeDtypeStruct((PER, n_out * both, both), BF16),
                    jax.ShapeDtypeStruct((PER * 8, both), F32),
                ),
                in_specs=vmem(1 + n_out),
                out_specs=tuple(vmem(2)),
                compiler_params=params,
                cost_estimate=pl.CostEstimate(flops=work, bytes_accessed=2**20, transcendentals=work // (2 * size)),
                name="score",
            )(q_by[r] if done is None else after(q_by[r], done), *ks)

    def apply(r, wide):
        with jax.named_scope("apply"):
            return pl.pallas_call(
                functools.partial(apply_kernel, wide, rows),
                out_shape=shapes(wide),
                in_specs=vmem(2 + n_out),
                out_specs=tuple(vmem(len(shapes(wide)))),
                compiler_params=params,
                cost_estimate=pl.CostEstimate(flops=work, bytes_accessed=2**20, transcendentals=0),
                name="apply",
            )(*weights_by[r], *vs)

    def add(arrays, wide):
        with jax.named_scope("add"):
            return pl.pallas_call(
                functools.partial(add_kernel, len(arrays), wide),
                out_shape=shapes(wide),
                in_specs=vmem(len(arrays)),
                out_specs=tuple(vmem(len(shapes(wide)))),
                compiler_params=params,
                name="add",
            )(*arrays)

    arrived = {r: [] for r in range(chips)}
    ends = []

    def send(r, parts):
        with jax.named_scope("return"):
            if single(r):
                both_blocks = lax.ppermute(parts[0], "inner", along_inner(r, 0))
                ends.append(both_blocks[:block, :])
                ends.append(lax.ppermute(both_blocks[block:, :], "inner", along_inner(0, 1)))
            else:
                arrived[r - low(r)].append(lax.ppermute(parts[0], "inner", along_inner(low(r), 0)))

    def both_kernels(r, done):
        weights_by[r] = score(r, done)
        partial[r] = apply(r, r > 0)
        return partial[r][0]

    done = None
    weights_by, partial = {}, {}
    for r in sorted(range(1, chips), key=lambda r: (r != chips - 1, r != 1, -r)):
        done = both_kernels(r, done)
    for r in reversed(range(2, chips)):
        parts = partial[r]
        if arrived[r]:
            parts = add([parts[0], *arrived[r]], True)
            done = parts[0]
        send(r, parts)
    done = both_kernels(0, done)
    if chips > 1:
        send(1, partial[1])
    with jax.named_scope("return"):
        ends = [partial[0][0], lax.ppermute(partial[0][1], "inner", along_inner(0, 1))] + ends
    with jax.named_scope("combine"):
        return pl.pallas_call(
            functools.partial(combine_kernel, len(ends)),
            out_shape=jax.ShapeDtypeStruct((tok, width), BF16),
            in_specs=vmem(len(ends)),
            out_specs=vmem()[0],
            compiler_params=params,
            name="combine",
        )(*ends)


def solution(mesh):
    n_out, n_in = mesh.shape["outer"], mesh.shape["inner"]
    return jax.shard_map(
        functools.partial(shards, n_out, n_in),
        mesh=mesh,
        in_specs=(
            P(("outer", "inner"), None),
            P(("outer", "inner"), None),
            P(("outer", "inner"), None),
            P(("outer", "inner")),
        ),
        out_specs=P(("outer", "inner"), None),
        check_vma=False,
    )
```
